256 devices in a mesh: section: 4 (over z_lo), tile: 64 (over x, z_hi, y, core).
Axes of the slice: x: 4, y: 4, z: 8 (z_hi: 2, z_lo: 4; z = z_hi * 4 + z_lo), core: 2. Of those that a mesh axis runs over, the one named last changes fastest.
Arguments:
- saved_inputs: bfloat16 [4, 8, 64, 4, 8, 256], P('section', None, 'tile'), may hold values from -300 to 300
- cotangent: bfloat16 [8, 64, 4, 8, 256], P(None, 'tile'), may hold values from -6 to 6
- kernels: bfloat16 [4, 6912, 256], P('section'), may hold values from -0.078125 to 0.078125
- gains: float32 [4, 256], P('section'), may hold values from 0.1 to 1.9
- biases: float32 [4, 256], P('section'), may hold values from -3 to 3
Outputs:
- input_grads: bfloat16 [4, 8, 64, 4, 8, 256], P('section', None, 'tile')
- kernel_grads: float32 [4, 6912, 256], P('section', 'tile')
- gain_grads: float32 [4, 256], P('section')
- bias_grads: float32 [4, 256], P('section')
The draws below stay inside these ranges and needn't reach their ends.
All inputs are finite; a program needn't handle non-finite values.
Results may differ from the reference program's by a relative error of at most 0.0055.
Values may be sent and summed in bfloat16 or wider, within the bound.
A program may use at most 128 MiB of HBM per device.

```python
import math
import jax
import jax.numpy as jnp
from jax import lax

CHANNELS = 256
GROUPS = 32
GRID_COLS = 8
TILE_ROWS = 4
TILE_COLS = 8
BLOCKS = 4
FRAMES = 8
GRID_ROWS = 8
N_TILE = 64


def draw_saved_inputs(key, part):
    key = jax.random.fold_in(key, 7)
    key_base, key_chan, key_pix = jax.random.split(key, 3)
    shape = (BLOCKS, FRAMES, N_TILE, TILE_ROWS, TILE_COLS, CHANNELS)
    position = jnp.arange(N_TILE, dtype=jnp.float32) / max(N_TILE - 1, 1)
    channel_scale = jnp.exp(jax.random.uniform(key_chan, (BLOCKS, 1, 1, 1, 1, CHANNELS), minval=-1.15, maxval=1.15))
    pixel_scale = jnp.exp(jax.random.uniform(key_pix, (BLOCKS, FRAMES, N_TILE, TILE_ROWS, TILE_COLS, 1), minval=-0.35, maxval=0.35))
    values = jax.random.normal(key_base, shape)
    tile_scale = jnp.exp(position * math.log(3.0))
    tile_scale = tile_scale.reshape(1, 1, N_TILE, 1, 1, 1)
    return (values * channel_scale * tile_scale * pixel_scale).astype(jnp.bfloat16)


def block_scale(key, shape, cuts, low, top_value):
    factor_of = 1.0
    for dim, parts in cuts:
        steps = jax.random.uniform(jax.random.fold_in(jax.random.fold_in(key, 6), dim), (parts,), jnp.float32, low / len(cuts), top_value / len(cuts))
        factor_of = factor_of * jnp.repeat(jnp.exp(steps), shape[dim] // parts).reshape((-1,) + (1,) * (len(shape) - 1 - dim))
    return factor_of


def gaussian(stream_key, extent, scale, limit, shards=(), kind=jnp.bfloat16):
    gain = block_scale(stream_key, extent, shards, -0.22, 0.18) if shards else 1.0
    entries = jax.random.normal(stream_key, extent, jnp.float32) * scale * gain
    return jnp.minimum(jnp.maximum(entries, -limit), limit).astype(kind)


def setup_inputs(seed: int = 0) -> dict:
    key_list = jax.random.split(jax.random.key(seed), 6)
    saved_inputs = draw_saved_inputs(jax.random.fold_in(key_list[5], 71), 0)
    cotangent = gaussian(key_list[1], (FRAMES, N_TILE, TILE_ROWS, TILE_COLS, CHANNELS), 1.0, 6.0, ((1, 64),))
    kernels = gaussian(key_list[2], (BLOCKS, 27 * CHANNELS, CHANNELS), (27 * CHANNELS) ** -0.5, 0.078125, ((0, 4),))
    gains = jnp.clip(1.0 + 0.18 * jax.random.normal(key_list[3], (BLOCKS, CHANNELS), jnp.float32), 0.1, 1.9)
    biases = gaussian(key_list[4], (BLOCKS, CHANNELS), 0.5, 3.0, ((0, 4),), jnp.float32)
    return {"saved_inputs": saved_inputs, "cotangent": cotangent, "kernels": kernels, "gains": gains, "biases": biases}


NORM_EPSILON = 1e-05

def to_frames(tiled):
    length = tiled.shape[0]
    shaped = tiled.reshape(length, GRID_ROWS, GRID_COLS, TILE_ROWS, TILE_COLS, CHANNELS)
    return shaped.transpose(0, 1, 3, 2, 4, 5).reshape(length, GRID_ROWS * TILE_ROWS, GRID_COLS * TILE_COLS, CHANNELS)

def to_tiles(whole):
    length = whole.shape[0]
    shaped = whole.reshape(length, GRID_ROWS, TILE_ROWS, GRID_COLS, TILE_COLS, CHANNELS)
    return shaped.transpose(0, 1, 3, 2, 4, 5).reshape(length, N_TILE, TILE_ROWS, TILE_COLS, CHANNELS)

def convolve(active_f, kernel_f):
    result = lax.conv_general_dilated(active_f[None], kernel_f, (1, 1, 1), ((2, 0), (1, 1), (1, 1)), dimension_numbers=('NDHWC', 'DHWIO', 'NDHWC'), precision=lax.Precision.HIGHEST)
    return result[0]

def block_grads(saved, upstream, kernel, gain_row, bias_row):
    height = saved.shape[1]
    width = saved.shape[2]
    per_group = CHANNELS // GROUPS
    entry_count = height * width * per_group
    grouped = saved.astype(jnp.float32).reshape(FRAMES, height * width, GROUPS, per_group)
    group_mean = lax.optimization_barrier(jnp.sum(grouped, axis=(1, 3))) / entry_count
    squares = lax.optimization_barrier(jnp.sum(grouped * grouped, axis=(1, 3))) / entry_count
    rstd = lax.rsqrt(squares - group_mean * group_mean + NORM_EPSILON)
    normed = (grouped - group_mean[:, None, :, None]) * rstd[:, None, :, None]
    normed = normed.reshape(FRAMES, height, width, CHANNELS)
    hidden = normed * gain_row + bias_row
    active = jax.nn.silu(hidden).astype(jnp.bfloat16)
    kernel_f = kernel.astype(jnp.float32).reshape(3, 3, 3, CHANNELS, CHANNELS)
    upstream_f = upstream.astype(jnp.float32)
    unused, pull_back = jax.vjp(convolve, active.astype(jnp.float32), kernel_f)
    grad_active, grad_kernel = pull_back(upstream_f)
    sigmoid_h = jax.nn.sigmoid(hidden)
    grad_hidden = grad_active * sigmoid_h * (1.0 + hidden * (1.0 - sigmoid_h))
    gain_term = lax.optimization_barrier(jnp.sum(grad_hidden * normed, axis=(0, 1, 2)))
    bias_term = lax.optimization_barrier(jnp.sum(grad_hidden, axis=(0, 1, 2)))
    weighted = (grad_hidden * gain_row).reshape(FRAMES, height * width, GROUPS, per_group)
    normed_g = normed.reshape(FRAMES, height * width, GROUPS, per_group)
    first = lax.optimization_barrier(jnp.sum(weighted, axis=(1, 3))) / entry_count
    second = lax.optimization_barrier(jnp.sum(weighted * normed_g, axis=(1, 3))) / entry_count
    norm_back = rstd[:, None, :, None] * (weighted - first[:, None, :, None] - normed_g * second[:, None, :, None])
    result = (upstream_f + norm_back.reshape(FRAMES, height, width, CHANNELS)).astype(jnp.bfloat16)
    return (result, grad_kernel.reshape(27 * CHANNELS, CHANNELS), gain_term, bias_term)

def reference(saved_inputs, cotangent, kernels, gains, biases):
    scale = 1.0 / math.sqrt(FRAMES * N_TILE * TILE_ROWS * TILE_COLS)
    upstream = to_frames(cotangent)
    input_list = [None] * BLOCKS
    kernel_list = [None] * BLOCKS
    gain_list = [None] * BLOCKS
    bias_list = [None] * BLOCKS
    for layer in range(BLOCKS - 1, -1, -1):
        result, grad_kernel, gain_term, bias_term = block_grads(to_frames(saved_inputs[layer]), upstream, kernels[layer], gains[layer], biases[layer])
        input_list[layer] = to_tiles(result)
        kernel_list[layer] = grad_kernel * scale
        gain_list[layer] = gain_term * scale
        bias_list[layer] = bias_term * scale
        upstream = result
    return (jnp.stack(input_list), jnp.stack(kernel_list), jnp.stack(gain_list), jnp.stack(bias_list))
```

```python
import functools
import math

import jax
import jax.numpy as jnp
from jax import lax
from jax.experimental import pallas as pl
from jax.experimental.pallas import tpu as pltpu
from jax.sharding import PartitionSpec as P

CH = 256
GROUPS = 32
PER_GROUP = CH // GROUPS
FR = 4
PX = 64
ROWS = FR * PX
ENTRIES = float(64 * 32 * PER_GROUP)
SCALE = 1.0 / math.sqrt(8 * 64 * 32)
EPS = 1e-05
MESH = pl.DeviceIdType.MESH
SIDES = ((-1, 0), (1, 0), (0, -1), (0, 1))
CORNERS = ((-1, -1), (-1, 1), (1, -1), (1, 1))
F32 = jnp.float32
BF16 = jnp.bfloat16


def kernel(
    x_ref, cot_ref, k_ref, gain_ref, bias_ref,
    out_ref, kout_ref, gout_ref, bout_ref,
    xr, cr, osend, orecv, rf, csend, hsend, nsend, gc, hr, nr, gp, gcol, kt_ref, a_t, xhat, dfac, stat,
    sa, sb, ua, ub, zg, zgr, dko, dks, dkr, dkb, rx, sx, ys, yr, sy, zs, zr, fs, fsend, frecv,
    ssem, zsem, hsem, nsem, gsem, tsem, pasem, pbsem, qasem, qbsem, csem, xsem, ysem, lsem,
):
    s = lax.axis_index("section")
    t = lax.axis_index("tile")
    x = t // 16
    zh = (t // 8) % 2
    y = (t // 2) % 4
    core = t % 2
    col = t % 8

    def dev(sec, x2, zh2, col2):
        return (sec, x2 * 16 + zh2 * 8 + col2)

    zpeer = dev(s, x, 1 - zh, col)
    cpeer = dev(s, x, zh, y * 2 + 1 - core)

    def remote(src, dst, sem_pair, device):
        return pltpu.make_async_remote_copy(
            src_ref=src, dst_ref=dst, send_sem=sem_pair.at[0], recv_sem=sem_pair.at[1],
            device_id=device, device_id_type=MESH,
        )

    xcopy = remote(x_ref.at[pl.ds((1 - zh) * FR, FR)], xr, zsem.at[0], zpeer)
    ccopy = remote(cot_ref.at[pl.ds((1 - zh) * FR, FR)], cr, zsem.at[1], zpeer)
    xcopy.start()

    @pl.when(s == 3)
    def _():
        ccopy.start()

    def patch(own, other):
        own = own.astype(F32)
        other = other.astype(F32)
        upper = jnp.where(zh == 0, own, other)
        lower = jnp.where(zh == 0, other, own)
        return jnp.concatenate([upper, lower], axis=1).reshape(ROWS, CH)

    lane = lax.broadcasted_iota(jnp.int32, (CH, 128), 1)
    chan = lax.broadcasted_iota(jnp.int32, (CH, 128), 0)
    gather_m = (chan // PER_GROUP == lane).astype(F32)
    lane2 = lax.broadcasted_iota(jnp.int32, (128, CH), 0)
    chan2 = lax.broadcasted_iota(jnp.int32, (128, CH), 1)
    spread_m = (chan2 // PER_GROUP == lane2).astype(F32)

    def grouped(first, second):
        return jnp.dot(
            jnp.concatenate([first, second], axis=0), gather_m,
            precision=lax.Precision.HIGHEST, preferred_element_type=F32,
        )

    def spread(groups):
        return jnp.dot(
            groups, spread_m, precision=lax.Precision.HIGHEST, preferred_element_type=F32
        )

    def col_copies(buf, sems):
        return [
            remote(buf.at[col], buf.at[col], sems.at[k - 1], dev(s, x, zh, (col + k) % 8))
            for k in range(1, 8)
        ]

    def x_copies(buf, sems):
        return [
            remote(buf.at[x], buf.at[x], sems.at[k - 1], dev(s, (x + k) % 4, zh, col))
            for k in range(1, 4)
        ]

    xcopy.wait()
    xv = patch(x_ref[pl.ds(zh * FR, FR)], xr[...])
    xhat[...] = xv
    x3 = xv.reshape(FR, PX, CH)
    sa[col] = jnp.concatenate(
        [grouped(jnp.sum(x3, axis=1), jnp.sum(x3 * x3, axis=1)), jnp.zeros((8, 128), F32)], axis=0
    )
    sa_copies = col_copies(sa, pasem)
    for c in sa_copies:
        c.start()

    def pack(value):
        rf[...] = value
        csend[...] = value.astype(BF16)
        v4 = value.reshape(FR, 8, 8, CH)
        hsend[0] = v4[:, 0].reshape(32, CH).astype(BF16)
        hsend[1] = v4[:, 7].reshape(32, CH).astype(BF16)
        for i, lead in ((2, 0), (3, 7)):
            for f in range(FR):
                rows = [rf[f * PX + r * 8 + lead : f * PX + r * 8 + lead + 1, :] for r in range(8)]
                stat[f * 8 : f * 8 + 8, :] = jnp.concatenate(rows, axis=0)
            hsend[i] = stat[...].astype(BF16)
        for i, pixel in enumerate((0, 7, 56, 63)):
            rows = [rf[f * PX + pixel : f * PX + pixel + 1, :] for f in range(FR)]
            nsend[i] = jnp.concatenate(rows + [jnp.zeros((12, CH), F32)], axis=0).astype(BF16)

    def rim_copies(sec):
        near, far = [], []
        for i, (dx, dc) in enumerate(SIDES):
            x2, c2 = (x + dx + 4) % 4, (col + dc + 8) % 8
            far.append(remote(hsend.at[i, pl.ds(0, 16)], hr.at[i, pl.ds(32, 16)], hsem.at[1, i], dev(sec, x2, 0, c2)))
            near.append(remote(hsend.at[i], hr.at[i, pl.ds(0, 32)], hsem.at[0, i], dev(sec, x2, zh, c2)))
        for i, (dx, dc) in enumerate(CORNERS):
            x2, c2 = (x + dx + 4) % 4, (col + dc + 8) % 8
            far.append(remote(nsend.at[i], nr.at[1, i], nsem.at[1, i], dev(sec, x2, 0, c2)))
            near.append(remote(nsend.at[i], nr.at[0, i], nsem.at[0, i], dev(sec, x2, zh, c2)))
        return near, far

    def center_copies(sec):
        near = remote(csend, gc.at[pl.ds(0, ROWS)], gsem.at[0], dev(sec, x, zh, col))
        far = remote(csend.at[pl.ds(0, 2 * PX)], gc.at[pl.ds(ROWS, 2 * PX)], gsem.at[1], dev(sec, x, 0, col))
        return near, far

    def send_patch(sec, remote_center):
        near, far = rim_copies(sec)
        center_near, center_far = center_copies(sec)

        @pl.when(zh == 1)
        def _():
            for c in far:
                c.start()
            center_far.start()

        for c in near:
            c.start()
        if remote_center:
            center_near.start()

    def wait_sent(sec, remote_center):
        near, far = rim_copies(sec)
        center_near, center_far = center_copies(sec)
        for c in near:
            c.wait_send()
        if remote_center:
            center_near.wait_send()

        @pl.when(zh == 1)
        def _():
            for c in far:
                c.wait_send()
            center_far.wait_send()

    @pl.when(s == 3)
    def _():
        ccopy.wait()
        value = patch(cot_ref[pl.ds(zh * FR, FR)], cr[...])
        pack(value)
        gc[0:ROWS, :] = value.astype(BF16)
        send_patch(3, False)

    def flip(i, carry):
        at = pl.multiple_of(i * CH, CH)
        kt_ref[pl.ds(at, CH), :] = jnp.transpose(k_ref[pl.ds(at, CH), :])
        return carry

    lax.fori_loop(0, 27, flip, 0)

    for c in sa_copies:
        c.wait()
    sb[x] = jnp.sum(sa[...], axis=0)
    sb_copies = x_copies(sb, pbsem)
    for c in sb_copies:
        c.start()
    for c in sb_copies:
        c.wait()
    total = spread(jnp.sum(sb[...], axis=0)[0:8] / ENTRIES)
    mean = total[0:4]
    rstd = lax.rsqrt(total[4:8] - mean * mean + EPS)
    gain = gain_ref[...]
    xh = (xhat[...].reshape(FR, PX, CH) - mean[:, None, :]) * rstd[:, None, :]
    h = xh * gain[None] + bias_ref[...][None]
    sg = jax.nn.sigmoid(h)
    xhat[...] = xh.reshape(ROWS, CH)
    dfac[...] = (sg * (1.0 + h * (1.0 - sg))).reshape(ROWS, CH)
    a_t[...] = jnp.transpose((h * sg).reshape(ROWS, CH)).astype(BF16)

    near, far = rim_copies(s)
    center_near, center_far = center_copies(s)

    @pl.when(s < 3)
    def _():
        center_near.wait_recv()

    for c in near:
        c.wait_recv()

    @pl.when(zh == 0)
    def _():
        for c in far:
            c.wait_recv()
        center_far.wait_recv()

    edge = (x > 0, x < 3, col > 0, col < 7)

    def fill(frames, row0, corner_set):
        sides = [hr[i, row0 : row0 + 8 * len(frames), :].astype(F32) for i in range(4)]
        top = jnp.where(edge[0], sides[1], 0.0)
        bottom = jnp.where(edge[1], sides[0], 0.0)
        left = jnp.where(edge[2], sides[3], 0.0)
        right = jnp.where(edge[3], sides[2], 0.0)
        corners = [nr[corner_set, i].astype(F32) for i in range(4)]
        top_left = jnp.where(edge[0] & edge[2], corners[3], 0.0)
        top_right = jnp.where(edge[0] & edge[3], corners[2], 0.0)
        bottom_left = jnp.where(edge[1] & edge[2], corners[1], 0.0)
        bottom_right = jnp.where(edge[1] & edge[3], corners[0], 0.0)
        for n, f in enumerate(frames):
            base = f * 10
            cell = slice(n * 8, n * 8 + 8)
            center = gc[f * PX : f * PX + PX, :].astype(F32).reshape(8, 8, CH)
            gp[base + 1 : base + 9, 8:16, :] = center
            gp[base, 8:16, :] = top[cell]
            gp[base + 9, 8:16, :] = bottom[cell]
            for r in range(8):
                gp[base + 1 + r, 7:8, :] = left[n * 8 + r : n * 8 + r + 1]
                gp[base + 1 + r, 16:17, :] = right[n * 8 + r : n * 8 + r + 1]
            gp[base, 7:8, :] = top_left[n : n + 1]
            gp[base, 16:17, :] = top_right[n : n + 1]
            gp[base + 9, 7:8, :] = bottom_left[n : n + 1]
            gp[base + 9, 16:17, :] = bottom_right[n : n + 1]
            for ox in range(3):
                strip = gp[base : base + 10, 7 + ox : 15 + ox, :]
                for oy in range(3):
                    tap = (2 - oy) * 3 + (2 - ox)
                    gcol[f * PX : f * PX + PX, tap * CH : tap * CH + CH] = (
                        strip[oy : oy + 8].reshape(PX, CH).astype(BF16)
                    )

    fill(range(4), 0, 0)

    @pl.when(zh == 0)
    def _():
        fill(range(4, 6), 32, 1)

    @pl.when(zh == 1)
    def _():
        gcol[ROWS:, :] = jnp.zeros((2 * PX, 9 * CH), BF16)

    da = jnp.zeros((ROWS, CH), F32)
    for kt in range(3):
        da = da + jnp.dot(
            gcol[(2 - kt) * PX : (2 - kt) * PX + ROWS, :],
            kt_ref[kt * 9 * CH : (kt + 1) * 9 * CH, :],
            preferred_element_type=F32,
        )
    dh = da * dfac[...]
    rf[...] = dh
    dh3 = dh.reshape(FR, PX, CH)
    dh_sum = jnp.sum(dh3, axis=1)
    dhx_sum = jnp.sum(dh3 * xhat[...].reshape(FR, PX, CH), axis=1)
    gain_part = jnp.sum(dhx_sum, axis=0, keepdims=True)
    bias_part = jnp.sum(dh_sum, axis=0, keepdims=True)
    ua[col] = jnp.concatenate(
        [
            grouped(dh_sum * gain, dhx_sum * gain),
            gain_part[:, :128], gain_part[:, 128:], bias_part[:, :128], bias_part[:, 128:],
            jnp.zeros((4, 128), F32),
        ],
        axis=0,
    )
    ua_copies = col_copies(ua, qasem)
    for c in ua_copies:
        c.start()

    def kernel_term(kt):
        def one(j, carry):
            rows = pl.multiple_of(kt * 9 * CH + j * CH, CH)
            lanes = pl.multiple_of(j * CH, CH)
            part = jnp.dot(
                a_t[...],
                gcol[(2 - kt) * PX : (2 - kt) * PX + ROWS, pl.ds(lanes, CH)],
                preferred_element_type=F32,
            )
            dko[pl.ds(rows, CH), :] = jnp.where(core == 0, part[:, :128], part[:, 128:])
            dks[pl.ds(rows, CH), :] = jnp.where(core == 0, part[:, 128:], part[:, :128]).astype(BF16)
            return carry

        lax.fori_loop(0, 9, one, 0)
        span = pl.ds(kt * 9 * CH, 9 * CH)
        copy = remote(dks.at[span], dkr.at[span], csem.at[kt], cpeer)
        copy.start()
        return copy

    core_copies = [kernel_term(0)]
    for c in ua_copies:
        c.wait()
    ub[x] = jnp.sum(ua[...], axis=0)
    ub_copies = x_copies(ub, qbsem)
    for c in ub_copies:
        c.start()
    core_copies.append(kernel_term(1))
    for c in ub_copies:
        c.wait()
    plane = jnp.sum(ub[...], axis=0)
    zg[...] = plane
    zg_copy = remote(zg, zgr, zsem.at[3], zpeer)
    zg_copy.start()
    both = spread(plane[0:8] / ENTRIES)
    xh = xhat[...].reshape(FR, PX, CH)
    u = rf[...].reshape(FR, PX, CH) * gain[None]
    dxn = rstd[:, None, :] * (u - both[0:4][:, None, :] - xh * both[4:8][:, None, :])
    result = gc[0:ROWS, :].astype(F32) + dxn.reshape(ROWS, CH)

    @pl.when(s == 3)
    def _():
        wait_sent(3, False)

    pack(result)

    @pl.when(s > 0)
    def _():
        send_patch(s - 1, True)

    final = csend[...].reshape(FR, 2, 32, CH)
    osend[...] = jnp.where(zh == 0, final[:, 1], final[:, 0])
    o_copy = remote(osend, orecv, zsem.at[2], zpeer)
    o_copy.start()
    out_ref[pl.ds(zh * FR, FR)] = jnp.where(zh == 0, final[:, 0], final[:, 1])

    core_copies.append(kernel_term(2))
    for kt, c in enumerate(core_copies):
        c.wait()

        def join(j, carry):
            rows = pl.multiple_of(kt * 9 * CH + j * CH, CH)
            both_cores = dko[pl.ds(rows, CH), :] + dkr[pl.ds(rows, CH), :].astype(F32)
            dko[pl.ds(rows, CH), :] = both_cores
            dkb[pl.ds(rows, CH), :] = both_cores.astype(BF16)
            return carry

        lax.fori_loop(0, 9, join, 0)

    rs_copies = []
    for k in range(1, 4):
        x2 = (x + k) % 4
        c = remote(
            dkb.at[pl.ds(pl.multiple_of(x2 * 1728, 16), 1728)], rx.at[x], xsem.at[k - 1], dev(s, x2, zh, col)
        )
        c.start()
        rs_copies.append(c)
    for c in rs_copies:
        c.wait()

    def add_x(i, carry):
        at = pl.multiple_of(i * 432, 16)
        acc = dko[pl.ds(pl.multiple_of(x * 1728 + i * 432, 16), 432), :]
        for k in range(1, 4):
            acc = acc + rx[(x + k) % 4, pl.ds(at, 432), :].astype(F32)
        sx[pl.ds(at, 432), :] = acc
        return carry

    lax.fori_loop(0, 4, add_x, 0)
    pad = jnp.zeros((8, 128), F32)
    for y2 in range(4):
        for z2 in range(2):
            at = z2 * 864 + y2 * 216
            ys[y2, z2] = jnp.concatenate([sx[at : at + 216, :], pad], axis=0).astype(BF16)
    y_copies = []
    for k in range(1, 4):
        y2 = (y + k) % 4
        c = remote(ys.at[y2], yr.at[y], ysem.at[k - 1], dev(s, x, zh, y2 * 2 + core))
        c.start()
        y_copies.append(c)
    for c in y_copies:
        c.wait()
    for z2 in range(2):
        acc = sx[pl.ds(pl.multiple_of(z2 * 864 + y * 216, 8), 216), :]
        for k in range(1, 4):
            acc = acc + yr[(y + k) % 4, z2].astype(F32)[0:216]
        sy[z2] = acc
    zs[...] = jnp.concatenate([sy[1 - zh], pad], axis=0).astype(BF16)
    z_copy = remote(zs, zr, lsem.at[0], zpeer)
    z_copy.start()
    z_copy.wait()
    fs[...] = sy[zh] + zr[...].astype(F32)[0:216]
    low = fs[0:108, :]
    high = fs[108:216, :]
    mine = jnp.where(core == 0, low, high)
    fsend[0:108, :] = jnp.where(core == 0, high, low)
    fsend[108:112, :] = jnp.zeros((4, 128), F32)
    f_copy = remote(fsend, frecv, lsem.at[1], cpeer)
    f_copy.start()
    f_copy.wait()
    theirs = frecv[0:108, :]
    kout_ref[:, 0:128] = jnp.where(core == 0, mine, theirs) * SCALE
    kout_ref[:, 128:256] = jnp.where(core == 0, theirs, mine) * SCALE

    zg_copy.wait()
    sums = (zg[...] + zgr[...]) * SCALE
    gout_ref[:, 0:128] = sums[8:9]
    gout_ref[:, 128:256] = sums[9:10]
    bout_ref[:, 0:128] = sums[10:11]
    bout_ref[:, 128:256] = sums[11:12]
    o_copy.wait()
    out_ref[pl.ds((1 - zh) * FR, FR)] = orecv[...]

    @pl.when(s > 0)
    def _():
        wait_sent(s - 1, True)


def on_device(saved_inputs, cotangent, kernels, gains, biases):
    inputs = saved_inputs.reshape(8, 32, CH)
    seeds = cotangent.reshape(8, 32, CH)
    vmem = pl.BlockSpec(memory_space=pltpu.VMEM)
    v = pltpu.VMEM
    dma = pltpu.SemaphoreType.DMA
    out, kout, gout, bout = pl.pallas_call(
        kernel,
        out_shape=(
            jax.ShapeDtypeStruct((8, 32, CH), BF16),
            jax.ShapeDtypeStruct((108, CH), F32),
            jax.ShapeDtypeStruct((1, CH), F32),
            jax.ShapeDtypeStruct((1, CH), F32),
        ),
        in_specs=[vmem] * 5,
        out_specs=[vmem] * 4,
        scratch_shapes=[
            v((FR, 32, CH), BF16), v((FR, 32, CH), BF16), v((FR, 32, CH), BF16), v((FR, 32, CH), BF16),
            v((ROWS, CH), F32), v((ROWS, CH), BF16), v((4, 32, CH), BF16), v((4, 16, CH), BF16),
            v((ROWS + 2 * PX, CH), BF16), v((4, 48, CH), BF16), v((2, 4, 16, CH), BF16),
            v((60, 24, CH), F32), v((ROWS + 2 * PX, 9 * CH), BF16), v((27 * CH, CH), BF16),
            v((CH, ROWS), BF16), v((ROWS, CH), F32), v((ROWS, CH), F32), v((32, CH), F32),
            v((8, 16, 128), F32), v((4, 16, 128), F32), v((8, 16, 128), F32), v((4, 16, 128), F32),
            v((16, 128), F32), v((16, 128), F32),
            v((27 * CH, 128), F32), v((27 * CH, 128), BF16), v((27 * CH, 128), BF16), v((27 * CH, 128), BF16),
            v((4, 1728, 128), BF16), v((1728, 128), F32), v((4, 2, 224, 128), BF16), v((4, 2, 224, 128), BF16),
            v((2, 216, 128), F32), v((224, 128), BF16), v((224, 128), BF16), v((216, 128), F32),
            v((112, 128), F32), v((112, 128), F32),
            dma((1,)), dma((4, 2)), dma((2, 4, 2)), dma((2, 4, 2)), dma((2, 2)), dma((1,)),
            dma((7, 2)), dma((3, 2)), dma((7, 2)), dma((3, 2)), dma((3, 2)), dma((3, 2)), dma((3, 2)), dma((2, 2)),
        ],
        compiler_params=pltpu.CompilerParams(has_side_effects=True, vmem_limit_bytes=52 * 2**20),
        name="blocks",
    )(inputs, seeds, kernels[0], gains, biases)
    return (
        out.reshape(1, 8, 1, 4, 8, CH),
        kout[None],
        gout,
        bout,
    )


def solution(mesh):
    in_specs = (
        P("section", None, "tile", None, None, None),
        P(None, "tile", None, None, None),
        P("section", None, None),
        P("section", None),
        P("section", None),
    )
    out_specs = (
        P("section", None, "tile", None, None, None),
        P("section", "tile", None),
        P("section", None),
        P("section", None),
    )
    return jax.shard_map(
        on_device, mesh=mesh, in_specs=in_specs, out_specs=out_specs, check_vma=False
    )
```

```python
import functools
import math

import jax
import jax.numpy as jnp
from jax import lax
from jax.experimental import pallas as pl
from jax.experimental.pallas import tpu as pltpu
from jax.sharding import PartitionSpec as P

CH = 256
GROUPS = 32
PER_GROUP = CH // GROUPS
FR = 4
PX = 64
ROWS = FR * PX
ALL = ROWS + 2 * PX
ENTRIES = float(64 * 32 * PER_GROUP)
SCALE = 1.0 / math.sqrt(8 * 64 * 32)
EPS = 1e-05
VMEM_LIMIT = 63 * 2**20
MESH = pl.DeviceIdType.MESH
SIDES = ((-1, 0), (1, 0), (0, -1), (0, 1))
CORNERS = ((-1, -1), (-1, 1), (1, -1), (1, 1))
AROUND = [(dx, dy, dc) for dx in (-1, 0, 1) for dy, dc in ((0, 0), (-1, 1), (0, 1), (1, 1))]
CHIPS = [(dx, dy) for dx in range(4) for dy in range(4)]
QUARTERS = ((0, 7), (7, 14), (14, 21), (21, 27))
F32 = jnp.float32
BF16 = jnp.bfloat16


def kernel(
    x_hbm, cot_hbm, k_hbm, gain_hbm, bias_hbm,
    out_ref, kout_ref, gout_ref, bout_ref,
    x_ref, cot_ref, k_ref, gain_ref, bias_ref,
    xr, cr, osend, orecv, rf, strip,
    wc, wh, wn, gc, gh, gn, xwc, xwh, xwn, xgc, xgh, xgn,
    xc, xs, xn, gp, gcen, gcol, ccol, kt_ref, a_t, xhat, dfac, da,
    sa, sb, ua, ub, unear, ufar, xt, xtr, mom, zg, zgr,
    dko, dks, dkr, b0, b1, rx, ry, p0, p1, r2,
    lsem, zsem, wgs, whs, wns, xgs, xhs, xns, acs, aps, ucs, ups, tsem, csem, xsem, ysem, psem,
):
    s = lax.axis_index("section")
    t = lax.axis_index("tile")
    x = t // 16
    zh = (t // 8) % 2
    y = (t // 2) % 4
    core = t % 2
    col = t % 8
    chip = x * 4 + y

    def at(sec, dx, z2, dy, dc):
        return (sec, ((x + dx + 4) % 4) * 16 + z2 * 8 + ((y + dy + 4) % 4) * 2 + (core + dc) % 2)

    def beside(sec, dx, z2, dcol):
        return (sec, ((x + dx + 4) % 4) * 16 + z2 * 8 + (col + dcol + 8) % 8)

    zpeer = at(s, 0, 1 - zh, 0, 0)
    cpeer = at(s, 0, zh, 0, 1)

    def remote(src, dst, pair, device):
        return pltpu.make_async_remote_copy(
            src_ref=src, dst_ref=dst, send_sem=pair.at[0], recv_sem=pair.at[1],
            device_id=device, device_id_type=MESH,
        )

    x_load = pltpu.make_async_copy(x_hbm, x_ref, lsem.at[0])
    cot_load = pltpu.make_async_copy(cot_hbm, cot_ref, lsem.at[1])
    k_load = pltpu.make_async_copy(k_hbm, k_ref, lsem.at[2])
    gain_load = pltpu.make_async_copy(gain_hbm, gain_ref, lsem.at[3])
    bias_load = pltpu.make_async_copy(bias_hbm, bias_ref, lsem.at[4])
    x_load.start()
    gain_load.start()
    bias_load.start()

    @pl.when(s == 3)
    def _():
        cot_load.start()

    k_load.start()

    barrier = pltpu.get_barrier_semaphore()

    def greet(device):
        pl.semaphore_signal(barrier, inc=1, device_id=device, device_id_type=MESH)

    plane = {(dx, 0, dy, 0) for dx, dy in CHIPS}
    plane |= {(0, z, dy, dc) for z in range(2) for dy in range(4) for dc in range(2)}
    plane |= {(dx, z, 0, dc) for z in range(2) for dx in range(4) for dc in range(2)}
    plane = sorted(plane - {(0, 0, 0, 0)})
    for dx, z, dy, dc in plane:
        greet(at(s, dx, (zh + z) % 2, dy, dc))

    @pl.when(s < 3)
    def _():
        for dx, dy, dc in AROUND:
            greet(at(s + 1, dx, zh, dy, dc))

        @pl.when(zh == 0)
        def _():
            for dx, dy, dc in AROUND:
                greet(at(s + 1, dx, 1, dy, dc))

    @pl.when(s == 3)
    def _():
        for dx, dy, dc in AROUND:
            if (dx, dy, dc) != (0, 0, 0):
                greet(at(3, dx, zh, dy, dc))

        @pl.when(zh == 0)
        def _():
            for dx, dy, dc in AROUND:
                greet(at(3, dx, 1, dy, dc))

    expected = len(plane) + jnp.where(s > 0, (1 + zh) * len(AROUND), 0)
    expected = expected + jnp.where(s == 3, len(AROUND) - 1 + zh * len(AROUND), 0)
    pl.semaphore_wait(barrier, expected)

    theirs = pl.ds((1 - zh) * FR, FR)
    ours = pl.ds(zh * FR, FR)
    x_copy = remote(x_hbm.at[theirs], xr, zsem.at[0], zpeer)
    cot_copy = remote(cot_hbm.at[theirs], cr, zsem.at[1], zpeer)

    @pl.when(s == 3)
    def _():
        cot_copy.start()

    x_copy.start()

    def patch(own, other):
        own = own.astype(F32)
        other = other.astype(F32)
        upper = jnp.where(zh == 0, own, other)
        lower = jnp.where(zh == 0, other, own)
        return jnp.concatenate([upper, lower], axis=1).reshape(ROWS, CH)

    def indicator(shape, channel_dim):
        channel = lax.broadcasted_iota(jnp.int32, shape, channel_dim)
        group = lax.broadcasted_iota(jnp.int32, shape, 1 - channel_dim)
        return (channel // PER_GROUP == group).astype(F32)

    def grouped(first, second):
        return jnp.dot(
            jnp.concatenate([first, second], axis=0), indicator((CH, 128), 0),
            precision=lax.Precision.HIGHEST, preferred_element_type=F32,
        )

    def spread(groups):
        return jnp.dot(
            groups, indicator((128, CH), 1), precision=lax.Precision.HIGHEST, preferred_element_type=F32
        )

    def core_sum_copy(buf, pair):
        return remote(buf.at[core], buf.at[core], pair, cpeer)

    def chip_copies(buf, sems):
        return [
            remote(buf.at[chip], buf.at[chip], sems.at[i], at(s, dx, zh, dy, 0))
            for i, (dx, dy) in enumerate(CHIPS) if i
        ]

    def pack(value, center, sides, corners):
        rf[...] = value
        center[...] = value.astype(BF16)
        v4 = value.reshape(FR, 8, 8, CH)
        sides[0] = v4[:, 0].reshape(32, CH).astype(BF16)
        sides[1] = v4[:, 7].reshape(32, CH).astype(BF16)
        for i, lead in ((2, 0), (3, 7)):
            for f in range(FR):
                rows = [rf[f * PX + r * 8 + lead : f * PX + r * 8 + lead + 1, :] for r in range(8)]
                strip[f * 8 : f * 8 + 8, :] = jnp.concatenate(rows, axis=0)
            sides[i] = strip[...].astype(BF16)
        for i, pixel in enumerate((0, 7, 56, 63)):
            rows = [rf[f * PX + pixel : f * PX + pixel + 1, :] for f in range(FR)]
            corners[i] = jnp.concatenate(rows + [jnp.zeros((12, CH), F32)], axis=0).astype(BF16)

    def piece_copies(sec, send, recv, sems):
        center, sides, corners = send
        center_r, sides_r, corners_r = recv
        gs, hs, ns = sems
        near, far = [], []
        for i, (dx, dc) in enumerate(CORNERS):
            near.append(remote(corners.at[i], corners_r.at[0, i], ns.at[0, i], beside(sec, dx, zh, dc)))
            far.append(remote(corners.at[i], corners_r.at[1, i], ns.at[1, i], beside(sec, dx, 0, dc)))
        for i, (dx, dc) in enumerate(SIDES):
            near.append(remote(sides.at[i], sides_r.at[i, pl.ds(0, 32)], hs.at[0, i], beside(sec, dx, zh, dc)))
            far.append(
                remote(sides.at[i, pl.ds(0, 16)], sides_r.at[i, pl.ds(32, 16)], hs.at[1, i], beside(sec, dx, 0, dc))
            )
        middle = remote(center, center_r.at[pl.ds(0, ROWS)], gs.at[0], beside(sec, 0, zh, 0))
        far.append(
            remote(center.at[pl.ds(0, 2 * PX)], center_r.at[pl.ds(ROWS, 2 * PX)], gs.at[1], beside(sec, 0, 0, 0))
        )
        return near, middle, far

    def each(copies, what):
        for c in copies:
            getattr(c, what)()

    def send_pieces(copies, with_middle):
        near, middle, far = copies
        each(near, "start")
        if with_middle:
            middle.start()

        @pl.when(zh == 1)
        def _():
            each(far, "start")

    def wait_sent(copies, with_middle):
        near, middle, far = copies
        each(near + ([middle] if with_middle else []), "wait_send")

        @pl.when(zh == 1)
        def _():
            each(far, "wait_send")

    def wait_received(copies, with_middle):
        near, middle, far = copies
        each(near + ([middle] if with_middle else []), "wait_recv")

        @pl.when(zh == 0)
        def _():
            each(far, "wait_recv")

    w_send, w_recv, w_sems = (wc, wh, wn), (gc, gh, gn), (wgs, whs, wns)
    x_send, x_recv, x_sems = (xwc, xwh, xwn), (xgc, xgh, xgn), (xgs, xhs, xns)

    @pl.when(s == 3)
    def _():
        cot_load.wait()
        cot_copy.wait()
        value = patch(cot_ref[ours], cr[...])
        pack(value, wc, wh, wn)
        gc[0:ROWS, :] = value.astype(BF16)
        send_pieces(piece_copies(3, w_send, w_recv, w_sems), False)

    x_load.wait()
    x_copy.wait()
    xv = patch(x_ref[ours], xr[...])
    xhat[...] = xv
    x3 = xv.reshape(FR, PX, CH)
    sa[core] = grouped(jnp.sum(x3, axis=1), jnp.sum(x3 * x3, axis=1))
    sa_copy = core_sum_copy(sa, acs)
    sa_copy.start()

    @pl.when(s > 0)
    def _():
        pack(xv, xwc, xwh, xwn)

    sa_copy.wait()
    sb[chip] = sa[0] + sa[1]
    sb_copies = chip_copies(sb, aps)
    each(sb_copies, "start")

    @pl.when(s > 0)
    def _():
        send_pieces(piece_copies(s - 1, x_send, x_recv, x_sems), True)

    k_load.wait()

    def flip(i, carry):
        rows = pl.ds(pl.multiple_of(i * CH, CH), CH)
        kt_ref[rows, :] = jnp.transpose(k_ref[rows, :])
        return carry

    lax.fori_loop(0, 27, flip, 0)

    gain_load.wait()
    bias_load.wait()
    each(sb_copies, "wait")
    xt[...] = jnp.sum(sb[...], axis=0)
    xt_near = remote(xt, xtr.at[0], tsem.at[0], at(s - 1, 0, zh, 0, 0))
    xt_far = remote(xt, xtr.at[1], tsem.at[1], at(s - 1, 0, 0, 0, 0))

    @pl.when(s > 0)
    def _():
        xt_near.start()

        @pl.when(zh == 1)
        def _():
            xt_far.start()

    def moments(total):
        total = spread(total / ENTRIES)
        mean = total[0:4]
        return mean, lax.rsqrt(total[4:8] - mean * mean + EPS)

    mean, rstd = moments(xt[...])
    gain = gain_ref[...]
    xh = (xhat[...].reshape(FR, PX, CH) - mean[:, None, :]) * rstd[:, None, :]
    h = xh * gain[None] + bias_ref[...][None]
    sg = jax.nn.sigmoid(h)
    xhat[...] = xh.reshape(ROWS, CH)
    dfac[...] = (sg * (1.0 + h * (1.0 - sg))).reshape(ROWS, CH)
    a_t[...] = jnp.transpose((h * sg).reshape(ROWS, CH)).astype(BF16)

    @pl.when(s < 3)
    def _():
        wait_received(piece_copies(s, x_send, x_recv, x_sems), True)
        remote(xt, xtr.at[0], tsem.at[0], cpeer).wait_recv()

        @pl.when(zh == 0)
        def _():
            remote(xt, xtr.at[1], tsem.at[1], cpeer).wait_recv()

        def normalise(frames, part, row0):
            mean_up, rstd_up = moments(xtr[part])
            n = len(frames)
            mom[frames[0] : frames[0] + n, :] = rstd_up[0:n]
            m, r = mean_up[0:n][:, None, :], rstd_up[0:n][:, None, :]
            px = slice(frames[0] * PX, (frames[0] + n) * PX)
            xc[px, :] = ((xgc[px, :].astype(F32).reshape(n, PX, CH) - m) * r).reshape(n * PX, CH)
            for i in range(4):
                side = xgh[i, row0 : row0 + 8 * n, :].astype(F32).reshape(n, 8, CH)
                xs[i, row0 : row0 + 8 * n, :] = ((side - m) * r).reshape(8 * n, CH)
                xn[part, i, 0:n, :] = (xgn[part, i].astype(F32)[0:n] - mean_up[0:n]) * rstd_up[0:n]

        normalise(range(4), 0, 0)

        @pl.when(zh == 0)
        def _():
            normalise(range(4, 6), 1, 32)

    arriving = piece_copies(s, w_send, w_recv, w_sems)

    edge = (x > 0, x < 3, col > 0, col < 7)

    def columns(frames, center, sides, corners, out):
        top = jnp.where(edge[0], sides[1], 0.0)
        bottom = jnp.where(edge[1], sides[0], 0.0)
        left = jnp.where(edge[2], sides[3], 0.0)
        right = jnp.where(edge[3], sides[2], 0.0)
        top_left = jnp.where(edge[0] & edge[2], corners[3], 0.0)
        top_right = jnp.where(edge[0] & edge[3], corners[2], 0.0)
        bottom_left = jnp.where(edge[1] & edge[2], corners[1], 0.0)
        bottom_right = jnp.where(edge[1] & edge[3], corners[0], 0.0)
        center = center.reshape(len(frames), 8, 8, CH)
        for i, f in enumerate(frames):
            base = f * 10
            cell = slice(i * 8, i * 8 + 8)
            gp[base + 1 : base + 9, 8:16, :] = center[i]
            gp[base, 8:16, :] = top[cell]
            gp[base + 9, 8:16, :] = bottom[cell]
            for r in range(8):
                gp[base + 1 + r, 7:8, :] = left[i * 8 + r : i * 8 + r + 1]
                gp[base + 1 + r, 16:17, :] = right[i * 8 + r : i * 8 + r + 1]
            gp[base, 7:8, :] = top_left[i : i + 1]
            gp[base, 16:17, :] = top_right[i : i + 1]
            gp[base + 9, 7:8, :] = bottom_left[i : i + 1]
            gp[base + 9, 16:17, :] = bottom_right[i : i + 1]
            for ox in range(3):
                band = gp[base : base + 10, 7 + ox : 15 + ox, :]
                for oy in range(3):
                    tap = (2 - oy) * 3 + (2 - ox)
                    out[f * PX : f * PX + PX, tap * CH : tap * CH + CH] = (
                        band[oy : oy + 8].reshape(PX, CH).astype(BF16)
                    )

    def fill(frames, part, row0):
        n = len(frames)
        px = slice(frames[0] * PX, (frames[0] + n) * PX)
        columns(
            frames, gc[px, :].astype(F32),
            [gh[i, row0 : row0 + 8 * n, :].astype(F32) for i in range(4)],
            [gn[part, i].astype(F32)[0:n] for i in range(4)], gcol,
        )

    def fill_correction(frames, part, row0, sums):
        n = len(frames)
        both = spread(sums / ENTRIES)
        r_up = mom[frames[0] : frames[0] + n, :]
        c1, c2 = r_up * both[0:n], r_up * both[4 : 4 + n]

        def term(hat, rows):
            value = c1[:, None, :] + hat.reshape(n, rows, CH) * c2[:, None, :]
            return value.reshape(n * rows, CH)

        px = slice(frames[0] * PX, (frames[0] + n) * PX)
        center = term(xc[px, :], PX)
        if part == 0:
            gcen[...] = gc[px, :].astype(F32) - center
        columns(
            frames, center, [term(xs[i, row0 : row0 + 8 * n, :], 8) for i in range(4)],
            [c1 + xn[part, i, 0:n, :] * c2 for i in range(4)], ccol,
        )

    def convolve(cols):
        value = jnp.zeros((ROWS, CH), F32)
        for kt in range(3):
            value = value + jnp.dot(
                cols[(2 - kt) * PX : (2 - kt) * PX + ROWS, :],
                kt_ref[kt * 9 * CH : (kt + 1) * 9 * CH, :],
                preferred_element_type=F32,
            )
        return value

    near, middle, far = arriving
    each(near, "wait_recv")

    @pl.when(s < 3)
    def _():
        middle.wait_recv()

    fill(range(4), 0, 0)

    @pl.when(zh == 0)
    def _():
        each(far, "wait_recv")
        fill(range(4, 6), 1, 32)

    @pl.when(zh == 1)
    def _():
        gcol[ROWS:, :] = jnp.zeros((2 * PX, 9 * CH), BF16)
        ccol[ROWS:, :] = jnp.zeros((2 * PX, 9 * CH), BF16)

    da[...] = convolve(gcol)

    @pl.when(s == 3)
    def _():
        gcen[...] = gc[0:ROWS, :].astype(F32)
        ccol[...] = jnp.zeros_like(ccol)

    @pl.when(s < 3)
    def _():
        remote(zg.at[pl.ds(0, 8)], unear, tsem.at[3], cpeer).wait_recv()
        fill_correction(range(4), 0, 0, unear[...])

        @pl.when(zh == 0)
        def _():
            remote(zg.at[pl.ds(0, 8)], ufar, tsem.at[2], cpeer).wait_recv()
            fill_correction(range(4, 6), 1, 32, ufar[...])

        da[...] = da[...] - convolve(ccol)

    dh3 = (da[...] * dfac[...]).reshape(FR, PX, CH)
    dh_sum = jnp.sum(dh3, axis=1)
    dhx_sum = jnp.sum(dh3 * xhat[...].reshape(FR, PX, CH), axis=1)
    gain_part = jnp.sum(dhx_sum, axis=0, keepdims=True)
    bias_part = jnp.sum(dh_sum, axis=0, keepdims=True)
    ua[core] = jnp.concatenate(
        [
            grouped(dh_sum * gain, dhx_sum * gain),
            gain_part[:, :128], gain_part[:, 128:], bias_part[:, :128], bias_part[:, 128:],
            jnp.zeros((4, 128), F32),
        ],
        axis=0,
    )
    ua_copy = core_sum_copy(ua, ucs)
    ua_copy.start()

    w = gcen[...] + (rstd[:, None, :] * (dh3 * gain[None])).reshape(ROWS, CH)
    dfac[...] = w

    @pl.when(s == 3)
    def _():
        wait_sent(piece_copies(3, w_send, w_recv, w_sems), False)

    w_copies = piece_copies(s - 1, w_send, w_recv, w_sems)

    @pl.when(s > 0)
    def _():
        pack(w, wc, wh, wn)
        each(w_copies[0], "start")
        w_copies[1].start()

    ua_copy.wait()
    ub[chip] = ua[0] + ua[1]
    ub_copies = chip_copies(ub, ups)
    each(ub_copies, "start")

    @pl.when((s > 0) & (zh == 1))
    def _():
        each(w_copies[2], "start")

    def quarter(q):
        first, last = QUARTERS[q]

        def one(tap, carry):
            rows = pl.multiple_of(tap * CH, CH)
            lanes = pl.multiple_of((tap % 9) * CH, CH)
            frames = pl.multiple_of((2 - tap // 9) * PX, PX)
            part = jnp.dot(
                a_t[...], gcol[pl.ds(frames, ROWS), pl.ds(lanes, CH)], preferred_element_type=F32
            ) - jnp.dot(
                a_t[...], ccol[pl.ds(frames, ROWS), pl.ds(lanes, CH)], preferred_element_type=F32
            )
            dko[pl.ds(rows, CH), :] = jnp.where(core == 0, part[:, :128], part[:, 128:])
            dks[pl.ds(rows, CH), :] = jnp.where(core == 0, part[:, 128:], part[:, :128]).astype(BF16)
            return carry

        lax.fori_loop(first, last, one, 0)
        span = pl.ds(q * 1728, 1728)
        copy = remote(dks.at[span], dkr.at[span], csem.at[q], cpeer)
        copy.start()
        return copy

    pad8 = jnp.zeros((8, 128), F32)
    y_copies = []

    def x_first(q):
        return pltpu.make_async_remote_copy(
            src_ref=b0.at[q], dst_ref=rx.at[x], send_sem=xsem.at[q, 0], recv_sem=xsem.at[x, 1],
            device_id=at(s, q - x, zh, 0, 0), device_id_type=MESH,
        )

    def x_first_arrival(source):
        return pltpu.make_async_remote_copy(
            src_ref=b0.at[0], dst_ref=rx.at[source], send_sem=xsem.at[0, 0], recv_sem=xsem.at[source, 1],
            device_id=cpeer, device_id_type=MESH,
        )

    def join(q, copy):
        copy.wait()
        for half in range(4):
            at0 = q * 1728 + half * 432
            both_cores = dko[at0 : at0 + 432, :] + dkr[at0 : at0 + 432, :].astype(F32)
            dko[at0 : at0 + 432, :] = both_cores
            if half < 2:
                b0[q, half * 432 : half * 432 + 432, :] = both_cores.astype(BF16)
            else:
                for i in range(2):
                    piece = jnp.concatenate([both_cores[i * 216 : i * 216 + 216], pad8], axis=0)
                    b1[q, (half - 2) * 2 + i] = piece.astype(BF16)

        @pl.when(x != q)
        def _():
            x_first(q).start()

        for k in range(1, 4):
            y2 = (y + k) % 4
            c = remote(b1.at[q, y2], ry.at[y, q], ysem.at[q, k - 1], at(s, 0, zh, k, 0))
            c.start()
            y_copies.append(c)

    core_copies = [quarter(0), quarter(1)]
    each(ub_copies, "wait")
    total = jnp.sum(ub[...], axis=0)
    zg[...] = total
    near_sum = remote(zg.at[pl.ds(0, 8)], unear, tsem.at[3], at(s - 1, 0, zh, 0, 0))
    far_sum = remote(zg.at[pl.ds(0, 8)], ufar, tsem.at[2], at(s - 1, 0, 0, 0, 0))

    @pl.when(s > 0)
    def _():
        near_sum.start()

        @pl.when(zh == 1)
        def _():
            far_sum.start()

    join(0, core_copies[0])
    zg_copy = remote(zg, zgr, zsem.at[3], zpeer)
    zg_copy.start()
    both = spread(total[0:8] / ENTRIES)
    c1, c2 = rstd * both[0:4], rstd * both[4:8]
    xh = xhat[...].reshape(FR, PX, CH)
    final = dfac[...].reshape(FR, PX, CH) - c1[:, None, :] - xh * c2[:, None, :]
    final = final.astype(BF16).reshape(FR, 2, 32, CH)
    osend[...] = jnp.where(zh == 0, final[:, 1], final[:, 0])
    o_copy = remote(osend, orecv, zsem.at[2], zpeer)
    o_copy.start()
    out_ref[ours] = jnp.where(zh == 0, final[:, 0], final[:, 1])

    core_copies.append(quarter(2))
    join(1, core_copies[1])
    core_copies.append(quarter(3))
    join(2, core_copies[2])
    join(3, core_copies[3])

    pad4 = jnp.zeros((4, 128), F32)

    def cut(value, buf, i):
        buf[i, 0] = jnp.concatenate([value[0:108], pad4], axis=0).astype(BF16)
        buf[i, 1] = jnp.concatenate([value[108:216], pad4], axis=0).astype(BF16)

    each(y_copies, "wait")
    for q in range(4):
        acc = dko[pl.ds(pl.multiple_of(q * 1728 + 864 + y * 216, 8), 216), :]
        for k in range(1, 4):
            acc = acc + ry[(y + k) % 4, q].astype(F32)[0:216]
        cut(acc, p1, q)

    def to_owner(plane_id, i, dc):
        dx, dy = (i, 0) if plane_id else (0, i)
        index = (x + i) % 4 if plane_id else (y + i) % 4
        slot = x if plane_id else y
        buf = p1 if plane_id else p0
        return pltpu.make_async_remote_copy(
            src_ref=buf.at[index, (core + dc) % 2], dst_ref=r2.at[core, zh, slot],
            send_sem=psem.at[plane_id, 0, i * 2 + dc], recv_sem=psem.at[zh, 1, i * 2 + dc],
            device_id=at(s, dx, plane_id, dy, dc), device_id_type=MESH,
        )

    def deliver(plane_id):
        for i in range(4):
            for dc in range(2):
                if (i, dc) != (0, 0):
                    to_owner(plane_id, i, dc).start()

        @pl.when(zh != plane_id)
        def _():
            to_owner(plane_id, 0, 0).start()

        @pl.when(zh == plane_id)
        def _():
            buf, slot = (p1, x) if plane_id else (p0, y)
            r2[core, zh, slot] = buf[slot, core]

    deliver(1)
    for k in range(1, 4):
        x_first_arrival((x + k) % 4).wait_recv()
    for half in range(2):
        acc = dko[pl.ds(pl.multiple_of(x * 1728 + half * 432, 16), 432), :]
        for k in range(1, 4):
            acc = acc + rx[(x + k) % 4, half * 432 : half * 432 + 432, :].astype(F32)
        cut(acc[0:216], p0, half * 2)
        cut(acc[216:432], p0, half * 2 + 1)
    deliver(0)

    zg_copy.wait()
    sums = (zg[...] + zgr[...]) * SCALE
    gout_ref[:, 0:128] = sums[8:9]
    gout_ref[:, 128:256] = sums[9:10]
    bout_ref[:, 0:128] = sums[10:11]
    bout_ref[:, 128:256] = sums[11:12]
    o_copy.wait()
    out_ref[theirs] = orecv[...]

    @pl.when(s > 0)
    def _():
        wait_sent(piece_copies(s - 1, x_send, x_recv, x_sems), True)
        wait_sent(w_copies, True)
        xt_near.wait_send()
        near_sum.wait_send()

        @pl.when(zh == 1)
        def _():
            xt_far.wait_send()
            far_sum.wait_send()

    for q in range(4):

        @pl.when(x != q)
        def _():
            x_first(q).wait_send()

    for source in range(2):
        for j in range(8):
            arrival = pltpu.make_async_remote_copy(
                src_ref=p0.at[0, 0], dst_ref=r2.at[0, 0, 0], send_sem=psem.at[0, 0, j],
                recv_sem=psem.at[source, 1, j], device_id=cpeer, device_id_type=MESH,
            )
            if j:
                arrival.wait_recv()
            else:

                @pl.when(zh != source)
                def _():
                    arrival.wait_recv()

    for half in range(2):
        acc = jnp.zeros((112, 128), F32)
        for source in range(2):
            for i in range(4):
                acc = acc + r2[half, source, i].astype(F32)
        kout_ref[:, half * 128 : half * 128 + 128] = acc[0:108] * SCALE

    for plane_id in range(2):
        for i in range(4):
            for dc in range(2):
                if (i, dc) != (0, 0):
                    to_owner(plane_id, i, dc).wait_send()
                else:

                    @pl.when(zh != plane_id)
                    def _():
                        to_owner(plane_id, 0, 0).wait_send()


def on_device(saved_inputs, cotangent, kernels, gains, biases):
    inputs = saved_inputs.reshape(8, 32, CH)
    seeds = cotangent.reshape(8, 32, CH)
    vmem = pl.BlockSpec(memory_space=pltpu.VMEM)
    hbm = pl.BlockSpec(memory_space=pltpu.HBM)
    v = pltpu.VMEM
    dma = pltpu.SemaphoreType.DMA
    out, kout, gout, bout = pl.pallas_call(
        kernel,
        out_shape=(
            jax.ShapeDtypeStruct((8, 32, CH), BF16),
            jax.ShapeDtypeStruct((108, CH), F32),
            jax.ShapeDtypeStruct((1, CH), F32),
            jax.ShapeDtypeStruct((1, CH), F32),
        ),
        in_specs=[hbm] * 5,
        out_specs=[vmem] * 4,
        scratch_shapes=[
            v((8, 32, CH), BF16), v((8, 32, CH), BF16), v((27 * CH, CH), BF16), v((1, CH), F32), v((1, CH), F32),
            v((FR, 32, CH), BF16), v((FR, 32, CH), BF16), v((FR, 32, CH), BF16), v((FR, 32, CH), BF16),
            v((ROWS, CH), F32), v((32, CH), F32),
            v((ROWS, CH), BF16), v((4, 32, CH), BF16), v((4, 16, CH), BF16),
            v((ALL, CH), BF16), v((4, 48, CH), BF16), v((2, 4, 16, CH), BF16),
            v((ROWS, CH), BF16), v((4, 32, CH), BF16), v((4, 16, CH), BF16),
            v((ALL, CH), BF16), v((4, 48, CH), BF16), v((2, 4, 16, CH), BF16),
            v((ALL, CH), F32), v((4, 48, CH), F32), v((2, 4, 16, CH), F32), v((60, 24, CH), F32),
            v((ROWS, CH), F32), v((ALL, 9 * CH), BF16), v((ALL, 9 * CH), BF16), v((27 * CH, CH), BF16),
            v((CH, ROWS), BF16), v((ROWS, CH), F32), v((ROWS, CH), F32), v((ROWS, CH), F32),
            v((2, 8, 128), F32), v((16, 8, 128), F32), v((2, 16, 128), F32), v((16, 16, 128), F32),
            v((8, 128), F32), v((8, 128), F32), v((8, 128), F32), v((2, 8, 128), F32), v((8, CH), F32),
            v((16, 128), F32), v((16, 128), F32),
            v((27 * CH, 128), F32), v((27 * CH, 128), BF16), v((27 * CH, 128), BF16),
            v((4, 864, 128), BF16), v((4, 4, 224, 128), BF16), v((4, 864, 128), BF16), v((4, 4, 224, 128), BF16),
            v((4, 2, 112, 128), BF16), v((4, 2, 112, 128), BF16), v((2, 2, 4, 112, 128), BF16),
            dma((5,)), dma((4, 2)), dma((2, 2)), dma((2, 4, 2)), dma((2, 4, 2)),
            dma((2, 2)), dma((2, 4, 2)), dma((2, 4, 2)),
            dma((2,)), dma((16, 2)), dma((2,)), dma((16, 2)), dma((4, 2)), dma((4, 2)),
            dma((4, 2)), dma((4, 3, 2)), dma((2, 2, 8)),
        ],
        compiler_params=pltpu.CompilerParams(
            collective_id=0, has_side_effects=True, vmem_limit_bytes=VMEM_LIMIT
        ),
        name="blocks",
    )(inputs, seeds, kernels[0], gains, biases)
    return out.reshape(1, 8, 1, 4, 8, CH), kout[None], gout, bout


def solution(mesh):
    in_specs = (
        P("section", None, "tile", None, None, None),
        P(None, "tile", None, None, None),
        P("section", None, None),
        P("section", None),
        P("section", None),
    )
    out_specs = (
        P("section", None, "tile", None, None, None),
        P("section", "tile", None),
        P("section", None),
        P("section", None),
    )
    return jax.shard_map(
        on_device, mesh=mesh, in_specs=in_specs, out_specs=out_specs, check_vma=False
    )
```

```python
import functools
import math

import jax
import jax.numpy as jnp
from jax import lax
from jax.experimental import pallas as pl
from jax.experimental.pallas import tpu as pltpu
from jax.sharding import PartitionSpec as P

CH = 256
GROUPS = 32
PER_GROUP = CH // GROUPS
FR = 4
PX = 64
ROWS = FR * PX
ALL = ROWS + 2 * PX
ENTRIES = float(64 * 32 * PER_GROUP)
SCALE = 1.0 / math.sqrt(8 * 64 * 32)
EPS = 1e-05
VMEM_LIMIT = 63 * 2**20
MESH = pl.DeviceIdType.MESH
SIDES = ((-1, 0), (1, 0), (0, -1), (0, 1))
CORNERS = ((-1, -1), (-1, 1), (1, -1), (1, 1))
AROUND = [(dx, dy, dc) for dx in (-1, 0, 1) for dy, dc in ((0, 0), (-1, 1), (0, 1), (1, 1))]
CHIPS = [(dx, dy) for dx in range(4) for dy in range(4)]
QUARTER = 1728
F32 = jnp.float32
BF16 = jnp.bfloat16


def kernel(
    x_hbm, cot_hbm, k_hbm, gain_hbm, bias_hbm,
    out_ref, kout_ref, gout_ref, bout_ref,
    x_ref, cot_ref, k_ref, gain_ref, bias_ref,
    xr, xst, xstr, osend, orecv, rf, strip, lrs, rows_s, nooks, lr,
    wc, wh, wn, gc, gh, gn, xwc, xwh, xwn, xgc, xgh, xgn,
    xc, xs, xn, gp, gcen, gcol, ccol, kt_ref, a_t, xhat, dfac, da,
    sa, sb, ua, ub, unear, ufar, xt, xtr, mom, zg, zgr,
    dko, dks, dkr, b0, b1, rx, ry, p0, p1, t0, t1, r2x, r2y, p3, r3,
    lsem, zsem, dsem, wgs, whs, wns, xgs, xhs, xns, acs, aps, ucs, ups, tsem, csem, xsem, ysem, xsem2, ysem2, psem,
):
    s = lax.axis_index("section")
    t = lax.axis_index("tile")
    x = t // 16
    zh = (t // 8) % 2
    y = (t // 2) % 4
    core = t % 2
    col = t % 8
    chip = x * 4 + y

    def at(sec, dx, z2, dy, dc):
        return (sec, ((x + dx + 4) % 4) * 16 + z2 * 8 + ((y + dy + 4) % 4) * 2 + (core + dc) % 2)

    def beside(sec, dx, z2, dcol):
        return (sec, ((x + dx + 4) % 4) * 16 + z2 * 8 + (col + dcol + 8) % 8)

    zpeer = at(s, 0, 1 - zh, 0, 0)
    cpeer = at(s, 0, zh, 0, 1)

    def remote(src, dst, pair, device):
        return pltpu.make_async_remote_copy(
            src_ref=src, dst_ref=dst, send_sem=pair.at[0], recv_sem=pair.at[1],
            device_id=device, device_id_type=MESH,
        )

    x_load = pltpu.make_async_copy(x_hbm, x_ref, lsem.at[0])
    cot_load = pltpu.make_async_copy(cot_hbm, cot_ref, lsem.at[1])
    k_load = pltpu.make_async_copy(k_hbm, k_ref, lsem.at[2])
    gain_load = pltpu.make_async_copy(gain_hbm, gain_ref, lsem.at[3])
    bias_load = pltpu.make_async_copy(bias_hbm, bias_ref, lsem.at[4])
    x_load.start()
    gain_load.start()
    bias_load.start()

    @pl.when(s == 3)
    def _():
        cot_load.start()

    k_load.start()

    barrier = pltpu.get_barrier_semaphore()

    def greet(device):
        pl.semaphore_signal(barrier, inc=1, device_id=device, device_id_type=MESH)

    plane = [(dx, 0, dy, 0) for dx, dy in CHIPS if (dx, dy) != (0, 0)]
    plane += [(0, 1, 0, 0), (0, 1, 0, 1), (0, 0, 0, 1)]
    for dx, z, dy, dc in plane:
        greet(at(s, dx, (zh + z) % 2, dy, dc))

    @pl.when(s < 3)
    def _():
        for dx, dy, dc in AROUND:
            greet(at(s + 1, dx, zh, dy, dc))

        @pl.when(zh == 0)
        def _():
            for dx, dy, dc in AROUND:
                greet(at(s + 1, dx, 1, dy, dc))

    @pl.when(s == 3)
    def _():
        for dx, dy, dc in AROUND:
            if (dx, dy, dc) != (0, 0, 0):
                greet(at(3, dx, zh, dy, dc))
            greet(at(3, dx, 1 - zh, dy, dc))

    expected = len(plane) + jnp.where(s > 0, (1 + zh) * len(AROUND), 0)
    expected = expected + jnp.where(s == 3, 2 * len(AROUND) - 1, 0)
    pl.semaphore_wait(barrier, expected)

    theirs = pl.ds((1 - zh) * FR, FR)
    ours = pl.ds(zh * FR, FR)
    x_copy = remote(x_hbm.at[theirs], xr, zsem.at[0], zpeer)

    def patch(own, other):
        own = own.astype(F32)
        other = other.astype(F32)
        upper = jnp.where(zh == 0, own, other)
        lower = jnp.where(zh == 0, other, own)
        return jnp.concatenate([upper, lower], axis=1).reshape(ROWS, CH)

    def indicator(shape, channel_dim):
        channel = lax.broadcasted_iota(jnp.int32, shape, channel_dim)
        group = lax.broadcasted_iota(jnp.int32, shape, 1 - channel_dim)
        return (channel // PER_GROUP == group).astype(F32)

    def grouped(first, second):
        return jnp.dot(
            jnp.concatenate([first, second], axis=0), indicator((CH, 128), 0),
            precision=lax.Precision.HIGHEST, preferred_element_type=F32,
        )

    def spread(groups):
        return jnp.dot(
            groups, indicator((128, CH), 1), precision=lax.Precision.HIGHEST, preferred_element_type=F32
        )

    def core_sum_copy(buf, pair):
        return remote(buf.at[core], buf.at[core], pair, cpeer)

    def chip_copies(buf, sems):
        return [
            remote(buf.at[chip], buf.at[chip], sems.at[i], at(s, dx, zh, dy, 0))
            for i, (dx, dy) in enumerate(CHIPS) if i
        ]

    x_load.wait()

    def tile_sums(frames):
        value = x_ref[frames].astype(F32)
        return grouped(jnp.sum(value, axis=1), jnp.sum(value * value, axis=1))

    xst[...] = tile_sums(theirs)
    xst_copy = remote(xst, xstr, zsem.at[1], zpeer)
    xst_copy.start()
    own_sums = tile_sums(ours)

    def pack(value, center, sides, corners):
        rf[...] = value
        center[...] = value.astype(BF16).reshape(FR, 2, 32, CH)
        v4 = value.reshape(FR, 8, 8, CH)
        sides[0] = v4[:, 0].reshape(32, CH).astype(BF16)
        sides[1] = v4[:, 7].reshape(32, CH).astype(BF16)
        for i, lead in ((2, 0), (3, 7)):
            for f in range(FR):
                rows = [rf[f * PX + r * 8 + lead : f * PX + r * 8 + lead + 1, :] for r in range(8)]
                strip[f * 8 : f * 8 + 8, :] = jnp.concatenate(rows, axis=0)
            sides[i] = strip[...].astype(BF16)
        for i, pixel in enumerate((0, 7, 56, 63)):
            rows = [rf[f * PX + pixel : f * PX + pixel + 1, :] for f in range(FR)]
            corners[i] = jnp.concatenate(rows + [jnp.zeros((12, CH), F32)], axis=0).astype(BF16)

    def piece_copies(sec, send, recv, sems):
        center, sides, corners = send
        center_r, sides_r, corners_r = recv
        gs, hs, ns = sems
        near, far = [], []
        for i, (dx, dc) in enumerate(CORNERS):
            near.append(remote(corners.at[i], corners_r.at[i, 0], ns.at[0, i], beside(sec, dx, zh, dc)))
            far.append(remote(corners.at[i], corners_r.at[i, 1], ns.at[1, i], beside(sec, dx, 0, dc)))
        for i, (dx, dc) in enumerate(SIDES):
            near.append(remote(sides.at[i], sides_r.at[i, pl.ds(0, 32)], hs.at[0, i], beside(sec, dx, zh, dc)))
            far.append(
                remote(sides.at[i, pl.ds(0, 16)], sides_r.at[i, pl.ds(32, 16)], hs.at[1, i], beside(sec, dx, 0, dc))
            )
        middle = remote(center, center_r.at[pl.ds(0, FR)], gs.at[0], beside(sec, 0, zh, 0))
        far.append(
            remote(center.at[pl.ds(0, 2)], center_r.at[pl.ds(FR, 2)], gs.at[1], beside(sec, 0, 0, 0))
        )
        return near, middle, far

    def each(copies, what):
        for c in copies:
            getattr(c, what)()

    def send_pieces(copies, with_middle):
        near, middle, far = copies
        each(near, "start")
        if with_middle:
            middle.start()

        @pl.when(zh == 1)
        def _():
            each(far, "start")

    def wait_sent(copies, with_middle):
        near, middle, far = copies
        each(near + ([middle] if with_middle else []), "wait_send")

        @pl.when(zh == 1)
        def _():
            each(far, "wait_send")

    def wait_received(copies, with_middle):
        near, middle, far = copies
        each(near + ([middle] if with_middle else []), "wait_recv")

        @pl.when(zh == 0)
        def _():
            each(far, "wait_recv")

    w_send, w_recv, w_sems = (wc, wh, wn), (gc, gh, gn), (wgs, whs, wns)
    x_send, x_recv, x_sems = (xwc, xwh, xwn), (xgc, xgh, xgn), (xgs, xhs, xns)

    frames_of = (pl.ds(0, 6), pl.ds(4, 4))
    count_of = (6, 4)

    def direct_copies(plane_id):
        n = count_of[plane_id]
        lead = 4 * plane_id
        lr_rows = pl.ds(16 * plane_id, 32 - 16 * plane_id)
        row_rows = pl.ds(8 * lead, 8 * n)
        down = 2 * zh - 1
        pair = dsem.at[plane_id]

        def send(src, dst, slot, device):
            return pltpu.make_async_remote_copy(
                src_ref=src, dst_ref=dst, send_sem=pair.at[0, slot], recv_sem=dsem.at[zh, 1, slot],
                device_id=device, device_id_type=MESH,
            )

        nook_rows = pl.ds(plane_id, 2 - plane_id)
        landing = pl.ds(0, 2 - plane_id)
        copies = [
            send(nooks.at[0, nook_rows], gn.at[2 * zh, landing], 3, beside(3, down, plane_id, -1)),
            send(nooks.at[1, nook_rows], gn.at[2 * zh + 1, landing], 4, beside(3, down, plane_id, 1)),
            send(rows_s.at[row_rows], gh.at[zh, pl.ds(0, 8 * n)], 2, beside(3, down, plane_id, 0)),
            send(lrs.at[0, lr_rows], lr.at[0, zh, pl.ds(0, 32 - 16 * plane_id)], 0, beside(3, 0, plane_id, -1)),
            send(lrs.at[1, lr_rows], lr.at[1, zh, pl.ds(0, 32 - 16 * plane_id)], 1, beside(3, 0, plane_id, 1)),
        ]
        center = send(
            cot_hbm.at[frames_of[plane_id]], gc.at[pl.ds(0, n), zh], 5, beside(3, 0, plane_id, 0)
        )
        return copies, center

    def own_half(plane_id):
        return pltpu.make_async_copy(
            cot_hbm.at[frames_of[plane_id]], gc.at[pl.ds(0, count_of[plane_id]), plane_id], lsem.at[5]
        )

    def direct_arrivals(plane_id):
        n = count_of[plane_id]
        arrivals = []
        for source in range(2):
            sizes = (
                lr.at[0, 0, pl.ds(0, 32 - 16 * plane_id)], lr.at[0, 0, pl.ds(0, 32 - 16 * plane_id)],
                gh.at[0, pl.ds(0, 8 * n)],
                gn.at[0, pl.ds(0, 2 - plane_id)], gn.at[0, pl.ds(0, 2 - plane_id)],
            ) + ((gc.at[pl.ds(0, n), 0],) if source != plane_id else ())
            for slot, ref in enumerate(sizes):
                arrivals.append(
                    pltpu.make_async_remote_copy(
                        src_ref=ref, dst_ref=ref, send_sem=dsem.at[0, 0, slot],
                        recv_sem=dsem.at[source, 1, slot], device_id=cpeer, device_id_type=MESH,
                    )
                )
        return arrivals

    @pl.when(s == 3)
    def _():
        for plane_id in range(2):

            @pl.when(zh == plane_id)
            def _():
                direct_copies(1 - plane_id)[1].start()
                own_half(plane_id).start()

        cot_load.wait()
        rf[...] = cot_ref[...].astype(F32).reshape(ROWS, CH)
        for i, lead in ((0, 0), (1, 7)):
            for f in range(8):
                picks = [rf[f * 32 + r * 8 + lead : f * 32 + r * 8 + lead + 1, :] for r in range(4)]
                strip[f * 4 : f * 4 + 4, :] = jnp.concatenate(picks, axis=0)
            lrs[i] = strip[...].astype(BF16)
        outer_rows = []
        for f in range(8):
            outer_rows.append(
                jnp.where(zh == 0, rf[f * 32 : f * 32 + 8, :], rf[f * 32 + 24 : f * 32 + 32, :])
            )
        rows_s[...] = jnp.concatenate(outer_rows, axis=0).astype(BF16)
        for i, end in ((0, 0), (1, 7)):
            for part in range(2):
                picks = [outer_rows[part * 4 + f][end : end + 1] for f in range(4)]
                nooks[i, part] = jnp.concatenate(picks + [jnp.zeros((12, CH), F32)], axis=0).astype(BF16)
        for plane_id in (1, 0):
            each(direct_copies(plane_id)[0], "start")
        x_copy.start()

    def direct_done():
        for plane_id in range(2):

            @pl.when(zh == plane_id)
            def _():
                each(direct_arrivals(plane_id), "wait_recv")
                own_half(plane_id).wait()
                n = count_of[plane_id]
                for i in range(2):
                    halves = [lr[i, z2].astype(F32)[0 : 4 * n].reshape(n, 4, CH) for z2 in range(2)]
                    gh[2 + i, 0 : 8 * n, :] = (
                        jnp.concatenate(halves, axis=1).reshape(8 * n, CH).astype(BF16)
                    )

            each(direct_copies(plane_id)[0], "wait_send")

            @pl.when(zh != plane_id)
            def _():
                direct_copies(plane_id)[1].wait_send()

    xst_copy.wait()
    sa[core] = own_sums + xstr[...]
    sa_copy = core_sum_copy(sa, acs)
    sa_copy.start()
    sa_copy.wait()
    sb[chip] = sa[0] + sa[1]
    sb_copies = chip_copies(sb, aps)
    each(sb_copies, "start")

    @pl.when(s < 3)
    def _():
        x_copy.start()

    k_load.wait()

    def flip(i, carry):
        rows = pl.ds(pl.multiple_of(i * CH, CH), CH)
        kt_ref[rows, :] = jnp.transpose(k_ref[rows, :])
        return carry

    lax.fori_loop(0, 27, flip, 0)

    x_copy.wait()
    xv = patch(x_ref[ours], xr[...])
    xhat[...] = xv

    @pl.when(s > 0)
    def _():
        pack(xv, xwc, xwh, xwn)
        send_pieces(piece_copies(s - 1, x_send, x_recv, x_sems), True)

    gain_load.wait()
    bias_load.wait()
    each(sb_copies, "wait")
    xt[...] = jnp.sum(sb[...], axis=0)
    xt_near = remote(xt, xtr.at[0], tsem.at[0], at(s - 1, 0, zh, 0, 0))
    xt_far = remote(xt, xtr.at[1], tsem.at[1], at(s - 1, 0, 0, 0, 0))

    @pl.when(s > 0)
    def _():
        xt_near.start()

        @pl.when(zh == 1)
        def _():
            xt_far.start()

    def moments(total):
        total = spread(total / ENTRIES)
        mean = total[0:4]
        return mean, lax.rsqrt(total[4:8] - mean * mean + EPS)

    mean, rstd = moments(xt[...])
    gain = gain_ref[...]
    xh = (xhat[...].reshape(FR, PX, CH) - mean[:, None, :]) * rstd[:, None, :]
    h = xh * gain[None] + bias_ref[...][None]
    sg = jax.nn.sigmoid(h)
    xhat[...] = xh.reshape(ROWS, CH)
    dfac[...] = (sg * (1.0 + h * (1.0 - sg))).reshape(ROWS, CH)
    a_t[...] = jnp.transpose((h * sg).reshape(ROWS, CH)).astype(BF16)

    @pl.when(s < 3)
    def _():
        wait_received(piece_copies(s, x_send, x_recv, x_sems), True)
        remote(xt, xtr.at[0], tsem.at[0], cpeer).wait_recv()

        @pl.when(zh == 0)
        def _():
            remote(xt, xtr.at[1], tsem.at[1], cpeer).wait_recv()

        def normalise(frames, part, row0):
            mean_up, rstd_up = moments(xtr[part])
            n = len(frames)
            mom[frames[0] : frames[0] + n, :] = rstd_up[0:n]
            m, r = mean_up[0:n][:, None, :], rstd_up[0:n][:, None, :]
            px = slice(frames[0] * PX, (frames[0] + n) * PX)
            up = xgc[frames[0] : frames[0] + n].astype(F32).reshape(n, PX, CH)
            xc[px, :] = ((up - m) * r).reshape(n * PX, CH)
            for i in range(4):
                side = xgh[i, row0 : row0 + 8 * n, :].astype(F32).reshape(n, 8, CH)
                xs[i, row0 : row0 + 8 * n, :] = ((side - m) * r).reshape(8 * n, CH)
                xn[part, i, 0:n, :] = (xgn[i, part].astype(F32)[0:n] - mean_up[0:n]) * rstd_up[0:n]

        normalise(range(4), 0, 0)

        @pl.when(zh == 0)
        def _():
            normalise(range(4, 6), 1, 32)

    arriving = piece_copies(s, w_send, w_recv, w_sems)

    edge = (x > 0, x < 3, col > 0, col < 7)

    def columns(frames, center, sides, corners, out):
        top = jnp.where(edge[0], sides[1], 0.0)
        bottom = jnp.where(edge[1], sides[0], 0.0)
        left = jnp.where(edge[2], sides[3], 0.0)
        right = jnp.where(edge[3], sides[2], 0.0)
        top_left = jnp.where(edge[0] & edge[2], corners[3], 0.0)
        top_right = jnp.where(edge[0] & edge[3], corners[2], 0.0)
        bottom_left = jnp.where(edge[1] & edge[2], corners[1], 0.0)
        bottom_right = jnp.where(edge[1] & edge[3], corners[0], 0.0)
        center = center.reshape(len(frames), 8, 8, CH)
        for i, f in enumerate(frames):
            base = f * 10
            cell = slice(i * 8, i * 8 + 8)
            gp[base + 1 : base + 9, 8:16, :] = center[i]
            gp[base, 8:16, :] = top[cell]
            gp[base + 9, 8:16, :] = bottom[cell]
            for r in range(8):
                gp[base + 1 + r, 7:8, :] = left[i * 8 + r : i * 8 + r + 1]
                gp[base + 1 + r, 16:17, :] = right[i * 8 + r : i * 8 + r + 1]
            gp[base, 7:8, :] = top_left[i : i + 1]
            gp[base, 16:17, :] = top_right[i : i + 1]
            gp[base + 9, 7:8, :] = bottom_left[i : i + 1]
            gp[base + 9, 16:17, :] = bottom_right[i : i + 1]
            for ox in range(3):
                band = gp[base : base + 10, 7 + ox : 15 + ox, :]
                for oy in range(3):
                    tap = (2 - oy) * 3 + (2 - ox)
                    out[f * PX : f * PX + PX, tap * CH : tap * CH + CH] = (
                        band[oy : oy + 8].reshape(PX, CH).astype(BF16)
                    )

    def fill(frames, part, row0):
        n = len(frames)
        columns(
            frames, gc[frames[0] : frames[0] + n].astype(F32),
            [gh[i, row0 : row0 + 8 * n, :].astype(F32) for i in range(4)],
            [gn[i, part].astype(F32)[0:n] for i in range(4)], gcol,
        )

    def fill_correction(frames, part, row0, sums):
        n = len(frames)
        both = spread(sums / ENTRIES)
        r_up = mom[frames[0] : frames[0] + n, :]
        c1, c2 = r_up * both[0:n], r_up * both[4 : 4 + n]

        def term(hat, rows):
            value = c1[:, None, :] + hat.reshape(n, rows, CH) * c2[:, None, :]
            return value.reshape(n * rows, CH)

        px = slice(frames[0] * PX, (frames[0] + n) * PX)
        center = term(xc[px, :], PX)
        if part == 0:
            gcen[...] = gc[0:FR].astype(F32).reshape(ROWS, CH) - center
        columns(
            frames, center, [term(xs[i, row0 : row0 + 8 * n, :], 8) for i in range(4)],
            [c1 + xn[part, i, 0:n, :] * c2 for i in range(4)], ccol,
        )

    def convolve(cols):
        value = jnp.zeros((ROWS, CH), F32)
        for kt in range(3):
            value = value + jnp.dot(
                cols[(2 - kt) * PX : (2 - kt) * PX + ROWS, :],
                kt_ref[kt * 9 * CH : (kt + 1) * 9 * CH, :],
                preferred_element_type=F32,
            )
        return value

    near, middle, far = arriving

    @pl.when(s == 3)
    def _():
        direct_done()

    @pl.when(s < 3)
    def _():
        each(near, "wait_recv")
        middle.wait_recv()

    fill(range(4), 0, 0)

    @pl.when(zh == 0)
    def _():
        @pl.when(s < 3)
        def _():
            each(far, "wait_recv")

        fill(range(4, 6), 1, 32)

    @pl.when(zh == 1)
    def _():
        gcol[ROWS:, :] = jnp.zeros((2 * PX, 9 * CH), BF16)
        ccol[ROWS:, :] = jnp.zeros((2 * PX, 9 * CH), BF16)

    def taps(first, last):
        def one(tap, carry):
            rows = pl.multiple_of(tap * CH, CH)
            lanes = pl.multiple_of((tap % 9) * CH, CH)
            frames = pl.multiple_of((2 - tap // 9) * PX, PX)
            part = jnp.dot(
                a_t[...], gcol[pl.ds(frames, ROWS), pl.ds(lanes, CH)], preferred_element_type=F32
            ) - jnp.dot(
                a_t[...], ccol[pl.ds(frames, ROWS), pl.ds(lanes, CH)], preferred_element_type=F32
            )
            dko[pl.ds(rows, CH), :] = jnp.where(core == 0, part[:, :128], part[:, 128:])
            dks[pl.ds(rows, CH), :] = jnp.where(core == 0, part[:, 128:], part[:, :128]).astype(BF16)
            return carry

        lax.fori_loop(first, last, one, 0)

    def own_rows(step, offset, count):
        q = (x + 1 + step) % 4
        return pl.ds(pl.multiple_of(q * QUARTER + offset, 8), count)

    def core_copy(step):
        q = (x + 1 + step) % 4
        span = pl.ds(pl.multiple_of(q * QUARTER, 16), QUARTER)
        return remote(dks.at[span], dkr.at[span], csem.at[step], cpeer)

    def quarter(step):
        q = (x + 1 + step) % 4
        if step == 0:
            @pl.when(x < 3)
            def _():
                taps(7 * x + 6, 7 * x + 7)

        if step < 3:
            taps(7 * q, 7 * q + 7 - q // 3)
        else:
            taps(7 * x, 7 * x + 6)
        core_copy(step).start()

    def x_first(step):
        return remote(b0.at[step], rx.at[step], xsem.at[step], at(s, step + 1, zh, 0, 0))

    def y_first(step, k):
        return remote(b1.at[step, (y + k) % 4], ry.at[k - 1, step], ysem.at[step, k - 1], at(s, 0, zh, k, 0))

    pad8 = jnp.zeros((8, 128), F32)

    def join(step):
        core_copy(step).wait()
        for half in range(4):
            rows = own_rows(step, half * 432, 432)
            both_cores = dko[rows, :] + dkr[rows, :].astype(F32)
            dko[rows, :] = both_cores
            if half >= 2:
                for i in range(2):
                    piece = jnp.concatenate([both_cores[i * 216 : i * 216 + 216], pad8], axis=0)
                    b1[step, (half - 2) * 2 + i] = piece.astype(BF16)
            elif step < 3:
                b0[step, half * 432 : half * 432 + 432, :] = both_cores.astype(BF16)
        if step < 3:
            x_first(step).start()
        for k in range(1, 4):
            y_first(step, k).start()

    def then_x(step):
        return remote(p1.at[step], r2x.at[step], xsem2.at[step], at(s, step + 1, zh, 0, 0))

    def then_y(k):
        return remote(p0.at[(y + k) % 4], r2y.at[k - 1], ysem2.at[k - 1], at(s, 0, zh, k, 0))

    def sum_y(step):
        for k in range(1, 4):
            y_first(step, k).wait()
        acc = dko[own_rows(step, 864 + y * 216, 216), :]
        for k in range(3):
            acc = acc + ry[k, step].astype(F32)[0:216]
        if step < 3:
            p1[step] = jnp.concatenate([acc, pad8], axis=0).astype(BF16)
            then_x(step).start()
        else:
            t1[...] = acc

    def sum_x():
        for step in range(3):
            x_first(step).wait()
        for half in range(2):
            acc = dko[own_rows(3, half * 432, 432), :]
            for k in range(3):
                acc = acc + rx[k, half * 432 : half * 432 + 432, :].astype(F32)
            for i in range(2):
                piece = acc[i * 216 : i * 216 + 216]
                t0[half * 2 + i] = piece
                p0[half * 2 + i] = jnp.concatenate([piece, pad8], axis=0).astype(BF16)
        for k in range(1, 4):
            then_y(k).start()

    da[...] = convolve(gcol)

    @pl.when(s == 3)
    def _():
        gcen[...] = gc[0:FR].astype(F32).reshape(ROWS, CH)
        ccol[...] = jnp.zeros_like(ccol)

    @pl.when(s < 3)
    def _():
        remote(zg.at[pl.ds(0, 8)], unear, tsem.at[3], cpeer).wait_recv()
        fill_correction(range(4), 0, 0, unear[...])

        @pl.when(zh == 0)
        def _():
            remote(zg.at[pl.ds(0, 8)], ufar, tsem.at[2], cpeer).wait_recv()
            fill_correction(range(4, 6), 1, 32, ufar[...])


    @pl.when(s == 0)
    def _():
        quarter(0)
        quarter(1)
        join(0)
        quarter(2)
        join(1)
        quarter(3)
        join(2)
        join(3)

    @pl.when(s < 3)
    def _():
        da[...] = da[...] - convolve(ccol)

    dh3 = (da[...] * dfac[...]).reshape(FR, PX, CH)
    dh_sum = jnp.sum(dh3, axis=1)
    dhx_sum = jnp.sum(dh3 * xhat[...].reshape(FR, PX, CH), axis=1)
    gain_part = jnp.sum(dhx_sum, axis=0, keepdims=True)
    bias_part = jnp.sum(dh_sum, axis=0, keepdims=True)
    ua[core] = jnp.concatenate(
        [
            grouped(dh_sum * gain, dhx_sum * gain),
            gain_part[:, :128], gain_part[:, 128:], bias_part[:, :128], bias_part[:, 128:],
            jnp.zeros((4, 128), F32),
        ],
        axis=0,
    )
    ua_copy = core_sum_copy(ua, ucs)
    ua_copy.start()

    w = gcen[...] + (rstd[:, None, :] * (dh3 * gain[None])).reshape(ROWS, CH)
    dfac[...] = w

    w_copies = piece_copies(s - 1, w_send, w_recv, w_sems)

    @pl.when(s > 0)
    def _():
        pack(w, wc, wh, wn)
        each(w_copies[0], "start")
        w_copies[1].start()

    ua_copy.wait()
    ub[chip] = ua[0] + ua[1]
    ub_copies = chip_copies(ub, ups)
    each(ub_copies, "start")

    @pl.when((s > 0) & (zh == 1))
    def _():
        each(w_copies[2], "start")

    @pl.when(s > 0)
    def _():
        quarter(0)
        quarter(1)

    each(ub_copies, "wait")
    total = jnp.sum(ub[...], axis=0)
    zg[...] = total
    near_sum = remote(zg.at[pl.ds(0, 8)], unear, tsem.at[3], at(s - 1, 0, zh, 0, 0))
    far_sum = remote(zg.at[pl.ds(0, 8)], ufar, tsem.at[2], at(s - 1, 0, 0, 0, 0))

    @pl.when(s > 0)
    def _():
        near_sum.start()

        @pl.when(zh == 1)
        def _():
            far_sum.start()

    zg_copy = remote(zg, zgr, zsem.at[3], zpeer)
    zg_copy.start()
    both = spread(total[0:8] / ENTRIES)
    c1, c2 = rstd * both[0:4], rstd * both[4:8]
    xh = xhat[...].reshape(FR, PX, CH)
    final = dfac[...].reshape(FR, PX, CH) - c1[:, None, :] - xh * c2[:, None, :]
    final = final.astype(BF16).reshape(FR, 2, 32, CH)
    osend[...] = jnp.where(zh == 0, final[:, 1], final[:, 0])
    o_copy = remote(osend, orecv, zsem.at[2], zpeer)
    o_copy.start()
    out_ref[ours] = jnp.where(zh == 0, final[:, 0], final[:, 1])

    @pl.when(s > 0)
    def _():
        join(0)
        quarter(2)
        join(1)
        quarter(3)
        join(2)
        join(3)

    sum_y(0)
    sum_y(1)
    sum_y(2)
    sum_x()
    sum_y(3)

    pad4 = jnp.zeros((4, 128), F32)

    def to_owner(plane_id, dc):
        return pltpu.make_async_remote_copy(
            src_ref=p3.at[plane_id, (core + dc) % 2], dst_ref=r3.at[core, zh],
            send_sem=psem.at[plane_id, 0, dc], recv_sem=psem.at[zh, 1, dc],
            device_id=at(s, 0, plane_id, 0, dc), device_id_type=MESH,
        )

    def finish(plane_id):
        if plane_id:
            acc = t1[...]
            for step in range(3):
                then_x(step).wait()
                acc = acc + r2x[step].astype(F32)[0:216]
        else:
            acc = t0[y]
            for k in range(1, 4):
                then_y(k).wait()
                acc = acc + r2y[k - 1].astype(F32)[0:216]
        p3[plane_id, 0] = jnp.concatenate([acc[0:108], pad4], axis=0).astype(BF16)
        p3[plane_id, 1] = jnp.concatenate([acc[108:216], pad4], axis=0).astype(BF16)
        to_owner(plane_id, 1).start()

        @pl.when(zh != plane_id)
        def _():
            to_owner(plane_id, 0).start()

        @pl.when(zh == plane_id)
        def _():
            r3[core, zh] = p3[plane_id, core]

    finish(1)
    finish(0)

    zg_copy.wait()
    sums = (zg[...] + zgr[...]) * SCALE
    gout_ref[:, 0:128] = sums[8:9]
    gout_ref[:, 128:256] = sums[9:10]
    bout_ref[:, 0:128] = sums[10:11]
    bout_ref[:, 128:256] = sums[11:12]
    o_copy.wait()
    out_ref[theirs] = orecv[...]

    @pl.when(s > 0)
    def _():
        wait_sent(piece_copies(s - 1, x_send, x_recv, x_sems), True)
        wait_sent(w_copies, True)
        xt_near.wait_send()
        near_sum.wait_send()

        @pl.when(zh == 1)
        def _():
            xt_far.wait_send()
            far_sum.wait_send()

    for source in range(2):
        for dc in range(2):
            arrival = pltpu.make_async_remote_copy(
                src_ref=p3.at[0, 0], dst_ref=r3.at[0, 0], send_sem=psem.at[0, 0, dc],
                recv_sem=psem.at[source, 1, dc], device_id=cpeer, device_id_type=MESH,
            )
            if dc:
                arrival.wait_recv()
            else:

                @pl.when(zh != source)
                def _():
                    arrival.wait_recv()

    for half in range(2):
        value = r3[half, 0].astype(F32) + r3[half, 1].astype(F32)
        kout_ref[:, 0, half * 128 : half * 128 + 128] = value[0:108] * SCALE

    for plane_id in range(2):
        to_owner(plane_id, 1).wait_send()

        @pl.when(zh != plane_id)
        def _():
            to_owner(plane_id, 0).wait_send()


def write_out(*refs):
    for source, target in zip(refs[:4], refs[4:]):
        target[...] = source[...]


def on_device(saved_inputs, cotangent, kernels, gains, biases):
    inputs = saved_inputs.reshape(8, 32, CH)
    seeds = cotangent.reshape(8, 32, CH)
    vmem = pl.BlockSpec(memory_space=pltpu.VMEM)
    hbm = pl.BlockSpec(memory_space=pltpu.HBM)
    v = pltpu.VMEM
    dma = pltpu.SemaphoreType.DMA
    made = pl.pallas_call(
        kernel,
        out_shape=(
            jax.ShapeDtypeStruct((8, 32, CH), BF16),
            jax.ShapeDtypeStruct((108, 1, CH), F32),
            jax.ShapeDtypeStruct((1, CH), F32),
            jax.ShapeDtypeStruct((1, CH), F32),
        ),
        in_specs=[hbm] * 5,
        out_specs=[vmem] * 4,
        scratch_shapes=[
            v((8, 32, CH), BF16), v((8, 32, CH), BF16), v((27 * CH, CH), BF16), v((1, CH), F32), v((1, CH), F32),
            v((FR, 32, CH), BF16), v((8, 128), F32), v((8, 128), F32), v((FR, 32, CH), BF16), v((FR, 32, CH), BF16),
            v((ROWS, CH), F32), v((32, CH), F32),
            v((2, 32, CH), BF16), v((64, CH), BF16), v((2, 2, 16, CH), BF16), v((2, 2, 32, CH), BF16),
            v((FR, 2, 32, CH), BF16), v((4, 32, CH), BF16), v((4, 16, CH), BF16),
            v((6, 2, 32, CH), BF16), v((4, 48, CH), BF16), v((4, 2, 16, CH), BF16),
            v((FR, 2, 32, CH), BF16), v((4, 32, CH), BF16), v((4, 16, CH), BF16),
            v((6, 2, 32, CH), BF16), v((4, 48, CH), BF16), v((4, 2, 16, CH), BF16),
            v((ALL, CH), F32), v((4, 48, CH), F32), v((2, 4, 16, CH), F32), v((60, 24, CH), F32),
            v((ROWS, CH), F32), v((ALL, 9 * CH), BF16), v((ALL, 9 * CH), BF16), v((27 * CH, CH), BF16),
            v((CH, ROWS), BF16), v((ROWS, CH), F32), v((ROWS, CH), F32), v((ROWS, CH), F32),
            v((2, 8, 128), F32), v((16, 8, 128), F32), v((2, 16, 128), F32), v((16, 16, 128), F32),
            v((8, 128), F32), v((8, 128), F32), v((8, 128), F32), v((2, 8, 128), F32), v((8, CH), F32),
            v((16, 128), F32), v((16, 128), F32),
            v((27 * CH, 128), F32), v((27 * CH, 128), BF16), v((27 * CH, 128), BF16),
            v((3, 864, 128), BF16), v((4, 4, 224, 128), BF16), v((3, 864, 128), BF16), v((3, 4, 224, 128), BF16),
            v((4, 224, 128), BF16), v((3, 224, 128), BF16), v((4, 216, 128), F32), v((216, 128), F32),
            v((3, 224, 128), BF16), v((3, 224, 128), BF16), v((2, 2, 112, 128), BF16), v((2, 2, 112, 128), BF16),
            dma((6,)), dma((4, 2)), dma((2, 2, 6)), dma((2, 2)), dma((2, 4, 2)), dma((2, 4, 2)),
            dma((2, 2)), dma((2, 4, 2)), dma((2, 4, 2)),
            dma((2,)), dma((16, 2)), dma((2,)), dma((16, 2)), dma((4, 2)), dma((4, 2)),
            dma((3, 2)), dma((4, 3, 2)), dma((3, 2)), dma((3, 2)), dma((2, 2, 2)),
        ],
        compiler_params=pltpu.CompilerParams(
            collective_id=0, has_side_effects=True, vmem_limit_bytes=VMEM_LIMIT
        ),
        name="blocks",
    )(inputs, seeds, kernels[0], gains, biases)
    out, kout, gout, bout = pl.pallas_call(
        write_out,
        out_shape=tuple(jax.ShapeDtypeStruct(m.shape, m.dtype) for m in made),
        in_specs=[vmem] * 4,
        out_specs=[vmem] * 4,
        name="write_out",
    )(*made)
    return out.reshape(1, 8, 1, 4, 8, CH), kout.reshape(1, 108, CH), gout, bout


def solution(mesh):
    in_specs = (
        P("section", None, "tile", None, None, None),
        P(None, "tile", None, None, None),
        P("section", None, None),
        P("section", None),
        P("section", None),
    )
    out_specs = (
        P("section", None, "tile", None, None, None),
        P("section", "tile", None),
        P("section", None),
        P("section", None),
    )
    return jax.shard_map(
        on_device, mesh=mesh, in_specs=in_specs, out_specs=out_specs, check_vma=False
    )
```

```python
import functools
import math

import jax
import jax.numpy as jnp
from jax import lax
from jax.experimental import pallas as pl
from jax.experimental.pallas import tpu as pltpu
from jax.sharding import PartitionSpec as P

CH = 256
GROUPS = 32
PER_GROUP = CH // GROUPS
FR = 4
PX = 64
ROWS = FR * PX
ALL = ROWS + 2 * PX
ENTRIES = float(64 * 32 * PER_GROUP)
SCALE = 1.0 / math.sqrt(8 * 64 * 32)
EPS = 1e-05
VMEM_LIMIT = 63 * 2**20
MESH = pl.DeviceIdType.MESH
SIDES = ((-1, 0), (1, 0), (0, -1), (0, 1))
CORNERS = ((-1, -1), (-1, 1), (1, -1), (1, 1))
AROUND = [(dx, dy, dc) for dx in (-1, 0, 1) for dy, dc in ((0, 0), (-1, 1), (0, 1), (1, 1))]
CHIPS = sorted(
    ((dx, dy) for dx in range(4) for dy in range(4)),
    key=lambda d: (d != (0, 0), -min(d[0], 4 - d[0]) - min(d[1], 4 - d[1]), d),
)
QUARTER = 1728
F32 = jnp.float32
BF16 = jnp.bfloat16


def kernel(
    x_hbm, cot_hbm, k_hbm, gain_hbm, bias_hbm,
    out_ref, kout_ref, gout_ref, bout_ref,
    x_ref, cot_ref, k_ref, gain_ref, bias_ref,
    xr, xst, xstr, osend, orecv, rf, strip, lrs, rows_s, nooks, lr,
    wc, wh, wn, gc, gh, gn, xwc, xwh, xwn, xgc, xgh, xgn,
    xc, xs, xn, gp, gcen, cols, kt_ref, a_t, xhat, dfac, da, rs,
    sa, sb, ua, ub, unear, ufar, xt, xtr, mom, zg, zgr,
    dko, dks, dkr, b0, b1, rx, ry, p0, p1, t0, t1, r2x, r2y, p3, r3,
    lsem, zsem, dsem, wgs, whs, wns, xgs, xhs, xns, acs, aps, ucs, ups, tsem, csem, xsem, ysem, xsem2, ysem2, psem,
):
    s = lax.axis_index("section")
    t = lax.axis_index("tile")
    x = t // 16
    zh = (t // 8) % 2
    y = (t // 2) % 4
    core = t % 2
    col = t % 8
    chip = x * 4 + y

    def at(sec, dx, z2, dy, dc):
        return (sec, ((x + dx + 4) % 4) * 16 + z2 * 8 + ((y + dy + 4) % 4) * 2 + (core + dc) % 2)

    def beside(sec, dx, z2, dcol):
        return (sec, ((x + dx + 4) % 4) * 16 + z2 * 8 + (col + dcol + 8) % 8)

    zpeer = at(s, 0, 1 - zh, 0, 0)
    cpeer = at(s, 0, zh, 0, 1)

    def remote(src, dst, pair, device):
        return pltpu.make_async_remote_copy(
            src_ref=src, dst_ref=dst, send_sem=pair.at[0], recv_sem=pair.at[1],
            device_id=device, device_id_type=MESH,
        )

    x_load = pltpu.make_async_copy(x_hbm, x_ref, lsem.at[0])
    cot_load = pltpu.make_async_copy(cot_hbm, cot_ref, lsem.at[1])
    k_load = pltpu.make_async_copy(k_hbm, k_ref, lsem.at[2])
    gain_load = pltpu.make_async_copy(gain_hbm, gain_ref, lsem.at[3])
    bias_load = pltpu.make_async_copy(bias_hbm, bias_ref, lsem.at[4])
    x_load.start()
    gain_load.start()
    bias_load.start()

    @pl.when(s == 3)
    def _():
        cot_load.start()

    k_load.start()

    barrier = pltpu.get_barrier_semaphore()

    def greet(device):
        pl.semaphore_signal(barrier, inc=1, device_id=device, device_id_type=MESH)

    plane = [(dx, 0, dy, 0) for dx, dy in CHIPS if (dx, dy) != (0, 0)]
    plane += [(0, 1, 0, 0), (0, 1, 0, 1), (0, 0, 0, 1)]
    for dx, z, dy, dc in plane:
        greet(at(s, dx, (zh + z) % 2, dy, dc))

    @pl.when(s < 3)
    def _():
        for dx, dy, dc in AROUND:
            greet(at(s + 1, dx, zh, dy, dc))

        @pl.when(zh == 0)
        def _():
            for dx, dy, dc in AROUND:
                greet(at(s + 1, dx, 1, dy, dc))

    @pl.when(s == 3)
    def _():
        for dx, dy, dc in AROUND:
            if (dx, dy, dc) != (0, 0, 0):
                greet(at(3, dx, zh, dy, dc))
            greet(at(3, dx, 1 - zh, dy, dc))

    expected = len(plane) + jnp.where(s > 0, (1 + zh) * len(AROUND), 0)
    expected = expected + jnp.where(s == 3, 2 * len(AROUND) - 1, 0)
    pl.semaphore_wait(barrier, expected)

    theirs = pl.ds((1 - zh) * FR, FR)
    ours = pl.ds(zh * FR, FR)
    x_copy = remote(x_hbm.at[theirs], xr, zsem.at[0], zpeer)

    def patch(own, other):
        own = own.astype(F32)
        other = other.astype(F32)
        upper = jnp.where(zh == 0, own, other)
        lower = jnp.where(zh == 0, other, own)
        return jnp.concatenate([upper, lower], axis=1).reshape(ROWS, CH)

    def indicator(shape, channel_dim):
        channel = lax.broadcasted_iota(jnp.int32, shape, channel_dim)
        group = lax.broadcasted_iota(jnp.int32, shape, 1 - channel_dim)
        return (channel // PER_GROUP == group).astype(F32)

    def grouped(first, second):
        return jnp.dot(
            jnp.concatenate([first, second], axis=0), indicator((CH, 128), 0),
            precision=lax.Precision.HIGHEST, preferred_element_type=F32,
        )

    def spread(groups):
        return jnp.dot(
            groups, indicator((128, CH), 1), precision=lax.Precision.HIGHEST, preferred_element_type=F32
        )

    def core_sum_copy(buf, pair):
        return remote(buf.at[core], buf.at[core], pair, cpeer)

    def chip_copies(buf, sems):
        return [
            remote(buf.at[chip], buf.at[chip], sems.at[i], at(s, dx, zh, dy, 0))
            for i, (dx, dy) in enumerate(CHIPS) if i
        ]

    x_load.wait()

    def tile_sums(frames):
        value = x_ref[frames].astype(F32)
        return grouped(jnp.sum(value, axis=1), jnp.sum(value * value, axis=1))

    xst[...] = tile_sums(theirs)
    xst_copy = remote(xst, xstr, zsem.at[1], zpeer)
    xst_copy.start()

    @pl.when(s == 3)
    def _():
        x_copy.start()

    own_sums = tile_sums(ours)

    def each(copies, what):
        for c in copies:
            getattr(c, what)()

    def pack(value, send, copies):
        center, sides, corners = send
        near, middle, _ = copies
        rf[...] = value
        for i, pixel in enumerate((0, 7, 56, 63)):
            rows = [rf[f * PX + pixel : f * PX + pixel + 1, :] for f in range(FR)]
            corners[i] = jnp.concatenate(rows + [jnp.zeros((12, CH), F32)], axis=0).astype(BF16)
        each(near[0:4], "start")
        v4 = value.reshape(FR, 8, 8, CH)
        sides[0] = v4[:, 0].reshape(32, CH).astype(BF16)
        sides[1] = v4[:, 7].reshape(32, CH).astype(BF16)
        each(near[4:6], "start")
        for i, lead in ((2, 0), (3, 7)):
            for f in range(FR):
                rows = [rf[f * PX + r * 8 + lead : f * PX + r * 8 + lead + 1, :] for r in range(8)]
                strip[f * 8 : f * 8 + 8, :] = jnp.concatenate(rows, axis=0)
            sides[i] = strip[...].astype(BF16)
        each(near[6:8], "start")
        center[...] = value.astype(BF16).reshape(FR, 2, 32, CH)
        middle.start()

    def piece_copies(sec, send, recv, sems):
        center, sides, corners = send
        center_r, sides_r, corners_r = recv
        gs, hs, ns = sems
        near, far = [], []
        for i, (dx, dc) in enumerate(CORNERS):
            near.append(remote(corners.at[i], corners_r.at[i, 0], ns.at[0, i], beside(sec, dx, zh, dc)))
            far.append(remote(corners.at[i], corners_r.at[i, 1], ns.at[1, i], beside(sec, dx, 0, dc)))
        for i, (dx, dc) in enumerate(SIDES):
            near.append(remote(sides.at[i], sides_r.at[i, pl.ds(0, 32)], hs.at[0, i], beside(sec, dx, zh, dc)))
            far.append(
                remote(sides.at[i, pl.ds(0, 16)], sides_r.at[i, pl.ds(32, 16)], hs.at[1, i], beside(sec, dx, 0, dc))
            )
        middle = remote(center, center_r.at[pl.ds(0, FR)], gs.at[0], beside(sec, 0, zh, 0))
        far.append(
            remote(center.at[pl.ds(0, 2)], center_r.at[pl.ds(FR, 2)], gs.at[1], beside(sec, 0, 0, 0))
        )
        return near, middle, far

    def wait_sent(copies, with_middle):
        near, middle, far = copies
        each(near + ([middle] if with_middle else []), "wait_send")

        @pl.when(zh == 1)
        def _():
            each(far, "wait_send")

    def wait_received(copies, with_middle):
        near, middle, far = copies
        each(near + ([middle] if with_middle else []), "wait_recv")

        @pl.when(zh == 0)
        def _():
            each(far, "wait_recv")

    w_send, w_recv, w_sems = (wc, wh, wn), (gc, gh, gn), (wgs, whs, wns)
    x_send, x_recv, x_sems = (xwc, xwh, xwn), (xgc, xgh, xgn), (xgs, xhs, xns)

    frames_of = (pl.ds(0, 6), pl.ds(4, 4))
    count_of = (6, 4)

    def direct_copies(plane_id):
        n = count_of[plane_id]
        lead = 4 * plane_id
        lr_rows = pl.ds(16 * plane_id, 32 - 16 * plane_id)
        row_rows = pl.ds(8 * lead, 8 * n)
        down = 2 * zh - 1
        pair = dsem.at[plane_id]

        def send(src, dst, slot, device):
            return pltpu.make_async_remote_copy(
                src_ref=src, dst_ref=dst, send_sem=pair.at[0, slot], recv_sem=dsem.at[zh, 1, slot],
                device_id=device, device_id_type=MESH,
            )

        nook_rows = pl.ds(plane_id, 2 - plane_id)
        landing = pl.ds(0, 2 - plane_id)
        copies = [
            send(nooks.at[0, nook_rows], gn.at[2 * zh, landing], 3, beside(3, down, plane_id, -1)),
            send(nooks.at[1, nook_rows], gn.at[2 * zh + 1, landing], 4, beside(3, down, plane_id, 1)),
            send(rows_s.at[row_rows], gh.at[zh, pl.ds(0, 8 * n)], 2, beside(3, down, plane_id, 0)),
            send(lrs.at[0, lr_rows], lr.at[0, zh, pl.ds(0, 32 - 16 * plane_id)], 0, beside(3, 0, plane_id, -1)),
            send(lrs.at[1, lr_rows], lr.at[1, zh, pl.ds(0, 32 - 16 * plane_id)], 1, beside(3, 0, plane_id, 1)),
        ]
        center = send(
            cot_hbm.at[frames_of[plane_id]], gc.at[pl.ds(0, n), zh], 5, beside(3, 0, plane_id, 0)
        )
        return copies, center

    def own_half(plane_id):
        return pltpu.make_async_copy(
            cot_hbm.at[frames_of[plane_id]], gc.at[pl.ds(0, count_of[plane_id]), plane_id], lsem.at[5]
        )

    def direct_arrivals(plane_id):
        n = count_of[plane_id]
        arrivals = []
        for source in range(2):
            sizes = (
                lr.at[0, 0, pl.ds(0, 32 - 16 * plane_id)], lr.at[0, 0, pl.ds(0, 32 - 16 * plane_id)],
                gh.at[0, pl.ds(0, 8 * n)],
                gn.at[0, pl.ds(0, 2 - plane_id)], gn.at[0, pl.ds(0, 2 - plane_id)],
            ) + ((gc.at[pl.ds(0, n), 0],) if source != plane_id else ())
            for slot, ref in enumerate(sizes):
                arrivals.append(
                    pltpu.make_async_remote_copy(
                        src_ref=ref, dst_ref=ref, send_sem=dsem.at[0, 0, slot],
                        recv_sem=dsem.at[source, 1, slot], device_id=cpeer, device_id_type=MESH,
                    )
                )
        return arrivals

    @pl.when(s == 3)
    def _():
        for plane_id in range(2):

            @pl.when(zh == plane_id)
            def _():
                direct_copies(1 - plane_id)[1].start()
                own_half(plane_id).start()

        cot_load.wait()
        rf[...] = cot_ref[...].astype(F32).reshape(ROWS, CH)
        for i, lead in ((0, 0), (1, 7)):
            for f in range(8):
                picks = [rf[f * 32 + r * 8 + lead : f * 32 + r * 8 + lead + 1, :] for r in range(4)]
                strip[f * 4 : f * 4 + 4, :] = jnp.concatenate(picks, axis=0)
            lrs[i] = strip[...].astype(BF16)
        outer_rows = []
        for f in range(8):
            outer_rows.append(
                jnp.where(zh == 0, rf[f * 32 : f * 32 + 8, :], rf[f * 32 + 24 : f * 32 + 32, :])
            )
        rows_s[...] = jnp.concatenate(outer_rows, axis=0).astype(BF16)
        for i, end in ((0, 0), (1, 7)):
            for part in range(2):
                picks = [outer_rows[part * 4 + f][end : end + 1] for f in range(4)]
                nooks[i, part] = jnp.concatenate(picks + [jnp.zeros((12, CH), F32)], axis=0).astype(BF16)
        for plane_id in (1, 0):
            each(direct_copies(plane_id)[0], "start")

    def direct_done():
        for plane_id in range(2):

            @pl.when(zh == plane_id)
            def _():
                each(direct_arrivals(plane_id), "wait_recv")
                own_half(plane_id).wait()
                n = count_of[plane_id]
                for i in range(2):
                    halves = [lr[i, z2].astype(F32)[0 : 4 * n].reshape(n, 4, CH) for z2 in range(2)]
                    gh[2 + i, 0 : 8 * n, :] = (
                        jnp.concatenate(halves, axis=1).reshape(8 * n, CH).astype(BF16)
                    )

            each(direct_copies(plane_id)[0], "wait_send")

            @pl.when(zh != plane_id)
            def _():
                direct_copies(plane_id)[1].wait_send()

    xst_copy.wait()
    sa[core] = own_sums + xstr[...]
    sa_copy = core_sum_copy(sa, acs)
    sa_copy.start()
    sa_copy.wait()
    sb[chip] = sa[0] + sa[1]
    sb_copies = chip_copies(sb, aps)
    each(sb_copies, "start")

    @pl.when(s < 3)
    def _():
        x_copy.start()

    x_copy.wait()
    xv = patch(x_ref[ours], xr[...])
    xhat[...] = xv

    @pl.when(s > 0)
    def _():
        copies = piece_copies(s - 1, x_send, x_recv, x_sems)
        pack(xv, x_send, copies)

        @pl.when(zh == 1)
        def _():
            each(copies[2], "start")

    k_load.wait()

    def flip(i, carry):
        rows = pl.ds(pl.multiple_of(i * CH, CH), CH)
        kt_ref[rows, :] = jnp.transpose(k_ref[rows, :])
        return carry

    lax.fori_loop(0, 27, flip, 0)

    xt_near = remote(xt, xtr.at[0], tsem.at[0], at(s - 1, 0, zh, 0, 0))
    xt_far = remote(xt, xtr.at[1], tsem.at[1], at(s - 1, 0, 0, 0, 0))

    def moments(total):
        total = spread(total / ENTRIES)
        mean = total[0:4]
        return mean, lax.rsqrt(total[4:8] - mean * mean + EPS)

    def prepare():
        gain_load.wait()
        bias_load.wait()
        each(sb_copies, "wait")
        xt[...] = jnp.sum(sb[...], axis=0)
        @pl.when(s > 0)
        def _():
            xt_near.start()

            @pl.when(zh == 1)
            def _():
                xt_far.start()

        mean, rstd = moments(xt[...])
        gain = gain_ref[...]
        rs[0:FR, :] = rstd
        xh = (xhat[...].reshape(FR, PX, CH) - mean[:, None, :]) * rstd[:, None, :]
        h = xh * gain[None] + bias_ref[...][None]
        sg = jax.nn.sigmoid(h)
        xhat[...] = xh.reshape(ROWS, CH)
        dfac[...] = (sg * (1.0 + h * (1.0 - sg))).reshape(ROWS, CH)
        act = h * sg
        a_t[...] = jnp.transpose(jnp.concatenate([act, -act], axis=1).reshape(2 * ROWS, CH)).astype(BF16)

    @pl.when(s < 3)
    def _():
        prepare()

    @pl.when(s < 3)
    def _():
        wait_received(piece_copies(s, x_send, x_recv, x_sems), True)
        remote(xt, xtr.at[0], tsem.at[0], cpeer).wait_recv()

        @pl.when(zh == 0)
        def _():
            remote(xt, xtr.at[1], tsem.at[1], cpeer).wait_recv()

        def normalise(frames, part, row0):
            mean_up, rstd_up = moments(xtr[part])
            n = len(frames)
            mom[frames[0] : frames[0] + n, :] = rstd_up[0:n]
            m, r = mean_up[0:n][:, None, :], rstd_up[0:n][:, None, :]
            px = slice(frames[0] * PX, (frames[0] + n) * PX)
            up = xgc[frames[0] : frames[0] + n].astype(F32).reshape(n, PX, CH)
            xc[px, :] = ((up - m) * r).reshape(n * PX, CH)
            for i in range(4):
                side = xgh[i, row0 : row0 + 8 * n, :].astype(F32).reshape(n, 8, CH)
                xs[i, row0 : row0 + 8 * n, :] = ((side - m) * r).reshape(8 * n, CH)
                xn[part, i, 0:n, :] = (xgn[i, part].astype(F32)[0:n] - mean_up[0:n]) * rstd_up[0:n]

        normalise(range(4), 0, 0)

        @pl.when(zh == 0)
        def _():
            normalise(range(4, 6), 1, 32)

    arriving = piece_copies(s, w_send, w_recv, w_sems)

    edge = (x > 0, x < 3, col > 0, col < 7)

    def columns(frames, center, sides, corners, shift):
        top = jnp.where(edge[0], sides[1], 0.0)
        bottom = jnp.where(edge[1], sides[0], 0.0)
        left = jnp.where(edge[2], sides[3], 0.0)
        right = jnp.where(edge[3], sides[2], 0.0)
        top_left = jnp.where(edge[0] & edge[2], corners[3], 0.0)
        top_right = jnp.where(edge[0] & edge[3], corners[2], 0.0)
        bottom_left = jnp.where(edge[1] & edge[2], corners[1], 0.0)
        bottom_right = jnp.where(edge[1] & edge[3], corners[0], 0.0)
        center = center.reshape(len(frames), 8, 8, CH)
        for i, f in enumerate(frames):
            base = f * 10
            cell = slice(i * 8, i * 8 + 8)
            gp[base + 1 : base + 9, 8:16, :] = center[i]
            gp[base, 8:16, :] = top[cell]
            gp[base + 9, 8:16, :] = bottom[cell]
            for r in range(8):
                gp[base + 1 + r, 7:8, :] = left[i * 8 + r : i * 8 + r + 1]
                gp[base + 1 + r, 16:17, :] = right[i * 8 + r : i * 8 + r + 1]
            gp[base, 7:8, :] = top_left[i : i + 1]
            gp[base, 16:17, :] = top_right[i : i + 1]
            gp[base + 9, 7:8, :] = bottom_left[i : i + 1]
            gp[base + 9, 16:17, :] = bottom_right[i : i + 1]
            for ox in range(3):
                band = gp[base : base + 10, 7 + ox : 15 + ox, :]
                for oy in range(3):
                    tap = (2 - oy) * 3 + (2 - ox)
                    cols[f * 2 * PX + shift : f * 2 * PX + shift + PX, tap * CH : tap * CH + CH] = (
                        band[oy : oy + 8].reshape(PX, CH).astype(BF16)
                    )

    def fill(frames, part, row0):
        n = len(frames)
        columns(
            frames, gc[frames[0] : frames[0] + n].astype(F32),
            [gh[i, row0 : row0 + 8 * n, :].astype(F32) for i in range(4)],
            [gn[i, part].astype(F32)[0:n] for i in range(4)], 0,
        )

    def fill_correction(frames, part, row0, sums):
        n = len(frames)
        both = spread(sums / ENTRIES)
        r_up = mom[frames[0] : frames[0] + n, :]
        c1, c2 = r_up * both[0:n], r_up * both[4 : 4 + n]

        def term(hat, rows):
            value = c1[:, None, :] + hat.reshape(n, rows, CH) * c2[:, None, :]
            return value.reshape(n * rows, CH)

        px = slice(frames[0] * PX, (frames[0] + n) * PX)
        center = term(xc[px, :], PX)
        if part == 0:
            gcen[...] = gc[0:FR].astype(F32).reshape(ROWS, CH) - center
        columns(
            frames, center, [term(xs[i, row0 : row0 + 8 * n, :], 8) for i in range(4)],
            [c1 + xn[part, i, 0:n, :] * c2 for i in range(4)], PX,
        )

    def convolve(shift):
        value = jnp.zeros((ROWS, CH), F32)
        for kt in range(3):
            starts = [(2 - kt + f) * 2 * PX + shift for f in range(FR)]
            value = value + jnp.dot(
                jnp.concatenate([cols[r : r + PX, :] for r in starts], axis=0),
                kt_ref[kt * 9 * CH : (kt + 1) * 9 * CH, :],
                preferred_element_type=F32,
            )
        return value

    def gather():
        near, middle, far = arriving

        @pl.when(s == 3)
        def _():
            direct_done()

        @pl.when(s < 3)
        def _():
            each(near, "wait_recv")
            middle.wait_recv()

        fill(range(4), 0, 0)

        @pl.when(zh == 0)
        def _():
            @pl.when(s < 3)
            def _():
                each(far, "wait_recv")

            fill(range(4, 6), 1, 32)

        @pl.when(zh == 1)
        def _():
            cols[2 * ROWS :, :] = jnp.zeros((4 * PX, 9 * CH), BF16)

        da[...] = convolve(0)

    @pl.when(s == 3)
    def _():
        gather()
        prepare()

    @pl.when(s < 3)
    def _():
        gather()

    gain = gain_ref[...]
    rstd = rs[0:FR, :]

    def one_tap(tap):
        rows = pl.ds(pl.multiple_of(tap * CH, CH), CH)
        lanes = pl.multiple_of((tap % 9) * CH, CH)
        frames = pl.multiple_of((2 - tap // 9) * 2 * PX, 2 * PX)
        part = jnp.dot(
            a_t[...], cols[pl.ds(frames, 2 * ROWS), pl.ds(lanes, CH)], preferred_element_type=F32
        )
        dko[rows, :] = jnp.where(core == 0, part[:, :128], part[:, 128:])
        dks[rows, :] = jnp.where(core == 0, part[:, 128:], part[:, :128]).astype(BF16)

    def own_rows(step, offset, count):
        q = (x + 1 + step) % 4
        return pl.ds(pl.multiple_of(q * QUARTER + offset, 8), count)

    def core_copy(step):
        q = (x + 1 + step) % 4
        span = pl.ds(pl.multiple_of(q * QUARTER, 16), QUARTER)
        return remote(dks.at[span], dkr.at[span], csem.at[step], cpeer)

    def quarter(step):
        q = (x + 1 + step) % 4
        if step == 0:
            @pl.when(x < 3)
            def _():
                one_tap(7 * x + 6)

        for i in range(6):
            one_tap(7 * q + i)
        if step < 3:
            one_tap(7 * q + 6 - q // 3)
        core_copy(step).start()

    def x_first(step):
        return remote(b0.at[step], rx.at[step], xsem.at[step], at(s, step + 1, zh, 0, 0))

    def y_first(step, k):
        return remote(b1.at[step, (y + k) % 4], ry.at[k - 1, step], ysem.at[step, k - 1], at(s, 0, zh, k, 0))

    pad8 = jnp.zeros((8, 128), F32)

    def join(step):
        core_copy(step).wait()
        for half in range(4):
            rows = own_rows(step, half * 432, 432)
            both_cores = dko[rows, :] + dkr[rows, :].astype(F32)
            dko[rows, :] = both_cores
            if half >= 2:
                for i in range(2):
                    piece = jnp.concatenate([both_cores[i * 216 : i * 216 + 216], pad8], axis=0)
                    b1[step, (half - 2) * 2 + i] = piece.astype(BF16)
            elif step < 3:
                b0[step, half * 432 : half * 432 + 432, :] = both_cores.astype(BF16)
        if step < 3:
            x_first(step).start()
        for k in range(1, 4):
            y_first(step, k).start()

    def then_x(step):
        return remote(p1.at[step], r2x.at[step], xsem2.at[step], at(s, step + 1, zh, 0, 0))

    def then_y(k):
        return remote(p0.at[(y + k) % 4], r2y.at[k - 1], ysem2.at[k - 1], at(s, 0, zh, k, 0))

    def sum_y(step):
        for k in range(1, 4):
            y_first(step, k).wait()
        acc = dko[own_rows(step, 864 + y * 216, 216), :]
        for k in range(3):
            acc = acc + ry[k, step].astype(F32)[0:216]
        if step < 3:
            p1[step] = jnp.concatenate([acc, pad8], axis=0).astype(BF16)
            then_x(step).start()
        else:
            t1[...] = acc

    def sum_x():
        for step in range(3):
            x_first(step).wait()
        for half in range(2):
            acc = dko[own_rows(3, half * 432, 432), :]
            for k in range(3):
                acc = acc + rx[k, half * 432 : half * 432 + 432, :].astype(F32)
            for i in range(2):
                piece = acc[i * 216 : i * 216 + 216]
                t0[half * 2 + i] = piece
                p0[half * 2 + i] = jnp.concatenate([piece, pad8], axis=0).astype(BF16)
        for k in range(1, 4):
            then_y(k).start()

    @pl.when(s == 3)
    def _():
        gcen[...] = gc[0:FR].astype(F32).reshape(ROWS, CH)
        for f in range(6):
            cols[f * 2 * PX + PX : f * 2 * PX + 2 * PX, :] = jnp.zeros((PX, 9 * CH), BF16)

    @pl.when(s < 3)
    def _():
        remote(zg.at[pl.ds(0, 8)], unear, tsem.at[3], cpeer).wait_recv()
        fill_correction(range(4), 0, 0, unear[...])

        @pl.when(zh == 0)
        def _():
            remote(zg.at[pl.ds(0, 8)], ufar, tsem.at[2], cpeer).wait_recv()
            fill_correction(range(4, 6), 1, 32, ufar[...])


    @pl.when(s == 0)
    def _():
        quarter(0)
        quarter(1)
        join(0)
        quarter(2)
        join(1)
        quarter(3)
        join(2)
        join(3)

    @pl.when(s < 3)
    def _():
        da[...] = da[...] - convolve(PX)

    dh3 = (da[...] * dfac[...]).reshape(FR, PX, CH)
    dh_sum = jnp.sum(dh3, axis=1)
    dhx_sum = jnp.sum(dh3 * xhat[...].reshape(FR, PX, CH), axis=1)
    gain_part = jnp.sum(dhx_sum, axis=0, keepdims=True)
    bias_part = jnp.sum(dh_sum, axis=0, keepdims=True)
    ua[core] = jnp.concatenate(
        [
            grouped(dh_sum * gain, dhx_sum * gain),
            gain_part[:, :128], gain_part[:, 128:], bias_part[:, :128], bias_part[:, 128:],
            jnp.zeros((4, 128), F32),
        ],
        axis=0,
    )
    ua_copy = core_sum_copy(ua, ucs)
    ua_copy.start()

    w = gcen[...] + (rstd[:, None, :] * (dh3 * gain[None])).reshape(ROWS, CH)
    dfac[...] = w

    w_copies = piece_copies(s - 1, w_send, w_recv, w_sems)

    @pl.when(s > 0)
    def _():
        pack(w, w_send, w_copies)

    ua_copy.wait()
    ub[chip] = ua[0] + ua[1]
    ub_copies = chip_copies(ub, ups)
    each(ub_copies, "start")

    @pl.when((s > 0) & (zh == 1))
    def _():
        each(w_copies[2], "start")

    @pl.when(s > 0)
    def _():
        quarter(0)
        quarter(1)

    def axis_sums():
        sum_y(0)
        sum_y(1)
        sum_y(2)
        sum_x()
        sum_y(3)

    @pl.when(s == 0)
    def _():
        axis_sums()

    each(ub_copies, "wait")
    total = jnp.sum(ub[...], axis=0)
    zg[...] = total
    near_sum = remote(zg.at[pl.ds(0, 8)], unear, tsem.at[3], at(s - 1, 0, zh, 0, 0))
    far_sum = remote(zg.at[pl.ds(0, 8)], ufar, tsem.at[2], at(s - 1, 0, 0, 0, 0))

    @pl.when(s > 0)
    def _():
        near_sum.start()

        @pl.when(zh == 1)
        def _():
            far_sum.start()

    zg_copy = remote(zg, zgr, zsem.at[3], zpeer)
    zg_copy.start()
    both = spread(total[0:8] / ENTRIES)
    c1, c2 = rstd * both[0:4], rstd * both[4:8]
    xh = xhat[...].reshape(FR, PX, CH)
    final = dfac[...].reshape(FR, PX, CH) - c1[:, None, :] - xh * c2[:, None, :]
    final = final.astype(BF16).reshape(FR, 2, 32, CH)
    osend[...] = jnp.where(zh == 0, final[:, 1], final[:, 0])
    o_copy = remote(osend, orecv, zsem.at[2], zpeer)
    o_copy.start()
    out_ref[ours] = jnp.where(zh == 0, final[:, 0], final[:, 1])

    @pl.when(s > 0)
    def _():
        join(0)
        quarter(2)
        join(1)
        quarter(3)
        join(2)
        join(3)

    @pl.when(s > 0)
    def _():
        axis_sums()

    pad4 = jnp.zeros((4, 128), F32)

    def to_owner(plane_id, dc):
        return pltpu.make_async_remote_copy(
            src_ref=p3.at[plane_id, (core + dc) % 2], dst_ref=r3.at[core, zh],
            send_sem=psem.at[plane_id, 0, dc], recv_sem=psem.at[zh, 1, dc],
            device_id=at(s, 0, plane_id, 0, dc), device_id_type=MESH,
        )

    def finish(plane_id):
        if plane_id:
            acc = t1[...]
            for step in range(3):
                then_x(step).wait()
                acc = acc + r2x[step].astype(F32)[0:216]
        else:
            acc = t0[y]
            for k in range(1, 4):
                then_y(k).wait()
                acc = acc + r2y[k - 1].astype(F32)[0:216]
        p3[plane_id, 0] = jnp.concatenate([acc[0:108], pad4], axis=0).astype(BF16)
        p3[plane_id, 1] = jnp.concatenate([acc[108:216], pad4], axis=0).astype(BF16)
        to_owner(plane_id, 1).start()

        @pl.when(zh != plane_id)
        def _():
            to_owner(plane_id, 0).start()

        @pl.when(zh == plane_id)
        def _():
            r3[core, zh] = p3[plane_id, core]

    finish(1)
    finish(0)

    zg_copy.wait()
    sums = (zg[...] + zgr[...]) * SCALE
    gout_ref[:, 0:128] = sums[8:9]
    gout_ref[:, 128:256] = sums[9:10]
    bout_ref[:, 0:128] = sums[10:11]
    bout_ref[:, 128:256] = sums[11:12]
    o_copy.wait()
    out_ref[theirs] = orecv[...]

    @pl.when(s > 0)
    def _():
        wait_sent(piece_copies(s - 1, x_send, x_recv, x_sems), True)
        wait_sent(w_copies, True)
        xt_near.wait_send()
        near_sum.wait_send()

        @pl.when(zh == 1)
        def _():
            xt_far.wait_send()
            far_sum.wait_send()

    for source in range(2):
        for dc in range(2):
            arrival = pltpu.make_async_remote_copy(
                src_ref=p3.at[0, 0], dst_ref=r3.at[0, 0], send_sem=psem.at[0, 0, dc],
                recv_sem=psem.at[source, 1, dc], device_id=cpeer, device_id_type=MESH,
            )
            if dc:
                arrival.wait_recv()
            else:

                @pl.when(zh != source)
                def _():
                    arrival.wait_recv()

    for half in range(2):
        value = r3[half, 0].astype(F32) + r3[half, 1].astype(F32)
        kout_ref[:, 0, half * 128 : half * 128 + 128] = value[0:108] * SCALE

    for plane_id in range(2):
        to_owner(plane_id, 1).wait_send()

        @pl.when(zh != plane_id)
        def _():
            to_owner(plane_id, 0).wait_send()


def write_out(*refs):
    for source, target in zip(refs[:4], refs[4:]):
        target[...] = source[...]


def on_device(saved_inputs, cotangent, kernels, gains, biases):
    inputs = saved_inputs.reshape(8, 32, CH)
    seeds = cotangent.reshape(8, 32, CH)
    vmem = pl.BlockSpec(memory_space=pltpu.VMEM)
    hbm = pl.BlockSpec(memory_space=pltpu.HBM)
    v = pltpu.VMEM
    dma = pltpu.SemaphoreType.DMA
    made = pl.pallas_call(
        kernel,
        out_shape=(
            jax.ShapeDtypeStruct((8, 32, CH), BF16),
            jax.ShapeDtypeStruct((108, 1, CH), F32),
            jax.ShapeDtypeStruct((1, CH), F32),
            jax.ShapeDtypeStruct((1, CH), F32),
        ),
        in_specs=[hbm] * 5,
        out_specs=[vmem] * 4,
        scratch_shapes=[
            v((8, 32, CH), BF16), v((8, 32, CH), BF16), v((27 * CH, CH), BF16), v((1, CH), F32), v((1, CH), F32),
            v((FR, 32, CH), BF16), v((8, 128), F32), v((8, 128), F32), v((FR, 32, CH), BF16), v((FR, 32, CH), BF16),
            v((ROWS, CH), F32), v((32, CH), F32),
            v((2, 32, CH), BF16), v((64, CH), BF16), v((2, 2, 16, CH), BF16), v((2, 2, 32, CH), BF16),
            v((FR, 2, 32, CH), BF16), v((4, 32, CH), BF16), v((4, 16, CH), BF16),
            v((6, 2, 32, CH), BF16), v((4, 48, CH), BF16), v((4, 2, 16, CH), BF16),
            v((FR, 2, 32, CH), BF16), v((4, 32, CH), BF16), v((4, 16, CH), BF16),
            v((6, 2, 32, CH), BF16), v((4, 48, CH), BF16), v((4, 2, 16, CH), BF16),
            v((ALL, CH), F32), v((4, 48, CH), F32), v((2, 4, 16, CH), F32), v((60, 24, CH), F32),
            v((ROWS, CH), F32), v((2 * ALL, 9 * CH), BF16), v((27 * CH, CH), BF16),
            v((CH, 2 * ROWS), BF16), v((ROWS, CH), F32), v((ROWS, CH), F32), v((ROWS, CH), F32), v((8, CH), F32),
            v((2, 8, 128), F32), v((16, 8, 128), F32), v((2, 16, 128), F32), v((16, 16, 128), F32),
            v((8, 128), F32), v((8, 128), F32), v((8, 128), F32), v((2, 8, 128), F32), v((8, CH), F32),
            v((16, 128), F32), v((16, 128), F32),
            v((27 * CH, 128), F32), v((27 * CH, 128), BF16), v((27 * CH, 128), BF16),
            v((3, 864, 128), BF16), v((4, 4, 224, 128), BF16), v((3, 864, 128), BF16), v((3, 4, 224, 128), BF16),
            v((4, 224, 128), BF16), v((3, 224, 128), BF16), v((4, 216, 128), F32), v((216, 128), F32),
            v((3, 224, 128), BF16), v((3, 224, 128), BF16), v((2, 2, 112, 128), BF16), v((2, 2, 112, 128), BF16),
            dma((6,)), dma((4, 2)), dma((2, 2, 6)), dma((2, 2)), dma((2, 4, 2)), dma((2, 4, 2)),
            dma((2, 2)), dma((2, 4, 2)), dma((2, 4, 2)),
            dma((2,)), dma((16, 2)), dma((2,)), dma((16, 2)), dma((4, 2)), dma((4, 2)),
            dma((3, 2)), dma((4, 3, 2)), dma((3, 2)), dma((3, 2)), dma((2, 2, 2)),
        ],
        compiler_params=pltpu.CompilerParams(
            collective_id=0, has_side_effects=True, vmem_limit_bytes=VMEM_LIMIT
        ),
        name="blocks",
    )(inputs, seeds, kernels[0], gains, biases)
    out, kout, gout, bout = pl.pallas_call(
        write_out,
        out_shape=tuple(jax.ShapeDtypeStruct(m.shape, m.dtype) for m in made),
        in_specs=[vmem] * 4,
        out_specs=[vmem] * 4,
        name="write_out",
    )(*made)
    return out.reshape(1, 8, 1, 4, 8, CH), kout.reshape(1, 108, CH), gout, bout


def solution(mesh):
    in_specs = (
        P("section", None, "tile", None, None, None),
        P(None, "tile", None, None, None),
        P("section", None, None),
        P("section", None),
        P("section", None),
    )
    out_specs = (
        P("section", None, "tile", None, None, None),
        P("section", "tile", None),
        P("section", None),
        P("section", None),
    )
    return jax.shard_map(
        on_device, mesh=mesh, in_specs=in_specs, out_specs=out_specs, check_vma=False
    )
```

```python
import functools
import math

import jax
import jax.numpy as jnp
from jax import lax
from jax.experimental import pallas as pl
from jax.experimental.pallas import tpu as pltpu
from jax.sharding import PartitionSpec as P

CH = 256
GROUPS = 32
PER_GROUP = CH // GROUPS
FR = 4
PX = 64
ROWS = FR * PX
ALL = ROWS + 2 * PX
ENTRIES = float(64 * 32 * PER_GROUP)
SCALE = 1.0 / math.sqrt(8 * 64 * 32)
EPS = 1e-05
VMEM_LIMIT = 62 * 2**20
MESH = pl.DeviceIdType.MESH
SIDES = ((-1, 0), (1, 0), (0, -1), (0, 1))
CORNERS = ((-1, -1), (-1, 1), (1, -1), (1, 1))
AROUND = [(dx, dy, dc) for dx in (-1, 0, 1) for dy, dc in ((0, 0), (-1, 1), (0, 1), (1, 1))]
CHIPS = sorted(
    ((dx, dy) for dx in range(4) for dy in range(4)),
    key=lambda d: (d != (0, 0), -min(d[0], 4 - d[0]) - min(d[1], 4 - d[1]), d),
)
QUARTER = 1728
F32 = jnp.float32
BF16 = jnp.bfloat16


def kernel(
    x_hbm, cot_hbm, k_hbm, gain_hbm, bias_hbm,
    out_ref, kout_ref, gout_ref, bout_ref,
    x_ref, cot_ref, k_ref, gain_ref, bias_ref,
    xr, xst, xstr, osend, orecv, rf, strip, lrs, rows_s, nooks, lr,
    wc, wh, wn, gc, gh, gn, xwc, xwh, xwn, xgc, xgh, xgn,
    xc, xs, xn, gp, gcen, cols, kt_ref, a_t, xhat, dfac, da, rs,
    sb, ua, ub, unear, ufar, xt, xtr, mom, zg, zgr,
    dko, dks, dkr, b0, b1, rx, ry, p0, p1, t0, t1, r2x, r2y, p3, r3,
    lsem, zsem, dsem, wgs, whs, wns, xgs, xhs, xns, asem, aps, ucs, ups, tsem, csem, xsem, ysem, xsem2, ysem2, psem,
):
    s = lax.axis_index("section")
    t = lax.axis_index("tile")
    x = t // 16
    zh = (t // 8) % 2
    y = (t // 2) % 4
    core = t % 2
    col = t % 8
    chip = x * 4 + y

    def at(sec, dx, z2, dy, dc):
        return (sec, ((x + dx + 4) % 4) * 16 + z2 * 8 + ((y + dy + 4) % 4) * 2 + (core + dc) % 2)

    def beside(sec, dx, z2, dcol):
        return (sec, ((x + dx + 4) % 4) * 16 + z2 * 8 + (col + dcol + 8) % 8)

    zpeer = at(s, 0, 1 - zh, 0, 0)
    cpeer = at(s, 0, zh, 0, 1)

    def remote(src, dst, pair, device):
        return pltpu.make_async_remote_copy(
            src_ref=src, dst_ref=dst, send_sem=pair.at[0], recv_sem=pair.at[1],
            device_id=device, device_id_type=MESH,
        )

    x_load = pltpu.make_async_copy(x_hbm, x_ref, lsem.at[0])
    cot_load = pltpu.make_async_copy(cot_hbm, cot_ref, lsem.at[1])
    k_load = pltpu.make_async_copy(k_hbm, k_ref, lsem.at[2])
    gain_load = pltpu.make_async_copy(gain_hbm, gain_ref, lsem.at[3])
    bias_load = pltpu.make_async_copy(bias_hbm, bias_ref, lsem.at[4])
    x_load.start()
    gain_load.start()
    bias_load.start()

    @pl.when(s == 3)
    def _():
        cot_load.start()

    k_load.start()

    barrier = pltpu.get_barrier_semaphore()

    def greet(device):
        pl.semaphore_signal(barrier, inc=1, device_id=device, device_id_type=MESH)

    plane = [(dx, 0, dy, 0) for dx, dy in CHIPS if (dx, dy) != (0, 0)]
    plane += [(0, 1, 0, 0), (0, 1, 0, 1), (0, 0, 0, 1)]
    for dx, z, dy, dc in plane:
        greet(at(s, dx, (zh + z) % 2, dy, dc))

    @pl.when(s < 3)
    def _():
        for dx, dy, dc in AROUND:
            greet(at(s + 1, dx, zh, dy, dc))

        @pl.when(zh == 0)
        def _():
            for dx, dy, dc in AROUND:
                greet(at(s + 1, dx, 1, dy, dc))

    @pl.when(s == 3)
    def _():
        for dx, dy, dc in AROUND:
            if (dx, dy, dc) != (0, 0, 0):
                greet(at(3, dx, zh, dy, dc))
            greet(at(3, dx, 1 - zh, dy, dc))

    expected = len(plane) + jnp.where(s > 0, (1 + zh) * len(AROUND), 0)
    expected = expected + jnp.where(s == 3, 2 * len(AROUND) - 1, 0)
    pl.semaphore_wait(barrier, expected)

    def each(copies, what):
        for c in copies:
            getattr(c, what)()

    theirs = pl.ds((1 - zh) * FR, FR)
    ours = pl.ds(zh * FR, FR)
    x_copy = remote(x_hbm.at[theirs], xr, zsem.at[0], zpeer)

    def patch(own, other):
        own = own.astype(F32)
        other = other.astype(F32)
        upper = jnp.where(zh == 0, own, other)
        lower = jnp.where(zh == 0, other, own)
        return jnp.concatenate([upper, lower], axis=1).reshape(ROWS, CH)

    def indicator(shape, channel_dim):
        channel = lax.broadcasted_iota(jnp.int32, shape, channel_dim)
        group = lax.broadcasted_iota(jnp.int32, shape, 1 - channel_dim)
        return (channel // PER_GROUP == group).astype(F32)

    def grouped(first, second):
        return jnp.dot(
            jnp.concatenate([first, second], axis=0), indicator((CH, 128), 0),
            precision=lax.Precision.HIGHEST, preferred_element_type=F32,
        )

    def spread(groups):
        return jnp.dot(
            groups, indicator((128, CH), 1), precision=lax.Precision.HIGHEST, preferred_element_type=F32
        )

    def core_sum_copy(buf, pair):
        return remote(buf.at[core], buf.at[core], pair, cpeer)

    def chip_copies(buf, sems):
        return [
            remote(buf.at[chip], buf.at[chip], sems.at[i], at(s, dx, zh, dy, 0))
            for i, (dx, dy) in enumerate(CHIPS) if i
        ]

    x_load.wait()

    def tile_sums(frames):
        value = x_ref[frames].astype(F32)
        return grouped(jnp.sum(value, axis=1), jnp.sum(value * value, axis=1))

    xst[0] = tile_sums(theirs)
    xst[1] = tile_sums(ours)
    mine = zh * 2 + core
    xst_copies = [
        remote(xst.at[0], xstr.at[mine], asem.at[0], zpeer),
        remote(xst.at[0], xstr.at[mine], asem.at[1], at(s, 0, 1 - zh, 0, 1)),
        remote(xst.at[1], xstr.at[mine], asem.at[2], cpeer),
    ]
    each(xst_copies, "start")

    @pl.when(s == 3)
    def _():
        x_copy.start()

    xstr[mine] = xst[1]

    def pack(value, send, copies):
        center, sides, corners = send
        near, middle, _ = copies
        rf[...] = value
        for i, pixel in enumerate((0, 7, 56, 63)):
            rows = [rf[f * PX + pixel : f * PX + pixel + 1, :] for f in range(FR)]
            corners[i] = jnp.concatenate(rows + [jnp.zeros((12, CH), F32)], axis=0).astype(BF16)
        each(near[0:4], "start")
        v4 = value.reshape(FR, 8, 8, CH)
        sides[0] = v4[:, 0].reshape(32, CH).astype(BF16)
        sides[1] = v4[:, 7].reshape(32, CH).astype(BF16)
        each(near[4:6], "start")
        for i, lead in ((2, 0), (3, 7)):
            for f in range(FR):
                rows = [rf[f * PX + r * 8 + lead : f * PX + r * 8 + lead + 1, :] for r in range(8)]
                strip[f * 8 : f * 8 + 8, :] = jnp.concatenate(rows, axis=0)
            sides[i] = strip[...].astype(BF16)
        each(near[6:8], "start")
        center[...] = value.astype(BF16).reshape(FR, 2, 32, CH)
        middle.start()

    def piece_copies(sec, send, recv, sems):
        center, sides, corners = send
        center_r, sides_r, corners_r = recv
        gs, hs, ns = sems
        near, far = [], []
        for i, (dx, dc) in enumerate(CORNERS):
            near.append(remote(corners.at[i], corners_r.at[i, 0], ns.at[0, i], beside(sec, dx, zh, dc)))
            far.append(remote(corners.at[i], corners_r.at[i, 1], ns.at[1, i], beside(sec, dx, 0, dc)))
        for i, (dx, dc) in enumerate(SIDES):
            near.append(remote(sides.at[i], sides_r.at[i, pl.ds(0, 32)], hs.at[0, i], beside(sec, dx, zh, dc)))
            far.append(
                remote(sides.at[i, pl.ds(0, 16)], sides_r.at[i, pl.ds(32, 16)], hs.at[1, i], beside(sec, dx, 0, dc))
            )
        middle = remote(center, center_r.at[pl.ds(0, FR)], gs.at[0], beside(sec, 0, zh, 0))
        far.append(
            remote(center.at[pl.ds(0, 2)], center_r.at[pl.ds(FR, 2)], gs.at[1], beside(sec, 0, 0, 0))
        )
        return near, middle, far

    def wait_sent(copies, with_middle):
        near, middle, far = copies
        each(near + ([middle] if with_middle else []), "wait_send")

        @pl.when(zh == 1)
        def _():
            each(far, "wait_send")

    def wait_received(copies, with_middle):
        near, middle, far = copies
        each(near + ([middle] if with_middle else []), "wait_recv")

        @pl.when(zh == 0)
        def _():
            each(far, "wait_recv")

    w_send, w_recv, w_sems = (wc, wh, wn), (gc, gh, gn), (wgs, whs, wns)
    x_send, x_recv, x_sems = (xwc, xwh, xwn), (xgc, xgh, xgn), (xgs, xhs, xns)

    frames_of = (pl.ds(0, 6), pl.ds(4, 4))
    count_of = (6, 4)

    def direct_copies(plane_id):
        n = count_of[plane_id]
        lead = 4 * plane_id
        lr_rows = pl.ds(16 * plane_id, 32 - 16 * plane_id)
        row_rows = pl.ds(8 * lead, 8 * n)
        down = 2 * zh - 1
        pair = dsem.at[plane_id]

        def send(src, dst, slot, device):
            return pltpu.make_async_remote_copy(
                src_ref=src, dst_ref=dst, send_sem=pair.at[0, slot], recv_sem=dsem.at[zh, 1, slot],
                device_id=device, device_id_type=MESH,
            )

        nook_rows = pl.ds(plane_id, 2 - plane_id)
        landing = pl.ds(0, 2 - plane_id)
        copies = [
            send(nooks.at[0, nook_rows], gn.at[2 * zh, landing], 3, beside(3, down, plane_id, -1)),
            send(nooks.at[1, nook_rows], gn.at[2 * zh + 1, landing], 4, beside(3, down, plane_id, 1)),
            send(rows_s.at[row_rows], gh.at[zh, pl.ds(0, 8 * n)], 2, beside(3, down, plane_id, 0)),
            send(lrs.at[0, lr_rows], lr.at[0, zh, pl.ds(0, 32 - 16 * plane_id)], 0, beside(3, 0, plane_id, -1)),
            send(lrs.at[1, lr_rows], lr.at[1, zh, pl.ds(0, 32 - 16 * plane_id)], 1, beside(3, 0, plane_id, 1)),
        ]
        center = send(
            cot_hbm.at[frames_of[plane_id]], gc.at[pl.ds(0, n), zh], 5, beside(3, 0, plane_id, 0)
        )
        return copies, center

    def own_half(plane_id):
        return pltpu.make_async_copy(
            cot_hbm.at[frames_of[plane_id]], gc.at[pl.ds(0, count_of[plane_id]), plane_id], lsem.at[5]
        )

    def direct_arrivals(plane_id):
        n = count_of[plane_id]
        arrivals = []
        for source in range(2):
            sizes = (
                lr.at[0, 0, pl.ds(0, 32 - 16 * plane_id)], lr.at[0, 0, pl.ds(0, 32 - 16 * plane_id)],
                gh.at[0, pl.ds(0, 8 * n)],
                gn.at[0, pl.ds(0, 2 - plane_id)], gn.at[0, pl.ds(0, 2 - plane_id)],
            ) + ((gc.at[pl.ds(0, n), 0],) if source != plane_id else ())
            for slot, ref in enumerate(sizes):
                arrivals.append(
                    pltpu.make_async_remote_copy(
                        src_ref=ref, dst_ref=ref, send_sem=dsem.at[0, 0, slot],
                        recv_sem=dsem.at[source, 1, slot], device_id=cpeer, device_id_type=MESH,
                    )
                )
        return arrivals

    @pl.when(s == 3)
    def _():
        for plane_id in range(2):

            @pl.when(zh == plane_id)
            def _():
                direct_copies(1 - plane_id)[1].start()
                own_half(plane_id).start()

        cot_load.wait()
        rf[...] = cot_ref[...].astype(F32).reshape(ROWS, CH)
        for i, lead in ((0, 0), (1, 7)):
            for f in range(8):
                picks = [rf[f * 32 + r * 8 + lead : f * 32 + r * 8 + lead + 1, :] for r in range(4)]
                strip[f * 4 : f * 4 + 4, :] = jnp.concatenate(picks, axis=0)
            lrs[i] = strip[...].astype(BF16)
        outer_rows = []
        for f in range(8):
            outer_rows.append(
                jnp.where(zh == 0, rf[f * 32 : f * 32 + 8, :], rf[f * 32 + 24 : f * 32 + 32, :])
            )
        rows_s[...] = jnp.concatenate(outer_rows, axis=0).astype(BF16)
        for i, end in ((0, 0), (1, 7)):
            for part in range(2):
                picks = [outer_rows[part * 4 + f][end : end + 1] for f in range(4)]
                nooks[i, part] = jnp.concatenate(picks + [jnp.zeros((12, CH), F32)], axis=0).astype(BF16)
        for plane_id in (1, 0):
            each(direct_copies(plane_id)[0], "start")

    def direct_done():
        for plane_id in range(2):

            @pl.when(zh == plane_id)
            def _():
                each(direct_arrivals(plane_id), "wait_recv")
                own_half(plane_id).wait()
                n = count_of[plane_id]
                for i in range(2):
                    halves = [lr[i, z2].astype(F32)[0 : 4 * n].reshape(n, 4, CH) for z2 in range(2)]
                    gh[2 + i, 0 : 8 * n, :] = (
                        jnp.concatenate(halves, axis=1).reshape(8 * n, CH).astype(BF16)
                    )

            each(direct_copies(plane_id)[0], "wait_send")

            @pl.when(zh != plane_id)
            def _():
                direct_copies(plane_id)[1].wait_send()

    each(xst_copies, "wait")
    sb[chip] = jnp.sum(xstr[...], axis=0)
    sb_copies = chip_copies(sb, aps)
    each(sb_copies, "start")

    @pl.when(s < 3)
    def _():
        x_copy.start()

    x_copy.wait()
    xv = patch(x_ref[ours], xr[...])
    xhat[...] = xv

    @pl.when(s > 0)
    def _():
        copies = piece_copies(s - 1, x_send, x_recv, x_sems)
        pack(xv, x_send, copies)

        @pl.when(zh == 1)
        def _():
            each(copies[2], "start")

    k_load.wait()

    def flip(i, carry):
        rows = pl.ds(pl.multiple_of(i * CH, CH), CH)
        kt_ref[rows, :] = jnp.transpose(k_ref[rows, :])
        return carry

    lax.fori_loop(0, 27, flip, 0)

    xt_near = remote(xt, xtr.at[0], tsem.at[0], at(s - 1, 0, zh, 0, 0))
    xt_far = remote(xt, xtr.at[1], tsem.at[1], at(s - 1, 0, 0, 0, 0))

    def moments(total):
        total = spread(total / ENTRIES)
        mean = total[0:4]
        return mean, lax.rsqrt(total[4:8] - mean * mean + EPS)

    def prepare():
        gain_load.wait()
        bias_load.wait()
        each(sb_copies, "wait")
        xt[...] = jnp.sum(sb[...], axis=0)
        @pl.when(s > 0)
        def _():
            xt_near.start()

            @pl.when(zh == 1)
            def _():
                xt_far.start()

        mean, rstd = moments(xt[...])
        gain = gain_ref[...]
        rs[0:FR, :] = rstd
        xh = (xhat[...].reshape(FR, PX, CH) - mean[:, None, :]) * rstd[:, None, :]
        h = xh * gain[None] + bias_ref[...][None]
        sg = jax.nn.sigmoid(h)
        xhat[...] = xh.reshape(ROWS, CH)
        dfac[...] = (sg * (1.0 + h * (1.0 - sg))).reshape(ROWS, CH)
        act = h * sg
        a_t[...] = jnp.transpose(jnp.concatenate([act, -act], axis=1).reshape(2 * ROWS, CH)).astype(BF16)

    @pl.when(s < 3)
    def _():
        prepare()

    @pl.when(s < 3)
    def _():
        wait_received(piece_copies(s, x_send, x_recv, x_sems), True)
        remote(xt, xtr.at[0], tsem.at[0], cpeer).wait_recv()

        @pl.when(zh == 0)
        def _():
            remote(xt, xtr.at[1], tsem.at[1], cpeer).wait_recv()

        def normalise(frames, part, row0):
            mean_up, rstd_up = moments(xtr[part])
            n = len(frames)
            mom[frames[0] : frames[0] + n, :] = rstd_up[0:n]
            m, r = mean_up[0:n][:, None, :], rstd_up[0:n][:, None, :]
            px = slice(frames[0] * PX, (frames[0] + n) * PX)
            up = xgc[frames[0] : frames[0] + n].astype(F32).reshape(n, PX, CH)
            xc[px, :] = ((up - m) * r).reshape(n * PX, CH)
            for i in range(4):
                side = xgh[i, row0 : row0 + 8 * n, :].astype(F32).reshape(n, 8, CH)
                xs[i, row0 : row0 + 8 * n, :] = ((side - m) * r).reshape(8 * n, CH)
                xn[part, i, 0:n, :] = (xgn[i, part].astype(F32)[0:n] - mean_up[0:n]) * rstd_up[0:n]

        normalise(range(4), 0, 0)

        @pl.when(zh == 0)
        def _():
            normalise(range(4, 6), 1, 32)

    arriving = piece_copies(s, w_send, w_recv, w_sems)

    edge = (x > 0, x < 3, col > 0, col < 7)

    def columns(frames, center, sides, corners, shift):
        top = jnp.where(edge[0], sides[1], 0.0)
        bottom = jnp.where(edge[1], sides[0], 0.0)
        left = jnp.where(edge[2], sides[3], 0.0)
        right = jnp.where(edge[3], sides[2], 0.0)
        top_left = jnp.where(edge[0] & edge[2], corners[3], 0.0)
        top_right = jnp.where(edge[0] & edge[3], corners[2], 0.0)
        bottom_left = jnp.where(edge[1] & edge[2], corners[1], 0.0)
        bottom_right = jnp.where(edge[1] & edge[3], corners[0], 0.0)
        center = center.reshape(len(frames), 8, 8, CH)
        for i, f in enumerate(frames):
            base = f * 10
            cell = slice(i * 8, i * 8 + 8)
            gp[base + 1 : base + 9, 8:16, :] = center[i]
            gp[base, 8:16, :] = top[cell]
            gp[base + 9, 8:16, :] = bottom[cell]
            for r in range(8):
                gp[base + 1 + r, 7:8, :] = left[i * 8 + r : i * 8 + r + 1]
                gp[base + 1 + r, 16:17, :] = right[i * 8 + r : i * 8 + r + 1]
            gp[base, 7:8, :] = top_left[i : i + 1]
            gp[base, 16:17, :] = top_right[i : i + 1]
            gp[base + 9, 7:8, :] = bottom_left[i : i + 1]
            gp[base + 9, 16:17, :] = bottom_right[i : i + 1]
            for ox in range(3):
                band = gp[base : base + 10, 7 + ox : 15 + ox, :]
                for oy in range(3):
                    tap = (2 - oy) * 3 + (2 - ox)
                    cols[f * 2 * PX + shift : f * 2 * PX + shift + PX, tap * CH : tap * CH + CH] = (
                        band[oy : oy + 8].reshape(PX, CH).astype(BF16)
                    )

    def fill(frames, part, row0):
        n = len(frames)
        columns(
            frames, gc[frames[0] : frames[0] + n].astype(F32),
            [gh[i, row0 : row0 + 8 * n, :].astype(F32) for i in range(4)],
            [gn[i, part].astype(F32)[0:n] for i in range(4)], 0,
        )

    def fill_correction(frames, part, row0, sums):
        n = len(frames)
        both = spread(sums / ENTRIES)
        r_up = mom[frames[0] : frames[0] + n, :]
        c1, c2 = r_up * both[0:n], r_up * both[4 : 4 + n]

        def term(hat, rows):
            value = c1[:, None, :] + hat.reshape(n, rows, CH) * c2[:, None, :]
            return value.reshape(n * rows, CH)

        px = slice(frames[0] * PX, (frames[0] + n) * PX)
        center = term(xc[px, :], PX)
        if part == 0:
            gcen[...] = gc[0:FR].astype(F32).reshape(ROWS, CH) - center
        columns(
            frames, center, [term(xs[i, row0 : row0 + 8 * n, :], 8) for i in range(4)],
            [c1 + xn[part, i, 0:n, :] * c2 for i in range(4)], PX,
        )

    def convolve(shift):
        value = jnp.zeros((ROWS, CH), F32)
        for kt in range(3):
            starts = [(2 - kt + f) * 2 * PX + shift for f in range(FR)]
            value = value + jnp.dot(
                jnp.concatenate([cols[r : r + PX, :] for r in starts], axis=0),
                kt_ref[kt * 9 * CH : (kt + 1) * 9 * CH, :],
                preferred_element_type=F32,
            )
        return value

    def gather():
        near, middle, far = arriving

        @pl.when(s == 3)
        def _():
            direct_done()

        @pl.when(s < 3)
        def _():
            each(near, "wait_recv")
            middle.wait_recv()

        fill(range(4), 0, 0)

        @pl.when(zh == 0)
        def _():
            @pl.when(s < 3)
            def _():
                each(far, "wait_recv")

            fill(range(4, 6), 1, 32)

        @pl.when(zh == 1)
        def _():
            cols[2 * ROWS :, :] = jnp.zeros((4 * PX, 9 * CH), BF16)

        da[...] = convolve(0)

    @pl.when(s == 3)
    def _():
        gather()
        prepare()

    @pl.when(s < 3)
    def _():
        gather()

    gain = gain_ref[...]
    rstd = rs[0:FR, :]

    def one_tap(tap):
        rows = pl.ds(pl.multiple_of(tap * CH, CH), CH)
        lanes = pl.multiple_of((tap % 9) * CH, CH)
        frames = pl.multiple_of((2 - tap // 9) * 2 * PX, 2 * PX)
        part = jnp.dot(
            a_t[...], cols[pl.ds(frames, 2 * ROWS), pl.ds(lanes, CH)], preferred_element_type=F32
        )
        dko[rows, :] = jnp.where(core == 0, part[:, :128], part[:, 128:])
        dks[rows, :] = jnp.where(core == 0, part[:, 128:], part[:, :128]).astype(BF16)

    def own_rows(step, offset, count):
        q = (x + 1 + step) % 4
        return pl.ds(pl.multiple_of(q * QUARTER + offset, 8), count)

    def core_copy(step):
        q = (x + 1 + step) % 4
        span = pl.ds(pl.multiple_of(q * QUARTER, 16), QUARTER)
        return remote(dks.at[span], dkr.at[span], csem.at[step], cpeer)

    def quarter(step):
        q = (x + 1 + step) % 4
        if step == 0:
            @pl.when(x < 3)
            def _():
                one_tap(7 * x + 6)

        for i in range(6):
            one_tap(7 * q + i)
        if step < 3:
            one_tap(7 * q + 6 - q // 3)
        core_copy(step).start()

    def x_first(step):
        return remote(b0.at[step], rx.at[step], xsem.at[step], at(s, step + 1, zh, 0, 0))

    def y_first(step, k):
        return remote(b1.at[step, (y + k) % 4], ry.at[k - 1, step], ysem.at[step, k - 1], at(s, 0, zh, k, 0))

    pad8 = jnp.zeros((8, 128), F32)

    def join(step):
        core_copy(step).wait()
        for half in range(4):
            rows = own_rows(step, half * 432, 432)
            both_cores = dko[rows, :] + dkr[rows, :].astype(F32)
            dko[rows, :] = both_cores
            if half >= 2:
                for i in range(2):
                    piece = jnp.concatenate([both_cores[i * 216 : i * 216 + 216], pad8], axis=0)
                    b1[step, (half - 2) * 2 + i] = piece.astype(BF16)
            elif step < 3:
                b0[step, half * 432 : half * 432 + 432, :] = both_cores.astype(BF16)
        if step < 3:
            x_first(step).start()
        for k in range(1, 4):
            y_first(step, k).start()

    def then_x(step):
        return remote(p1.at[step], r2x.at[step], xsem2.at[step], at(s, step + 1, zh, 0, 0))

    def then_y(k):
        return remote(p0.at[(y + k) % 4], r2y.at[k - 1], ysem2.at[k - 1], at(s, 0, zh, k, 0))

    def sum_y(step):
        for k in range(1, 4):
            y_first(step, k).wait()
        acc = dko[own_rows(step, 864 + y * 216, 216), :]
        for k in range(3):
            acc = acc + ry[k, step].astype(F32)[0:216]
        if step < 3:
            p1[step] = jnp.concatenate([acc, pad8], axis=0).astype(BF16)
            then_x(step).start()
        else:
            t1[...] = acc

    def sum_x():
        for step in range(3):
            x_first(step).wait()
        for half in range(2):
            acc = dko[own_rows(3, half * 432, 432), :]
            for k in range(3):
                acc = acc + rx[k, half * 432 : half * 432 + 432, :].astype(F32)
            for i in range(2):
                piece = acc[i * 216 : i * 216 + 216]
                t0[half * 2 + i] = piece
                p0[half * 2 + i] = jnp.concatenate([piece, pad8], axis=0).astype(BF16)
        for k in range(1, 4):
            then_y(k).start()

    @pl.when(s == 3)
    def _():
        gcen[...] = gc[0:FR].astype(F32).reshape(ROWS, CH)
        for f in range(6):
            cols[f * 2 * PX + PX : f * 2 * PX + 2 * PX, :] = jnp.zeros((PX, 9 * CH), BF16)

    @pl.when(s < 3)
    def _():
        remote(zg.at[pl.ds(0, 8)], unear, tsem.at[3], cpeer).wait_recv()
        fill_correction(range(4), 0, 0, unear[...])

        @pl.when(zh == 0)
        def _():
            remote(zg.at[pl.ds(0, 8)], ufar, tsem.at[2], cpeer).wait_recv()
            fill_correction(range(4, 6), 1, 32, ufar[...])


    @pl.when(s == 0)
    def _():
        quarter(0)
        quarter(1)
        join(0)
        quarter(2)
        join(1)
        quarter(3)
        join(2)
        join(3)

    @pl.when(s < 3)
    def _():
        da[...] = da[...] - convolve(PX)

    dh3 = (da[...] * dfac[...]).reshape(FR, PX, CH)
    dh_sum = jnp.sum(dh3, axis=1)
    dhx_sum = jnp.sum(dh3 * xhat[...].reshape(FR, PX, CH), axis=1)
    gain_part = jnp.sum(dhx_sum, axis=0, keepdims=True)
    bias_part = jnp.sum(dh_sum, axis=0, keepdims=True)
    ua[core] = jnp.concatenate(
        [
            grouped(dh_sum * gain, dhx_sum * gain),
            gain_part[:, :128], gain_part[:, 128:], bias_part[:, :128], bias_part[:, 128:],
            jnp.zeros((4, 128), F32),
        ],
        axis=0,
    )
    ua_copy = core_sum_copy(ua, ucs)
    ua_copy.start()

    w = gcen[...] + (rstd[:, None, :] * (dh3 * gain[None])).reshape(ROWS, CH)
    dfac[...] = w

    w_copies = piece_copies(s - 1, w_send, w_recv, w_sems)

    @pl.when(s > 0)
    def _():
        pack(w, w_send, w_copies)

    ua_copy.wait()
    ub[chip] = ua[0] + ua[1]
    ub_copies = chip_copies(ub, ups)
    each(ub_copies, "start")

    @pl.when((s > 0) & (zh == 1))
    def _():
        each(w_copies[2], "start")

    @pl.when(s > 0)
    def _():
        quarter(0)
        quarter(1)

    def axis_sums():
        sum_y(0)
        sum_y(1)
        sum_y(2)
        sum_x()
        sum_y(3)

    @pl.when(s == 0)
    def _():
        axis_sums()

    each(ub_copies, "wait")
    total = jnp.sum(ub[...], axis=0)
    zg[...] = total
    near_sum = remote(zg.at[pl.ds(0, 8)], unear, tsem.at[3], at(s - 1, 0, zh, 0, 0))
    far_sum = remote(zg.at[pl.ds(0, 8)], ufar, tsem.at[2], at(s - 1, 0, 0, 0, 0))

    @pl.when(s > 0)
    def _():
        near_sum.start()

        @pl.when(zh == 1)
        def _():
            far_sum.start()

    zg_copy = remote(zg, zgr, zsem.at[3], zpeer)
    zg_copy.start()
    both = spread(total[0:8] / ENTRIES)
    c1, c2 = rstd * both[0:4], rstd * both[4:8]
    xh = xhat[...].reshape(FR, PX, CH)
    final = dfac[...].reshape(FR, PX, CH) - c1[:, None, :] - xh * c2[:, None, :]
    final = final.astype(BF16).reshape(FR, 2, 32, CH)
    osend[...] = jnp.where(zh == 0, final[:, 1], final[:, 0])
    o_copy = remote(osend, orecv, zsem.at[2], zpeer)
    o_copy.start()
    out_ref[ours] = jnp.where(zh == 0, final[:, 0], final[:, 1])

    @pl.when(s > 0)
    def _():
        join(0)
        quarter(2)
        join(1)
        quarter(3)
        join(2)
        join(3)

    @pl.when(s > 0)
    def _():
        axis_sums()

    pad4 = jnp.zeros((4, 128), F32)

    def to_owner(plane_id, dc):
        return pltpu.make_async_remote_copy(
            src_ref=p3.at[plane_id, (core + dc) % 2], dst_ref=r3.at[core, zh],
            send_sem=psem.at[plane_id, 0, dc], recv_sem=psem.at[zh, 1, dc],
            device_id=at(s, 0, plane_id, 0, dc), device_id_type=MESH,
        )

    def finish(plane_id):
        if plane_id:
            acc = t1[...]
            for step in range(3):
                then_x(step).wait()
                acc = acc + r2x[step].astype(F32)[0:216]
        else:
            acc = t0[y]
            for k in range(1, 4):
                then_y(k).wait()
                acc = acc + r2y[k - 1].astype(F32)[0:216]
        p3[plane_id, 0] = jnp.concatenate([acc[0:108], pad4], axis=0).astype(BF16)
        p3[plane_id, 1] = jnp.concatenate([acc[108:216], pad4], axis=0).astype(BF16)
        to_owner(plane_id, 1).start()

        @pl.when(zh != plane_id)
        def _():
            to_owner(plane_id, 0).start()

        @pl.when(zh == plane_id)
        def _():
            r3[core, zh] = p3[plane_id, core]

    finish(1)
    finish(0)

    zg_copy.wait()
    sums = (zg[...] + zgr[...]) * SCALE
    gout_ref[:, 0:128] = sums[8:9]
    gout_ref[:, 128:256] = sums[9:10]
    bout_ref[:, 0:128] = sums[10:11]
    bout_ref[:, 128:256] = sums[11:12]
    o_copy.wait()
    out_ref[theirs] = orecv[...]

    @pl.when(s > 0)
    def _():
        wait_sent(piece_copies(s - 1, x_send, x_recv, x_sems), True)
        wait_sent(w_copies, True)
        xt_near.wait_send()
        near_sum.wait_send()

        @pl.when(zh == 1)
        def _():
            xt_far.wait_send()
            far_sum.wait_send()

    for source in range(2):
        for dc in range(2):
            arrival = pltpu.make_async_remote_copy(
                src_ref=p3.at[0, 0], dst_ref=r3.at[0, 0], send_sem=psem.at[0, 0, dc],
                recv_sem=psem.at[source, 1, dc], device_id=cpeer, device_id_type=MESH,
            )
            if dc:
                arrival.wait_recv()
            else:

                @pl.when(zh != source)
                def _():
                    arrival.wait_recv()

    for half in range(2):
        value = r3[half, 0].astype(F32) + r3[half, 1].astype(F32)
        kout_ref[:, 0, half * 128 : half * 128 + 128] = value[0:108] * SCALE

    for plane_id in range(2):
        to_owner(plane_id, 1).wait_send()

        @pl.when(zh != plane_id)
        def _():
            to_owner(plane_id, 0).wait_send()


def write_out(*refs):
    for source, target in zip(refs[:4], refs[4:]):
        target[...] = source[...]


def on_device(saved_inputs, cotangent, kernels, gains, biases):
    inputs = saved_inputs.reshape(8, 32, CH)
    seeds = cotangent.reshape(8, 32, CH)
    vmem = pl.BlockSpec(memory_space=pltpu.VMEM)
    hbm = pl.BlockSpec(memory_space=pltpu.HBM)
    v = pltpu.VMEM
    dma = pltpu.SemaphoreType.DMA
    made = pl.pallas_call(
        kernel,
        out_shape=(
            jax.ShapeDtypeStruct((8, 32, CH), BF16),
            jax.ShapeDtypeStruct((108, 1, CH), F32),
            jax.ShapeDtypeStruct((1, CH), F32),
            jax.ShapeDtypeStruct((1, CH), F32),
        ),
        in_specs=[hbm] * 5,
        out_specs=[vmem] * 4,
        scratch_shapes=[
            v((8, 32, CH), BF16), v((8, 32, CH), BF16), v((27 * CH, CH), BF16), v((1, CH), F32), v((1, CH), F32),
            v((FR, 32, CH), BF16), v((2, 8, 128), F32), v((4, 8, 128), F32), v((FR, 32, CH), BF16), v((FR, 32, CH), BF16),
            v((ROWS, CH), F32), v((32, CH), F32),
            v((2, 32, CH), BF16), v((64, CH), BF16), v((2, 2, 16, CH), BF16), v((2, 2, 32, CH), BF16),
            v((FR, 2, 32, CH), BF16), v((4, 32, CH), BF16), v((4, 16, CH), BF16),
            v((6, 2, 32, CH), BF16), v((4, 48, CH), BF16), v((4, 2, 16, CH), BF16),
            v((FR, 2, 32, CH), BF16), v((4, 32, CH), BF16), v((4, 16, CH), BF16),
            v((6, 2, 32, CH), BF16), v((4, 48, CH), BF16), v((4, 2, 16, CH), BF16),
            v((ALL, CH), F32), v((4, 48, CH), F32), v((2, 4, 16, CH), F32), v((60, 24, CH), F32),
            v((ROWS, CH), F32), v((2 * ALL, 9 * CH), BF16), v((27 * CH, CH), BF16),
            v((CH, 2 * ROWS), BF16), v((ROWS, CH), F32), v((ROWS, CH), F32), v((ROWS, CH), F32), v((8, CH), F32),
            v((16, 8, 128), F32), v((2, 16, 128), F32), v((16, 16, 128), F32),
            v((8, 128), F32), v((8, 128), F32), v((8, 128), F32), v((2, 8, 128), F32), v((8, CH), F32),
            v((16, 128), F32), v((16, 128), F32),
            v((27 * CH, 128), F32), v((27 * CH, 128), BF16), v((27 * CH, 128), BF16),
            v((3, 864, 128), BF16), v((4, 4, 224, 128), BF16), v((3, 864, 128), BF16), v((3, 4, 224, 128), BF16),
            v((4, 224, 128), BF16), v((3, 224, 128), BF16), v((4, 216, 128), F32), v((216, 128), F32),
            v((3, 224, 128), BF16), v((3, 224, 128), BF16), v((2, 2, 112, 128), BF16), v((2, 2, 112, 128), BF16),
            dma((6,)), dma((4, 2)), dma((2, 2, 6)), dma((2, 2)), dma((2, 4, 2)), dma((2, 4, 2)),
            dma((2, 2)), dma((2, 4, 2)), dma((2, 4, 2)),
            dma((3, 2)), dma((16, 2)), dma((2,)), dma((16, 2)), dma((4, 2)), dma((4, 2)),
            dma((3, 2)), dma((4, 3, 2)), dma((3, 2)), dma((3, 2)), dma((2, 2, 2)),
        ],
        compiler_params=pltpu.CompilerParams(
            collective_id=0, has_side_effects=True, vmem_limit_bytes=VMEM_LIMIT
        ),
        name="blocks",
    )(inputs, seeds, kernels[0], gains, biases)
    out, kout, gout, bout = pl.pallas_call(
        write_out,
        out_shape=tuple(jax.ShapeDtypeStruct(m.shape, m.dtype) for m in made),
        in_specs=[vmem] * 4,
        out_specs=[vmem] * 4,
        name="write_out",
    )(*made)
    return out.reshape(1, 8, 1, 4, 8, CH), kout.reshape(1, 108, CH), gout, bout


def solution(mesh):
    in_specs = (
        P("section", None, "tile", None, None, None),
        P(None, "tile", None, None, None),
        P("section", None, None),
        P("section", None),
        P("section", None),
    )
    out_specs = (
        P("section", None, "tile", None, None, None),
        P("section", "tile", None),
        P("section", None),
        P("section", None),
    )
    return jax.shard_map(
        on_device, mesh=mesh, in_specs=in_specs, out_specs=out_specs, check_vma=False
    )
```

```python
import functools
import math

import jax
import jax.numpy as jnp
from jax import lax
from jax.experimental import pallas as pl
from jax.experimental.pallas import tpu as pltpu
from jax.sharding import PartitionSpec as P

CH = 256
GROUPS = 32
PER_GROUP = CH // GROUPS
FR = 4
PX = 64
ROWS = FR * PX
ALL = ROWS + 2 * PX
ENTRIES = float(64 * 32 * PER_GROUP)
SCALE = 1.0 / math.sqrt(8 * 64 * 32)
EPS = 1e-05
VMEM_LIMIT = 62 * 2**20
MESH = pl.DeviceIdType.MESH
SIDES = ((-1, 0), (1, 0), (0, -1), (0, 1))
CORNERS = ((-1, -1), (-1, 1), (1, -1), (1, 1))
AROUND = [(dx, dy, dc) for dx in (-1, 0, 1) for dy, dc in ((0, 0), (-1, 1), (0, 1), (1, 1))]
CHIPS = sorted(
    ((dx, dy) for dx in range(4) for dy in range(4)),
    key=lambda d: (d != (0, 0), -min(d[0], 4 - d[0]) - min(d[1], 4 - d[1]), d),
)
QUARTER = 1728
F32 = jnp.float32
BF16 = jnp.bfloat16


def kernel(
    x_hbm, cot_hbm, k_hbm, gain_hbm, bias_hbm,
    out_ref, kout_ref, gout_ref, bout_ref,
    x_ref, cot_ref, k_ref, gain_ref, bias_ref,
    xr, xst, xstr, osend, orecv, rf, strip, lrs, rows_s, nooks, lr,
    wc, wh, wn, gc, gh, gn, xwc, xwh, xwn, xgc, xgh, xgn,
    xc, xs, xn, gp, gcen, cols, kt_ref, a_t, xhat, dfac, da, rs,
    sb, ua, ub, unear, ufar, xt, xtr, mom, zg, zgr,
    dko, dks, dkr, b0, b1, rx, ry, p0, p1, t0, t1, r2x, r2y, p3, r3,
    lsem, zsem, dsem, wgs, whs, wns, xgs, xhs, xns, asem, aps, ucs, ups, tsem, csem, xsem, ysem, xsem2, ysem2, psem,
):
    s = lax.axis_index("section")
    t = lax.axis_index("tile")
    x = t // 16
    zh = (t // 8) % 2
    y = (t // 2) % 4
    core = t % 2
    col = t % 8
    chip = x * 4 + y

    def at(sec, dx, z2, dy, dc):
        return (sec, ((x + dx + 4) % 4) * 16 + z2 * 8 + ((y + dy + 4) % 4) * 2 + (core + dc) % 2)

    def beside(sec, dx, z2, dcol):
        return (sec, ((x + dx + 4) % 4) * 16 + z2 * 8 + (col + dcol + 8) % 8)

    zpeer = at(s, 0, 1 - zh, 0, 0)
    cpeer = at(s, 0, zh, 0, 1)

    def remote(src, dst, pair, device):
        return pltpu.make_async_remote_copy(
            src_ref=src, dst_ref=dst, send_sem=pair.at[0], recv_sem=pair.at[1],
            device_id=device, device_id_type=MESH,
        )

    x_load = pltpu.make_async_copy(x_hbm, x_ref, lsem.at[0])
    cot_load = pltpu.make_async_copy(cot_hbm, cot_ref, lsem.at[1])
    k_load = pltpu.make_async_copy(k_hbm, k_ref, lsem.at[2])
    gain_load = pltpu.make_async_copy(gain_hbm, gain_ref, lsem.at[3])
    bias_load = pltpu.make_async_copy(bias_hbm, bias_ref, lsem.at[4])
    x_load.start()
    gain_load.start()
    bias_load.start()

    @pl.when(s == 3)
    def _():
        cot_load.start()

    k_load.start()

    barrier = pltpu.get_barrier_semaphore()

    def greet(device):
        pl.semaphore_signal(barrier, inc=1, device_id=device, device_id_type=MESH)

    plane = [(dx, 0, dy, 0) for dx, dy in CHIPS if (dx, dy) != (0, 0)]
    plane = [(0, 1, 0, 0), (0, 1, 0, 1)] + plane + [(0, 0, 0, 1)]
    @pl.when(s == 3)
    def _():
        for dx, dy, dc in AROUND:
            greet(at(3, dx, 1 - zh, dy, dc))
        for dx, dy, dc in AROUND:
            if (dx, dy, dc) != (0, 0, 0):
                greet(at(3, dx, zh, dy, dc))

    for dx, z, dy, dc in plane:
        greet(at(s, dx, (zh + z) % 2, dy, dc))

    @pl.when(s < 3)
    def _():
        for dx, dy, dc in AROUND:
            greet(at(s + 1, dx, zh, dy, dc))

        @pl.when(zh == 0)
        def _():
            for dx, dy, dc in AROUND:
                greet(at(s + 1, dx, 1, dy, dc))

    expected = len(plane) + jnp.where(s > 0, (1 + zh) * len(AROUND), 0)
    expected = expected + jnp.where(s == 3, 2 * len(AROUND) - 1, 0)
    theirs = pl.ds((1 - zh) * FR, FR)
    ours = pl.ds(zh * FR, FR)

    def indicator(shape, channel_dim):
        channel = lax.broadcasted_iota(jnp.int32, shape, channel_dim)
        group = lax.broadcasted_iota(jnp.int32, shape, 1 - channel_dim)
        return (channel // PER_GROUP == group).astype(F32)

    def grouped(first, second):
        return jnp.dot(
            jnp.concatenate([first, second], axis=0), indicator((CH, 128), 0),
            precision=lax.Precision.HIGHEST, preferred_element_type=F32,
        )

    def spread(groups):
        return jnp.dot(
            groups, indicator((128, CH), 1), precision=lax.Precision.HIGHEST, preferred_element_type=F32
        )

    x_load.wait()

    def tile_sums(frames):
        value = x_ref[frames].astype(F32)
        return grouped(jnp.sum(value, axis=1), jnp.sum(value * value, axis=1))

    xst[0] = tile_sums(theirs)
    xst[1] = tile_sums(ours)
    pl.semaphore_wait(barrier, expected)

    def each(copies, what):
        for c in copies:
            getattr(c, what)()

    x_copy = remote(x_hbm.at[theirs], xr, zsem.at[0], zpeer)

    def patch(own, other):
        own = own.astype(F32)
        other = other.astype(F32)
        upper = jnp.where(zh == 0, own, other)
        lower = jnp.where(zh == 0, other, own)
        return jnp.concatenate([upper, lower], axis=1).reshape(ROWS, CH)

    def core_sum_copy(buf, pair):
        return remote(buf.at[core], buf.at[core], pair, cpeer)

    def chip_copies(buf, sems):
        return [
            remote(buf.at[chip], buf.at[chip], sems.at[i], at(s, dx, zh, dy, 0))
            for i, (dx, dy) in enumerate(CHIPS) if i
        ]

    mine = zh * 2 + core
    xst_copies = [
        remote(xst.at[0], xstr.at[mine], asem.at[0], zpeer),
        remote(xst.at[0], xstr.at[mine], asem.at[1], at(s, 0, 1 - zh, 0, 1)),
        remote(xst.at[1], xstr.at[mine], asem.at[2], cpeer),
    ]
    each(xst_copies, "start")

    @pl.when(s == 3)
    def _():
        x_copy.start()

    xstr[mine] = xst[1]

    def pack(value, send, copies):
        center, sides, corners = send
        near, middle, _ = copies
        rf[...] = value
        for i, pixel in enumerate((0, 7, 56, 63)):
            rows = [rf[f * PX + pixel : f * PX + pixel + 1, :] for f in range(FR)]
            corners[i] = jnp.concatenate(rows + [jnp.zeros((12, CH), F32)], axis=0).astype(BF16)
        each(near[0:4], "start")
        v4 = value.reshape(FR, 8, 8, CH)
        sides[0] = v4[:, 0].reshape(32, CH).astype(BF16)
        sides[1] = v4[:, 7].reshape(32, CH).astype(BF16)
        each(near[4:6], "start")
        for i, lead in ((2, 0), (3, 7)):
            for f in range(FR):
                rows = [rf[f * PX + r * 8 + lead : f * PX + r * 8 + lead + 1, :] for r in range(8)]
                strip[f * 8 : f * 8 + 8, :] = jnp.concatenate(rows, axis=0)
            sides[i] = strip[...].astype(BF16)
        each(near[6:8], "start")
        center[...] = value.astype(BF16).reshape(FR, 2, 32, CH)
        middle.start()

    def piece_copies(sec, send, recv, sems):
        center, sides, corners = send
        center_r, sides_r, corners_r = recv
        gs, hs, ns = sems
        near, far = [], []
        for i, (dx, dc) in enumerate(CORNERS):
            near.append(remote(corners.at[i], corners_r.at[i, 0], ns.at[0, i], beside(sec, dx, zh, dc)))
            far.append(remote(corners.at[i], corners_r.at[i, 1], ns.at[1, i], beside(sec, dx, 0, dc)))
        for i, (dx, dc) in enumerate(SIDES):
            near.append(remote(sides.at[i], sides_r.at[i, pl.ds(0, 32)], hs.at[0, i], beside(sec, dx, zh, dc)))
            far.append(
                remote(sides.at[i, pl.ds(0, 16)], sides_r.at[i, pl.ds(32, 16)], hs.at[1, i], beside(sec, dx, 0, dc))
            )
        middle = remote(center, center_r.at[pl.ds(0, FR)], gs.at[0], beside(sec, 0, zh, 0))
        far.append(
            remote(center.at[pl.ds(0, 2)], center_r.at[pl.ds(FR, 2)], gs.at[1], beside(sec, 0, 0, 0))
        )
        return near, middle, far

    def wait_sent(copies, with_middle):
        near, middle, far = copies
        each(near + ([middle] if with_middle else []), "wait_send")

        @pl.when(zh == 1)
        def _():
            each(far, "wait_send")

    def wait_received(copies, with_middle):
        near, middle, far = copies
        each(near + ([middle] if with_middle else []), "wait_recv")

        @pl.when(zh == 0)
        def _():
            each(far, "wait_recv")

    w_send, w_recv, w_sems = (wc, wh, wn), (gc, gh, gn), (wgs, whs, wns)
    x_send, x_recv, x_sems = (xwc, xwh, xwn), (xgc, xgh, xgn), (xgs, xhs, xns)

    frames_of = (pl.ds(0, 6), pl.ds(4, 4))
    count_of = (6, 4)

    def direct_copies(plane_id):
        n = count_of[plane_id]
        lead = 4 * plane_id
        lr_rows = pl.ds(16 * plane_id, 32 - 16 * plane_id)
        row_rows = pl.ds(8 * lead, 8 * n)
        down = 2 * zh - 1
        pair = dsem.at[plane_id]

        def send(src, dst, slot, device):
            return pltpu.make_async_remote_copy(
                src_ref=src, dst_ref=dst, send_sem=pair.at[0, slot], recv_sem=dsem.at[zh, 1, slot],
                device_id=device, device_id_type=MESH,
            )

        nook_rows = pl.ds(plane_id, 2 - plane_id)
        landing = pl.ds(0, 2 - plane_id)
        copies = [
            send(nooks.at[0, nook_rows], gn.at[2 * zh, landing], 3, beside(3, down, plane_id, -1)),
            send(nooks.at[1, nook_rows], gn.at[2 * zh + 1, landing], 4, beside(3, down, plane_id, 1)),
            send(rows_s.at[row_rows], gh.at[zh, pl.ds(0, 8 * n)], 2, beside(3, down, plane_id, 0)),
            send(lrs.at[0, lr_rows], lr.at[0, zh, pl.ds(0, 32 - 16 * plane_id)], 0, beside(3, 0, plane_id, -1)),
            send(lrs.at[1, lr_rows], lr.at[1, zh, pl.ds(0, 32 - 16 * plane_id)], 1, beside(3, 0, plane_id, 1)),
        ]
        center = send(
            cot_hbm.at[frames_of[plane_id]], gc.at[pl.ds(0, n), zh], 5, beside(3, 0, plane_id, 0)
        )
        return copies, center

    def own_half(plane_id):
        return pltpu.make_async_copy(
            cot_hbm.at[frames_of[plane_id]], gc.at[pl.ds(0, count_of[plane_id]), plane_id], lsem.at[5]
        )

    def direct_arrivals(plane_id):
        n = count_of[plane_id]
        arrivals = []
        for source in range(2):
            sizes = (
                lr.at[0, 0, pl.ds(0, 32 - 16 * plane_id)], lr.at[0, 0, pl.ds(0, 32 - 16 * plane_id)],
                gh.at[0, pl.ds(0, 8 * n)],
                gn.at[0, pl.ds(0, 2 - plane_id)], gn.at[0, pl.ds(0, 2 - plane_id)],
            ) + ((gc.at[pl.ds(0, n), 0],) if source != plane_id else ())
            for slot, ref in enumerate(sizes):
                arrivals.append(
                    pltpu.make_async_remote_copy(
                        src_ref=ref, dst_ref=ref, send_sem=dsem.at[0, 0, slot],
                        recv_sem=dsem.at[source, 1, slot], device_id=cpeer, device_id_type=MESH,
                    )
                )
        return arrivals

    @pl.when(s == 3)
    def _():
        for plane_id in range(2):

            @pl.when(zh == plane_id)
            def _():
                direct_copies(1 - plane_id)[1].start()
                own_half(plane_id).start()

        cot_load.wait()
        rf[...] = cot_ref[...].astype(F32).reshape(ROWS, CH)
        for i, lead in ((0, 0), (1, 7)):
            for f in range(8):
                picks = [rf[f * 32 + r * 8 + lead : f * 32 + r * 8 + lead + 1, :] for r in range(4)]
                strip[f * 4 : f * 4 + 4, :] = jnp.concatenate(picks, axis=0)
            lrs[i] = strip[...].astype(BF16)
        outer_rows = []
        for f in range(8):
            outer_rows.append(
                jnp.where(zh == 0, rf[f * 32 : f * 32 + 8, :], rf[f * 32 + 24 : f * 32 + 32, :])
            )
        rows_s[...] = jnp.concatenate(outer_rows, axis=0).astype(BF16)
        for i, end in ((0, 0), (1, 7)):
            for part in range(2):
                picks = [outer_rows[part * 4 + f][end : end + 1] for f in range(4)]
                nooks[i, part] = jnp.concatenate(picks + [jnp.zeros((12, CH), F32)], axis=0).astype(BF16)
        for plane_id in (1, 0):
            each(direct_copies(plane_id)[0], "start")

    def direct_done():
        for plane_id in range(2):

            @pl.when(zh == plane_id)
            def _():
                each(direct_arrivals(plane_id), "wait_recv")
                own_half(plane_id).wait()
                n = count_of[plane_id]
                for i in range(2):
                    halves = [lr[i, z2].astype(F32)[0 : 4 * n].reshape(n, 4, CH) for z2 in range(2)]
                    gh[2 + i, 0 : 8 * n, :] = (
                        jnp.concatenate(halves, axis=1).reshape(8 * n, CH).astype(BF16)
                    )

            each(direct_copies(plane_id)[0], "wait_send")

            @pl.when(zh != plane_id)
            def _():
                direct_copies(plane_id)[1].wait_send()

    each(xst_copies, "wait")
    sb[chip] = jnp.sum(xstr[...], axis=0)
    sb_copies = chip_copies(sb, aps)
    each(sb_copies, "start")

    @pl.when(s < 3)
    def _():
        x_copy.start()

    x_copy.wait()
    xv = patch(x_ref[ours], xr[...])
    xhat[...] = xv

    @pl.when(s > 0)
    def _():
        copies = piece_copies(s - 1, x_send, x_recv, x_sems)
        pack(xv, x_send, copies)

        @pl.when(zh == 1)
        def _():
            each(copies[2], "start")

    k_load.wait()

    def flip(i, carry):
        rows = pl.ds(pl.multiple_of(i * CH, CH), CH)
        kt_ref[rows, :] = jnp.transpose(k_ref[rows, :])
        return carry

    lax.fori_loop(0, 27, flip, 0)

    xt_near = remote(xt, xtr.at[0], tsem.at[0], at(s - 1, 0, zh, 0, 0))
    xt_far = remote(xt, xtr.at[1], tsem.at[1], at(s - 1, 0, 0, 0, 0))

    def moments(total):
        total = spread(total / ENTRIES)
        mean = total[0:4]
        return mean, lax.rsqrt(total[4:8] - mean * mean + EPS)

    def prepare():
        gain_load.wait()
        bias_load.wait()
        each(sb_copies, "wait")
        xt[...] = jnp.sum(sb[...], axis=0)
        @pl.when(s > 0)
        def _():
            xt_near.start()

            @pl.when(zh == 1)
            def _():
                xt_far.start()

        mean, rstd = moments(xt[...])
        gain = gain_ref[...]
        rs[0:FR, :] = rstd
        xh = (xhat[...].reshape(FR, PX, CH) - mean[:, None, :]) * rstd[:, None, :]
        h = xh * gain[None] + bias_ref[...][None]
        sg = jax.nn.sigmoid(h)
        xhat[...] = xh.reshape(ROWS, CH)
        dfac[...] = (sg * (1.0 + h * (1.0 - sg))).reshape(ROWS, CH)
        act = h * sg
        a_t[...] = jnp.transpose(jnp.concatenate([act, -act], axis=1).reshape(2 * ROWS, CH)).astype(BF16)

    @pl.when(s < 3)
    def _():
        prepare()

    @pl.when(s < 3)
    def _():
        wait_received(piece_copies(s, x_send, x_recv, x_sems), True)
        remote(xt, xtr.at[0], tsem.at[0], cpeer).wait_recv()

        @pl.when(zh == 0)
        def _():
            remote(xt, xtr.at[1], tsem.at[1], cpeer).wait_recv()

        def normalise(frames, part, row0):
            mean_up, rstd_up = moments(xtr[part])
            n = len(frames)
            mom[frames[0] : frames[0] + n, :] = rstd_up[0:n]
            m, r = mean_up[0:n][:, None, :], rstd_up[0:n][:, None, :]
            px = slice(frames[0] * PX, (frames[0] + n) * PX)
            up = xgc[frames[0] : frames[0] + n].astype(F32).reshape(n, PX, CH)
            xc[px, :] = ((up - m) * r).reshape(n * PX, CH)
            for i in range(4):
                side = xgh[i, row0 : row0 + 8 * n, :].astype(F32).reshape(n, 8, CH)
                xs[i, row0 : row0 + 8 * n, :] = ((side - m) * r).reshape(8 * n, CH)
                xn[part, i, 0:n, :] = (xgn[i, part].astype(F32)[0:n] - mean_up[0:n]) * rstd_up[0:n]

        normalise(range(4), 0, 0)

        @pl.when(zh == 0)
        def _():
            normalise(range(4, 6), 1, 32)

    arriving = piece_copies(s, w_send, w_recv, w_sems)

    edge = (x > 0, x < 3, col > 0, col < 7)

    def columns(frames, center, sides, corners, shift):
        top = jnp.where(edge[0], sides[1], 0.0)
        bottom = jnp.where(edge[1], sides[0], 0.0)
        left = jnp.where(edge[2], sides[3], 0.0)
        right = jnp.where(edge[3], sides[2], 0.0)
        top_left = jnp.where(edge[0] & edge[2], corners[3], 0.0)
        top_right = jnp.where(edge[0] & edge[3], corners[2], 0.0)
        bottom_left = jnp.where(edge[1] & edge[2], corners[1], 0.0)
        bottom_right = jnp.where(edge[1] & edge[3], corners[0], 0.0)
        center = center.reshape(len(frames), 8, 8, CH)
        for i, f in enumerate(frames):
            base = f * 10
            cell = slice(i * 8, i * 8 + 8)
            gp[base + 1 : base + 9, 8:16, :] = center[i]
            gp[base, 8:16, :] = top[cell]
            gp[base + 9, 8:16, :] = bottom[cell]
            for r in range(8):
                gp[base + 1 + r, 7:8, :] = left[i * 8 + r : i * 8 + r + 1]
                gp[base + 1 + r, 16:17, :] = right[i * 8 + r : i * 8 + r + 1]
            gp[base, 7:8, :] = top_left[i : i + 1]
            gp[base, 16:17, :] = top_right[i : i + 1]
            gp[base + 9, 7:8, :] = bottom_left[i : i + 1]
            gp[base + 9, 16:17, :] = bottom_right[i : i + 1]
            for ox in range(3):
                band = gp[base : base + 10, 7 + ox : 15 + ox, :]
                for oy in range(3):
                    tap = (2 - oy) * 3 + (2 - ox)
                    cols[f * 2 * PX + shift : f * 2 * PX + shift + PX, tap * CH : tap * CH + CH] = (
                        band[oy : oy + 8].reshape(PX, CH).astype(BF16)
                    )

    def fill(frames, part, row0):
        n = len(frames)
        columns(
            frames, gc[frames[0] : frames[0] + n].astype(F32),
            [gh[i, row0 : row0 + 8 * n, :].astype(F32) for i in range(4)],
            [gn[i, part].astype(F32)[0:n] for i in range(4)], 0,
        )

    def fill_correction(frames, part, row0, sums):
        n = len(frames)
        both = spread(sums / ENTRIES)
        r_up = mom[frames[0] : frames[0] + n, :]
        c1, c2 = r_up * both[0:n], r_up * both[4 : 4 + n]

        def term(hat, rows):
            value = c1[:, None, :] + hat.reshape(n, rows, CH) * c2[:, None, :]
            return value.reshape(n * rows, CH)

        px = slice(frames[0] * PX, (frames[0] + n) * PX)
        center = term(xc[px, :], PX)
        if part == 0:
            gcen[...] = gc[0:FR].astype(F32).reshape(ROWS, CH) - center
        columns(
            frames, center, [term(xs[i, row0 : row0 + 8 * n, :], 8) for i in range(4)],
            [c1 + xn[part, i, 0:n, :] * c2 for i in range(4)], PX,
        )

    def convolve(shift):
        value = jnp.zeros((ROWS, CH), F32)
        for kt in range(3):
            starts = [(2 - kt + f) * 2 * PX + shift for f in range(FR)]
            value = value + jnp.dot(
                jnp.concatenate([cols[r : r + PX, :] for r in starts], axis=0),
                kt_ref[kt * 9 * CH : (kt + 1) * 9 * CH, :],
                preferred_element_type=F32,
            )
        return value

    def gather():
        near, middle, far = arriving

        @pl.when(s == 3)
        def _():
            direct_done()

        @pl.when(s < 3)
        def _():
            each(near, "wait_recv")
            middle.wait_recv()

        fill(range(4), 0, 0)

        @pl.when(zh == 0)
        def _():
            @pl.when(s < 3)
            def _():
                each(far, "wait_recv")

            fill(range(4, 6), 1, 32)

        @pl.when(zh == 1)
        def _():
            cols[2 * ROWS :, :] = jnp.zeros((4 * PX, 9 * CH), BF16)

        da[...] = convolve(0)

    @pl.when(s == 3)
    def _():
        gather()
        prepare()

    @pl.when(s < 3)
    def _():
        gather()

    gain = gain_ref[...]
    rstd = rs[0:FR, :]

    def one_tap(tap):
        rows = pl.ds(pl.multiple_of(tap * CH, CH), CH)
        lanes = pl.multiple_of((tap % 9) * CH, CH)
        frames = pl.multiple_of((2 - tap // 9) * 2 * PX, 2 * PX)
        part = jnp.dot(
            a_t[...], cols[pl.ds(frames, 2 * ROWS), pl.ds(lanes, CH)], preferred_element_type=F32
        )
        dko[rows, :] = jnp.where(core == 0, part[:, :128], part[:, 128:])
        dks[rows, :] = jnp.where(core == 0, part[:, 128:], part[:, :128]).astype(BF16)

    def own_rows(step, offset, count):
        q = (x + 1 + step) % 4
        return pl.ds(pl.multiple_of(q * QUARTER + offset, 8), count)

    def core_copy(step):
        q = (x + 1 + step) % 4
        span = pl.ds(pl.multiple_of(q * QUARTER, 16), QUARTER)
        return remote(dks.at[span], dkr.at[span], csem.at[step], cpeer)

    def quarter(step):
        q = (x + 1 + step) % 4
        if step == 0:
            @pl.when(x < 3)
            def _():
                one_tap(7 * x + 6)

        for i in range(6):
            one_tap(7 * q + i)
        if step < 3:
            one_tap(7 * q + 6 - q // 3)
        core_copy(step).start()

    def x_first(step):
        return remote(b0.at[step], rx.at[step], xsem.at[step], at(s, step + 1, zh, 0, 0))

    def y_first(step, k):
        return remote(b1.at[step, (y + k) % 4], ry.at[k - 1, step], ysem.at[step, k - 1], at(s, 0, zh, k, 0))

    pad8 = jnp.zeros((8, 128), F32)

    def join(step):
        core_copy(step).wait()
        for half in range(4):
            rows = own_rows(step, half * 432, 432)
            both_cores = dko[rows, :] + dkr[rows, :].astype(F32)
            dko[rows, :] = both_cores
            if half >= 2:
                for i in range(2):
                    piece = jnp.concatenate([both_cores[i * 216 : i * 216 + 216], pad8], axis=0)
                    b1[step, (half - 2) * 2 + i] = piece.astype(BF16)
            elif step < 3:
                b0[step, half * 432 : half * 432 + 432, :] = both_cores.astype(BF16)
        if step < 3:
            x_first(step).start()
        for k in range(1, 4):
            y_first(step, k).start()

    def then_x(step):
        return remote(p1.at[step], r2x.at[step], xsem2.at[step], at(s, step + 1, zh, 0, 0))

    def then_y(k):
        return remote(p0.at[(y + k) % 4], r2y.at[k - 1], ysem2.at[k - 1], at(s, 0, zh, k, 0))

    def sum_y(step):
        for k in range(1, 4):
            y_first(step, k).wait()
        acc = dko[own_rows(step, 864 + y * 216, 216), :]
        for k in range(3):
            acc = acc + ry[k, step].astype(F32)[0:216]
        if step < 3:
            p1[step] = jnp.concatenate([acc, pad8], axis=0).astype(BF16)
            then_x(step).start()
        else:
            t1[...] = acc

    def sum_x():
        for step in range(3):
            x_first(step).wait()
        for half in range(2):
            acc = dko[own_rows(3, half * 432, 432), :]
            for k in range(3):
                acc = acc + rx[k, half * 432 : half * 432 + 432, :].astype(F32)
            for i in range(2):
                piece = acc[i * 216 : i * 216 + 216]
                t0[half * 2 + i] = piece
                p0[half * 2 + i] = jnp.concatenate([piece, pad8], axis=0).astype(BF16)
        for k in range(1, 4):
            then_y(k).start()

    @pl.when(s == 3)
    def _():
        gcen[...] = gc[0:FR].astype(F32).reshape(ROWS, CH)
        for f in range(6):
            cols[f * 2 * PX + PX : f * 2 * PX + 2 * PX, :] = jnp.zeros((PX, 9 * CH), BF16)

    @pl.when(s < 3)
    def _():
        remote(zg.at[pl.ds(0, 8)], unear, tsem.at[3], cpeer).wait_recv()
        fill_correction(range(4), 0, 0, unear[...])

        @pl.when(zh == 0)
        def _():
            remote(zg.at[pl.ds(0, 8)], ufar, tsem.at[2], cpeer).wait_recv()
            fill_correction(range(4, 6), 1, 32, ufar[...])


    @pl.when(s == 0)
    def _():
        quarter(0)
        quarter(1)
        join(0)
        quarter(2)
        join(1)
        quarter(3)
        join(2)
        join(3)

    @pl.when(s < 3)
    def _():
        da[...] = da[...] - convolve(PX)

    dh3 = (da[...] * dfac[...]).reshape(FR, PX, CH)
    dh_sum = jnp.sum(dh3, axis=1)
    dhx_sum = jnp.sum(dh3 * xhat[...].reshape(FR, PX, CH), axis=1)
    gain_part = jnp.sum(dhx_sum, axis=0, keepdims=True)
    bias_part = jnp.sum(dh_sum, axis=0, keepdims=True)
    ua[core] = jnp.concatenate(
        [
            grouped(dh_sum * gain, dhx_sum * gain),
            gain_part[:, :128], gain_part[:, 128:], bias_part[:, :128], bias_part[:, 128:],
            jnp.zeros((4, 128), F32),
        ],
        axis=0,
    )
    ua_copy = core_sum_copy(ua, ucs)
    ua_copy.start()

    w = gcen[...] + (rstd[:, None, :] * (dh3 * gain[None])).reshape(ROWS, CH)
    dfac[...] = w

    w_copies = piece_copies(s - 1, w_send, w_recv, w_sems)

    @pl.when(s > 0)
    def _():
        pack(w, w_send, w_copies)

    ua_copy.wait()
    ub[chip] = ua[0] + ua[1]
    ub_copies = chip_copies(ub, ups)
    each(ub_copies, "start")

    @pl.when((s > 0) & (zh == 1))
    def _():
        each(w_copies[2], "start")

    @pl.when(s > 0)
    def _():
        quarter(0)
        quarter(1)

    def axis_sums():
        sum_y(0)
        sum_y(1)
        sum_y(2)
        sum_x()
        sum_y(3)

    @pl.when(s == 0)
    def _():
        axis_sums()

    each(ub_copies, "wait")
    total = jnp.sum(ub[...], axis=0)
    zg[...] = total
    near_sum = remote(zg.at[pl.ds(0, 8)], unear, tsem.at[3], at(s - 1, 0, zh, 0, 0))
    far_sum = remote(zg.at[pl.ds(0, 8)], ufar, tsem.at[2], at(s - 1, 0, 0, 0, 0))

    @pl.when(s > 0)
    def _():
        near_sum.start()

        @pl.when(zh == 1)
        def _():
            far_sum.start()

    zg_copy = remote(zg, zgr, zsem.at[3], zpeer)
    zg_copy.start()
    both = spread(total[0:8] / ENTRIES)
    c1, c2 = rstd * both[0:4], rstd * both[4:8]
    xh = xhat[...].reshape(FR, PX, CH)
    final = dfac[...].reshape(FR, PX, CH) - c1[:, None, :] - xh * c2[:, None, :]
    final = final.astype(BF16).reshape(FR, 2, 32, CH)
    osend[...] = jnp.where(zh == 0, final[:, 1], final[:, 0])
    o_copy = remote(osend, orecv, zsem.at[2], zpeer)
    o_copy.start()
    out_ref[ours] = jnp.where(zh == 0, final[:, 0], final[:, 1])

    @pl.when(s > 0)
    def _():
        join(0)
        quarter(2)
        join(1)
        quarter(3)
        join(2)
        join(3)

    @pl.when(s > 0)
    def _():
        axis_sums()

    pad4 = jnp.zeros((4, 128), F32)

    def to_owner(plane_id, dc):
        return pltpu.make_async_remote_copy(
            src_ref=p3.at[plane_id, (core + dc) % 2], dst_ref=r3.at[core, zh],
            send_sem=psem.at[plane_id, 0, dc], recv_sem=psem.at[zh, 1, dc],
            device_id=at(s, 0, plane_id, 0, dc), device_id_type=MESH,
        )

    def finish(plane_id):
        if plane_id:
            acc = t1[...]
            for step in range(3):
                then_x(step).wait()
                acc = acc + r2x[step].astype(F32)[0:216]
        else:
            acc = t0[y]
            for k in range(1, 4):
                then_y(k).wait()
                acc = acc + r2y[k - 1].astype(F32)[0:216]
        p3[plane_id, 0] = jnp.concatenate([acc[0:108], pad4], axis=0).astype(BF16)
        p3[plane_id, 1] = jnp.concatenate([acc[108:216], pad4], axis=0).astype(BF16)
        to_owner(plane_id, 1).start()

        @pl.when(zh != plane_id)
        def _():
            to_owner(plane_id, 0).start()

        @pl.when(zh == plane_id)
        def _():
            r3[core, zh] = p3[plane_id, core]

    finish(1)
    finish(0)

    zg_copy.wait()
    sums = (zg[...] + zgr[...]) * SCALE
    gout_ref[:, 0:128] = sums[8:9]
    gout_ref[:, 128:256] = sums[9:10]
    bout_ref[:, 0:128] = sums[10:11]
    bout_ref[:, 128:256] = sums[11:12]
    o_copy.wait()
    out_ref[theirs] = orecv[...]

    @pl.when(s > 0)
    def _():
        wait_sent(piece_copies(s - 1, x_send, x_recv, x_sems), True)
        wait_sent(w_copies, True)
        xt_near.wait_send()
        near_sum.wait_send()

        @pl.when(zh == 1)
        def _():
            xt_far.wait_send()
            far_sum.wait_send()

    for source in range(2):
        for dc in range(2):
            arrival = pltpu.make_async_remote_copy(
                src_ref=p3.at[0, 0], dst_ref=r3.at[0, 0], send_sem=psem.at[0, 0, dc],
                recv_sem=psem.at[source, 1, dc], device_id=cpeer, device_id_type=MESH,
            )
            if dc:
                arrival.wait_recv()
            else:

                @pl.when(zh != source)
                def _():
                    arrival.wait_recv()

    for half in range(2):
        value = r3[half, 0].astype(F32) + r3[half, 1].astype(F32)
        kout_ref[:, 0, half * 128 : half * 128 + 128] = value[0:108] * SCALE

    for plane_id in range(2):
        to_owner(plane_id, 1).wait_send()

        @pl.when(zh != plane_id)
        def _():
            to_owner(plane_id, 0).wait_send()


def write_out(*refs):
    for source, target in zip(refs[:4], refs[4:]):
        target[...] = source[...]


def on_device(saved_inputs, cotangent, kernels, gains, biases):
    inputs = saved_inputs.reshape(8, 32, CH)
    seeds = cotangent.reshape(8, 32, CH)
    vmem = pl.BlockSpec(memory_space=pltpu.VMEM)
    hbm = pl.BlockSpec(memory_space=pltpu.HBM)
    v = pltpu.VMEM
    dma = pltpu.SemaphoreType.DMA
    made = pl.pallas_call(
        kernel,
        out_shape=(
            jax.ShapeDtypeStruct((8, 32, CH), BF16),
            jax.ShapeDtypeStruct((108, 1, CH), F32),
            jax.ShapeDtypeStruct((1, CH), F32),
            jax.ShapeDtypeStruct((1, CH), F32),
        ),
        in_specs=[hbm] * 5,
        out_specs=[vmem] * 4,
        scratch_shapes=[
            v((8, 32, CH), BF16), v((8, 32, CH), BF16), v((27 * CH, CH), BF16), v((1, CH), F32), v((1, CH), F32),
            v((FR, 32, CH), BF16), v((2, 8, 128), F32), v((4, 8, 128), F32), v((FR, 32, CH), BF16), v((FR, 32, CH), BF16),
            v((ROWS, CH), F32), v((32, CH), F32),
            v((2, 32, CH), BF16), v((64, CH), BF16), v((2, 2, 16, CH), BF16), v((2, 2, 32, CH), BF16),
            v((FR, 2, 32, CH), BF16), v((4, 32, CH), BF16), v((4, 16, CH), BF16),
            v((6, 2, 32, CH), BF16), v((4, 48, CH), BF16), v((4, 2, 16, CH), BF16),
            v((FR, 2, 32, CH), BF16), v((4, 32, CH), BF16), v((4, 16, CH), BF16),
            v((6, 2, 32, CH), BF16), v((4, 48, CH), BF16), v((4, 2, 16, CH), BF16),
            v((ALL, CH), F32), v((4, 48, CH), F32), v((2, 4, 16, CH), F32), v((60, 24, CH), F32),
            v((ROWS, CH), F32), v((2 * ALL, 9 * CH), BF16), v((27 * CH, CH), BF16),
            v((CH, 2 * ROWS), BF16), v((ROWS, CH), F32), v((ROWS, CH), F32), v((ROWS, CH), F32), v((8, CH), F32),
            v((16, 8, 128), F32), v((2, 16, 128), F32), v((16, 16, 128), F32),
            v((8, 128), F32), v((8, 128), F32), v((8, 128), F32), v((2, 8, 128), F32), v((8, CH), F32),
            v((16, 128), F32), v((16, 128), F32),
            v((27 * CH, 128), F32), v((27 * CH, 128), BF16), v((27 * CH, 128), BF16),
            v((3, 864, 128), BF16), v((4, 4, 224, 128), BF16), v((3, 864, 128), BF16), v((3, 4, 224, 128), BF16),
            v((4, 224, 128), BF16), v((3, 224, 128), BF16), v((4, 216, 128), F32), v((216, 128), F32),
            v((3, 224, 128), BF16), v((3, 224, 128), BF16), v((2, 2, 112, 128), BF16), v((2, 2, 112, 128), BF16),
            dma((6,)), dma((4, 2)), dma((2, 2, 6)), dma((2, 2)), dma((2, 4, 2)), dma((2, 4, 2)),
            dma((2, 2)), dma((2, 4, 2)), dma((2, 4, 2)),
            dma((3, 2)), dma((16, 2)), dma((2,)), dma((16, 2)), dma((4, 2)), dma((4, 2)),
            dma((3, 2)), dma((4, 3, 2)), dma((3, 2)), dma((3, 2)), dma((2, 2, 2)),
        ],
        compiler_params=pltpu.CompilerParams(
            collective_id=0, has_side_effects=True, vmem_limit_bytes=VMEM_LIMIT
        ),
        name="blocks",
    )(inputs, seeds, kernels[0], gains, biases)
    out, kout, gout, bout = pl.pallas_call(
        write_out,
        out_shape=tuple(jax.ShapeDtypeStruct(m.shape, m.dtype) for m in made),
        in_specs=[vmem] * 4,
        out_specs=[vmem] * 4,
        name="write_out",
    )(*made)
    return out.reshape(1, 8, 1, 4, 8, CH), kout.reshape(1, 108, CH), gout, bout


def solution(mesh):
    in_specs = (
        P("section", None, "tile", None, None, None),
        P(None, "tile", None, None, None),
        P("section", None, None),
        P("section", None),
        P("section", None),
    )
    out_specs = (
        P("section", None, "tile", None, None, None),
        P("section", "tile", None),
        P("section", None),
        P("section", None),
    )
    return jax.shard_map(
        on_device, mesh=mesh, in_specs=in_specs, out_specs=out_specs, check_vma=False
    )
```

```python
import functools
import math

import jax
import jax.numpy as jnp
from jax import lax
from jax.experimental import pallas as pl
from jax.experimental.pallas import tpu as pltpu
from jax.sharding import PartitionSpec as P

CH = 256
GROUPS = 32
PER_GROUP = CH // GROUPS
FR = 4
PX = 64
ROWS = FR * PX
ALL = ROWS + 2 * PX
ENTRIES = float(64 * 32 * PER_GROUP)
SCALE = 1.0 / math.sqrt(8 * 64 * 32)
EPS = 1e-05
VMEM_LIMIT = 62 * 2**20
MESH = pl.DeviceIdType.MESH
SIDES = ((-1, 0), (1, 0), (0, -1), (0, 1))
CORNERS = ((-1, -1), (-1, 1), (1, -1), (1, 1))
AROUND = [(dx, dy, dc) for dx in (-1, 0, 1) for dy, dc in ((0, 0), (-1, 1), (0, 1), (1, 1))]
CHIPS = sorted(
    ((dx, dy) for dx in range(4) for dy in range(4)),
    key=lambda d: (d != (0, 0), -min(d[0], 4 - d[0]) - min(d[1], 4 - d[1]), d),
)
QUARTER = 1728
F32 = jnp.float32
BF16 = jnp.bfloat16


def kernel(
    x_hbm, cot_hbm, k_hbm, gain_hbm, bias_hbm,
    out_ref, kout_ref, gout_ref, bout_ref,
    x_ref, cot_ref, k_ref, gain_ref, bias_ref,
    xr, xst, xstr, osend, orecv, rf, strip, lrs, rows_s, nooks, lr,
    wc, wh, wn, gc, gh, gn, xwc, xwh, xwn, xgc, xgh, xgn,
    xc, xs, xn, gp, gcen, cols, kt_ref, a_t, xhat, dfac, da, rs,
    sb, ua, ub, unear, ufar, xt, xtr, mom, zg, zgr,
    dko, dks, dkr, b0, b1, rx, ry, p0, p1, t0, t1, r2x, r2y, p3, r3,
    lsem, zsem, dsem, wgs, whs, wns, xgs, xhs, xns, asem, aps, ucs, ups, tsem, csem, xsem, ysem, xsem2, ysem2, psem,
):
    s = lax.axis_index("section")
    t = lax.axis_index("tile")
    x = t // 16
    zh = (t // 8) % 2
    y = (t // 2) % 4
    core = t % 2
    col = t % 8
    chip = x * 4 + y

    def at(sec, dx, z2, dy, dc):
        return (sec, ((x + dx + 4) % 4) * 16 + z2 * 8 + ((y + dy + 4) % 4) * 2 + (core + dc) % 2)

    def beside(sec, dx, z2, dcol):
        return (sec, ((x + dx + 4) % 4) * 16 + z2 * 8 + (col + dcol + 8) % 8)

    zpeer = at(s, 0, 1 - zh, 0, 0)
    cpeer = at(s, 0, zh, 0, 1)

    def remote(src, dst, pair, device):
        return pltpu.make_async_remote_copy(
            src_ref=src, dst_ref=dst, send_sem=pair.at[0], recv_sem=pair.at[1],
            device_id=device, device_id_type=MESH,
        )

    x_load = pltpu.make_async_copy(x_hbm, x_ref, lsem.at[0])
    cot_load = pltpu.make_async_copy(cot_hbm, cot_ref, lsem.at[1])
    k_load = pltpu.make_async_copy(k_hbm, k_ref, lsem.at[2])
    gain_load = pltpu.make_async_copy(gain_hbm, gain_ref, lsem.at[3])
    bias_load = pltpu.make_async_copy(bias_hbm, bias_ref, lsem.at[4])
    x_load.start()
    gain_load.start()
    bias_load.start()

    @pl.when(s == 3)
    def _():
        cot_load.start()

    k_load.start()

    barrier = pltpu.get_barrier_semaphore()

    def greet(device):
        pl.semaphore_signal(barrier, inc=1, device_id=device, device_id_type=MESH)

    plane = [(dx, 0, dy, 0) for dx, dy in CHIPS if (dx, dy) != (0, 0)]
    plane = [(0, 1, 0, 0), (0, 1, 0, 1)] + plane + [(0, 0, 0, 1)]
    @pl.when(s == 3)
    def _():
        for dx, dy, dc in AROUND:
            greet(at(3, dx, 1 - zh, dy, dc))
        for dx, dy, dc in AROUND:
            if (dx, dy, dc) != (0, 0, 0):
                greet(at(3, dx, zh, dy, dc))

    for dx, z, dy, dc in plane:
        greet(at(s, dx, (zh + z) % 2, dy, dc))

    @pl.when(s < 3)
    def _():
        for dx, dy, dc in AROUND:
            greet(at(s + 1, dx, zh, dy, dc))

        @pl.when(zh == 0)
        def _():
            for dx, dy, dc in AROUND:
                greet(at(s + 1, dx, 1, dy, dc))

    expected = len(plane) + jnp.where(s > 0, (1 + zh) * len(AROUND), 0)
    expected = expected + jnp.where(s == 3, 2 * len(AROUND) - 1, 0)
    theirs = pl.ds((1 - zh) * FR, FR)
    ours = pl.ds(zh * FR, FR)

    def indicator(shape, channel_dim):
        channel = lax.broadcasted_iota(jnp.int32, shape, channel_dim)
        group = lax.broadcasted_iota(jnp.int32, shape, 1 - channel_dim)
        return (channel // PER_GROUP == group).astype(F32)

    def grouped(first, second):
        return jnp.dot(
            jnp.concatenate([first, second], axis=0), indicator((CH, 128), 0),
            precision=lax.Precision.HIGHEST, preferred_element_type=F32,
        )

    def spread(groups):
        return jnp.dot(
            groups, indicator((128, CH), 1), precision=lax.Precision.HIGHEST, preferred_element_type=F32
        )

    x_load.wait()

    def tile_sums(frames):
        value = x_ref[frames].astype(F32)
        return grouped(jnp.sum(value, axis=1), jnp.sum(value * value, axis=1))

    xst[0] = tile_sums(theirs)
    xst[1] = tile_sums(ours)
    pl.semaphore_wait(barrier, expected)

    def each(copies, what):
        for c in copies:
            getattr(c, what)()

    x_copy = remote(x_hbm.at[theirs], xr, zsem.at[0], zpeer)

    def patch(own, other):
        own = own.astype(F32)
        other = other.astype(F32)
        upper = jnp.where(zh == 0, own, other)
        lower = jnp.where(zh == 0, other, own)
        return jnp.concatenate([upper, lower], axis=1).reshape(ROWS, CH)

    def core_sum_copy(buf, pair):
        return remote(buf.at[core], buf.at[core], pair, cpeer)

    def chip_copies(buf, sems):
        return [
            remote(buf.at[chip], buf.at[chip], sems.at[i], at(s, dx, zh, dy, 0))
            for i, (dx, dy) in enumerate(CHIPS) if i
        ]

    mine = zh * 2 + core
    xst_copies = [
        remote(xst.at[0], xstr.at[mine], asem.at[0], zpeer),
        remote(xst.at[0], xstr.at[mine], asem.at[1], at(s, 0, 1 - zh, 0, 1)),
        remote(xst.at[1], xstr.at[mine], asem.at[2], cpeer),
    ]
    each(xst_copies, "start")

    @pl.when(s == 3)
    def _():
        x_copy.start()

    xstr[mine] = xst[1]

    def pack(value, send, copies):
        center, sides, corners = send
        near, middle, _ = copies
        rf[...] = value
        for i, pixel in enumerate((0, 7, 56, 63)):
            rows = [rf[f * PX + pixel : f * PX + pixel + 1, :] for f in range(FR)]
            corners[i] = jnp.concatenate(rows + [jnp.zeros((12, CH), F32)], axis=0).astype(BF16)
        each(near[0:4], "start")
        v4 = value.reshape(FR, 8, 8, CH)
        sides[0] = v4[:, 0].reshape(32, CH).astype(BF16)
        sides[1] = v4[:, 7].reshape(32, CH).astype(BF16)
        each(near[4:6], "start")
        for i, lead in ((2, 0), (3, 7)):
            for f in range(FR):
                rows = [rf[f * PX + r * 8 + lead : f * PX + r * 8 + lead + 1, :] for r in range(8)]
                strip[f * 8 : f * 8 + 8, :] = jnp.concatenate(rows, axis=0)
            sides[i] = strip[...].astype(BF16)
        each(near[6:8], "start")
        center[...] = value.astype(BF16).reshape(FR, 2, 32, CH)
        middle.start()

    def piece_copies(sec, send, recv, sems):
        center, sides, corners = send
        center_r, sides_r, corners_r = recv
        gs, hs, ns = sems
        near, far = [], []
        for i, (dx, dc) in enumerate(CORNERS):
            near.append(remote(corners.at[i], corners_r.at[i, 0], ns.at[0, i], beside(sec, dx, zh, dc)))
            far.append(remote(corners.at[i], corners_r.at[i, 1], ns.at[1, i], beside(sec, dx, 0, dc)))
        for i, (dx, dc) in enumerate(SIDES):
            near.append(remote(sides.at[i], sides_r.at[i, pl.ds(0, 32)], hs.at[0, i], beside(sec, dx, zh, dc)))
            far.append(
                remote(sides.at[i, pl.ds(0, 16)], sides_r.at[i, pl.ds(32, 16)], hs.at[1, i], beside(sec, dx, 0, dc))
            )
        middle = remote(center, center_r.at[pl.ds(0, FR)], gs.at[0], beside(sec, 0, zh, 0))
        far.append(
            remote(center.at[pl.ds(0, 2)], center_r.at[pl.ds(FR, 2)], gs.at[1], beside(sec, 0, 0, 0))
        )
        return near, middle, far

    def wait_sent(copies, with_middle):
        near, middle, far = copies
        each(near + ([middle] if with_middle else []), "wait_send")

        @pl.when(zh == 1)
        def _():
            each(far, "wait_send")

    def wait_received(copies, with_middle):
        near, middle, far = copies
        each(near + ([middle] if with_middle else []), "wait_recv")

        @pl.when(zh == 0)
        def _():
            each(far, "wait_recv")

    w_send, w_recv, w_sems = (wc, wh, wn), (gc, gh, gn), (wgs, whs, wns)
    x_send, x_recv, x_sems = (xwc, xwh, xwn), (xgc, xgh, xgn), (xgs, xhs, xns)

    frames_of = (pl.ds(0, 6), pl.ds(4, 4))
    count_of = (6, 4)

    def direct_copies(plane_id):
        n = count_of[plane_id]
        lead = 4 * plane_id
        lr_rows = pl.ds(16 * plane_id, 32 - 16 * plane_id)
        row_rows = pl.ds(8 * lead, 8 * n)
        down = 2 * zh - 1
        pair = dsem.at[plane_id]

        def send(src, dst, slot, device):
            return pltpu.make_async_remote_copy(
                src_ref=src, dst_ref=dst, send_sem=pair.at[0, slot], recv_sem=dsem.at[zh, 1, slot],
                device_id=device, device_id_type=MESH,
            )

        nook_rows = pl.ds(plane_id, 2 - plane_id)
        landing = pl.ds(0, 2 - plane_id)
        copies = [
            send(nooks.at[0, nook_rows], gn.at[2 * zh, landing], 3, beside(3, down, plane_id, -1)),
            send(nooks.at[1, nook_rows], gn.at[2 * zh + 1, landing], 4, beside(3, down, plane_id, 1)),
            send(rows_s.at[row_rows], gh.at[zh, pl.ds(0, 8 * n)], 2, beside(3, down, plane_id, 0)),
            send(lrs.at[0, lr_rows], lr.at[0, zh, pl.ds(0, 32 - 16 * plane_id)], 0, beside(3, 0, plane_id, -1)),
            send(lrs.at[1, lr_rows], lr.at[1, zh, pl.ds(0, 32 - 16 * plane_id)], 1, beside(3, 0, plane_id, 1)),
        ]
        center = send(
            cot_hbm.at[frames_of[plane_id]], gc.at[pl.ds(0, n), zh], 5, beside(3, 0, plane_id, 0)
        )
        return copies, center

    def own_half(plane_id):
        return pltpu.make_async_copy(
            cot_hbm.at[frames_of[plane_id]], gc.at[pl.ds(0, count_of[plane_id]), plane_id], lsem.at[5]
        )

    def direct_arrivals(plane_id):
        n = count_of[plane_id]
        arrivals = []
        for source in range(2):
            sizes = (
                lr.at[0, 0, pl.ds(0, 32 - 16 * plane_id)], lr.at[0, 0, pl.ds(0, 32 - 16 * plane_id)],
                gh.at[0, pl.ds(0, 8 * n)],
                gn.at[0, pl.ds(0, 2 - plane_id)], gn.at[0, pl.ds(0, 2 - plane_id)],
            ) + ((gc.at[pl.ds(0, n), 0],) if source != plane_id else ())
            for slot, ref in enumerate(sizes):
                arrivals.append(
                    pltpu.make_async_remote_copy(
                        src_ref=ref, dst_ref=ref, send_sem=dsem.at[0, 0, slot],
                        recv_sem=dsem.at[source, 1, slot], device_id=cpeer, device_id_type=MESH,
                    )
                )
        return arrivals

    @pl.when(s == 3)
    def _():
        for plane_id in range(2):

            @pl.when(zh == plane_id)
            def _():
                direct_copies(1 - plane_id)[1].start()
                own_half(plane_id).start()

        cot_load.wait()
        rf[...] = cot_ref[...].astype(F32).reshape(ROWS, CH)
        for i, lead in ((0, 0), (1, 7)):
            for f in range(8):
                picks = [rf[f * 32 + r * 8 + lead : f * 32 + r * 8 + lead + 1, :] for r in range(4)]
                strip[f * 4 : f * 4 + 4, :] = jnp.concatenate(picks, axis=0)
            lrs[i] = strip[...].astype(BF16)
        outer_rows = []
        for f in range(8):
            outer_rows.append(
                jnp.where(zh == 0, rf[f * 32 : f * 32 + 8, :], rf[f * 32 + 24 : f * 32 + 32, :])
            )
        rows_s[...] = jnp.concatenate(outer_rows, axis=0).astype(BF16)
        for i, end in ((0, 0), (1, 7)):
            for part in range(2):
                picks = [outer_rows[part * 4 + f][end : end + 1] for f in range(4)]
                nooks[i, part] = jnp.concatenate(picks + [jnp.zeros((12, CH), F32)], axis=0).astype(BF16)
        for plane_id in (1, 0):
            each(direct_copies(plane_id)[0], "start")

    def direct_done():
        for plane_id in range(2):

            @pl.when(zh == plane_id)
            def _():
                each(direct_arrivals(plane_id), "wait_recv")
                own_half(plane_id).wait()
                n = count_of[plane_id]
                for i in range(2):
                    halves = [lr[i, z2].astype(F32)[0 : 4 * n].reshape(n, 4, CH) for z2 in range(2)]
                    gh[2 + i, 0 : 8 * n, :] = (
                        jnp.concatenate(halves, axis=1).reshape(8 * n, CH).astype(BF16)
                    )

            each(direct_copies(plane_id)[0], "wait_send")

            @pl.when(zh != plane_id)
            def _():
                direct_copies(plane_id)[1].wait_send()

    each(xst_copies, "wait")
    sb[chip] = jnp.sum(xstr[...], axis=0)
    sb_copies = chip_copies(sb, aps)
    each(sb_copies, "start")

    @pl.when(s < 3)
    def _():
        x_copy.start()

    x_copy.wait()
    xv = patch(x_ref[ours], xr[...])
    xhat[...] = xv

    @pl.when(s > 0)
    def _():
        copies = piece_copies(s - 1, x_send, x_recv, x_sems)
        pack(xv, x_send, copies)

        @pl.when(zh == 1)
        def _():
            each(copies[2], "start")

    k_load.wait()

    def flip(i, carry):
        rows = pl.ds(pl.multiple_of(i * CH, CH), CH)
        kt_ref[rows, :] = jnp.transpose(k_ref[rows, :])
        return carry

    lax.fori_loop(0, 27, flip, 0)

    xt_near = remote(xt, xtr.at[0], tsem.at[0], at(s - 1, 0, zh, 0, 0))
    xt_far = remote(xt, xtr.at[1], tsem.at[1], at(s - 1, 0, 0, 0, 0))

    def moments(total):
        total = spread(total / ENTRIES)
        mean = total[0:4]
        return mean, lax.rsqrt(total[4:8] - mean * mean + EPS)

    def prepare():
        gain_load.wait()
        bias_load.wait()
        each(sb_copies, "wait")
        xt[...] = jnp.sum(sb[...], axis=0)
        @pl.when(s > 0)
        def _():
            xt_near.start()

            @pl.when(zh == 1)
            def _():
                xt_far.start()

        mean, rstd = moments(xt[...])
        gain = gain_ref[...]
        rs[0:FR, :] = rstd
        xh = (xhat[...].reshape(FR, PX, CH) - mean[:, None, :]) * rstd[:, None, :]
        h = xh * gain[None] + bias_ref[...][None]
        sg = jax.nn.sigmoid(h)
        xhat[...] = xh.reshape(ROWS, CH)
        dfac[...] = (sg * (1.0 + h * (1.0 - sg))).reshape(ROWS, CH)
        act = h * sg
        a_t[...] = jnp.transpose(jnp.concatenate([act, -act], axis=1).reshape(2 * ROWS, CH)).astype(BF16)

    @pl.when(s < 3)
    def _():
        prepare()

    @pl.when(s < 3)
    def _():
        wait_received(piece_copies(s, x_send, x_recv, x_sems), True)
        remote(xt, xtr.at[0], tsem.at[0], cpeer).wait_recv()

        @pl.when(zh == 0)
        def _():
            remote(xt, xtr.at[1], tsem.at[1], cpeer).wait_recv()

        def normalise(frames, part, row0):
            mean_up, rstd_up = moments(xtr[part])
            n = len(frames)
            mom[frames[0] : frames[0] + n, :] = rstd_up[0:n]
            m, r = mean_up[0:n][:, None, :], rstd_up[0:n][:, None, :]
            px = slice(frames[0] * PX, (frames[0] + n) * PX)
            up = xgc[frames[0] : frames[0] + n].astype(F32).reshape(n, PX, CH)
            xc[px, :] = ((up - m) * r).reshape(n * PX, CH)
            for i in range(4):
                side = xgh[i, row0 : row0 + 8 * n, :].astype(F32).reshape(n, 8, CH)
                xs[i, row0 : row0 + 8 * n, :] = ((side - m) * r).reshape(8 * n, CH)
                xn[part, i, 0:n, :] = (xgn[i, part].astype(F32)[0:n] - mean_up[0:n]) * rstd_up[0:n]

        normalise(range(4), 0, 0)

        @pl.when(zh == 0)
        def _():
            normalise(range(4, 6), 1, 32)

    arriving = piece_copies(s, w_send, w_recv, w_sems)

    edge = (x > 0, x < 3, col > 0, col < 7)

    def columns(frames, center, sides, corners, shift):
        top = jnp.where(edge[0], sides[1], 0.0)
        bottom = jnp.where(edge[1], sides[0], 0.0)
        left = jnp.where(edge[2], sides[3], 0.0)
        right = jnp.where(edge[3], sides[2], 0.0)
        top_left = jnp.where(edge[0] & edge[2], corners[3], 0.0)
        top_right = jnp.where(edge[0] & edge[3], corners[2], 0.0)
        bottom_left = jnp.where(edge[1] & edge[2], corners[1], 0.0)
        bottom_right = jnp.where(edge[1] & edge[3], corners[0], 0.0)
        center = center.reshape(len(frames), 8, 8, CH)
        for i, f in enumerate(frames):
            base = f * 10
            cell = slice(i * 8, i * 8 + 8)
            gp[base + 1 : base + 9, 8:16, :] = center[i]
            gp[base, 8:16, :] = top[cell]
            gp[base + 9, 8:16, :] = bottom[cell]
            for r in range(8):
                gp[base + 1 + r, 7:8, :] = left[i * 8 + r : i * 8 + r + 1]
                gp[base + 1 + r, 16:17, :] = right[i * 8 + r : i * 8 + r + 1]
            gp[base, 7:8, :] = top_left[i : i + 1]
            gp[base, 16:17, :] = top_right[i : i + 1]
            gp[base + 9, 7:8, :] = bottom_left[i : i + 1]
            gp[base + 9, 16:17, :] = bottom_right[i : i + 1]
            for ox in range(3):
                band = gp[base : base + 10, 7 + ox : 15 + ox, :]
                for oy in range(3):
                    tap = (2 - oy) * 3 + (2 - ox)
                    cols[f * 2 * PX + shift : f * 2 * PX + shift + PX, tap * CH : tap * CH + CH] = (
                        band[oy : oy + 8].reshape(PX, CH).astype(BF16)
                    )

    def fill(frames, part, row0):
        n = len(frames)
        columns(
            frames, gc[frames[0] : frames[0] + n].astype(F32),
            [gh[i, row0 : row0 + 8 * n, :].astype(F32) for i in range(4)],
            [gn[i, part].astype(F32)[0:n] for i in range(4)], 0,
        )

    def fill_correction(frames, part, row0, sums):
        n = len(frames)
        both = spread(sums / ENTRIES)
        r_up = mom[frames[0] : frames[0] + n, :]
        c1, c2 = r_up * both[0:n], r_up * both[4 : 4 + n]

        def term(hat, rows):
            value = c1[:, None, :] + hat.reshape(n, rows, CH) * c2[:, None, :]
            return value.reshape(n * rows, CH)

        px = slice(frames[0] * PX, (frames[0] + n) * PX)
        center = term(xc[px, :], PX)
        if part == 0:
            gcen[...] = gc[0:FR].astype(F32).reshape(ROWS, CH) - center
        columns(
            frames, center, [term(xs[i, row0 : row0 + 8 * n, :], 8) for i in range(4)],
            [c1 + xn[part, i, 0:n, :] * c2 for i in range(4)], PX,
        )

    def convolve(shift):
        value = jnp.zeros((ROWS, CH), F32)
        for kt in range(3):
            starts = [(2 - kt + f) * 2 * PX + shift for f in range(FR)]
            value = value + jnp.dot(
                jnp.concatenate([cols[r : r + PX, :] for r in starts], axis=0),
                kt_ref[kt * 9 * CH : (kt + 1) * 9 * CH, :],
                preferred_element_type=F32,
            )
        return value

    def gather():
        near, middle, far = arriving

        @pl.when(s == 3)
        def _():
            direct_done()

        @pl.when(s < 3)
        def _():
            each(near, "wait_recv")
            middle.wait_recv()

        fill(range(4), 0, 0)

        @pl.when(zh == 0)
        def _():
            @pl.when(s < 3)
            def _():
                each(far, "wait_recv")

            fill(range(4, 6), 1, 32)

        @pl.when(zh == 1)
        def _():
            cols[2 * ROWS :, :] = jnp.zeros((4 * PX, 9 * CH), BF16)

        da[...] = convolve(0)

    @pl.when(s == 3)
    def _():
        gather()
        prepare()

    @pl.when(s < 3)
    def _():
        gather()

    gain = gain_ref[...]
    rstd = rs[0:FR, :]

    def one_tap(tap):
        rows = pl.ds(pl.multiple_of(tap * CH, CH), CH)
        lanes = pl.multiple_of((tap % 9) * CH, CH)
        frames = pl.multiple_of((2 - tap // 9) * 2 * PX, 2 * PX)
        part = jnp.dot(
            a_t[...], cols[pl.ds(frames, 2 * ROWS), pl.ds(lanes, CH)], preferred_element_type=F32
        )
        dko[rows, :] = jnp.where(core == 0, part[:, :128], part[:, 128:])
        dks[rows, :] = jnp.where(core == 0, part[:, 128:], part[:, :128]).astype(BF16)

    def own_rows(step, offset, count):
        q = (x + 1 + step) % 4
        return pl.ds(pl.multiple_of(q * QUARTER + offset, 8), count)

    def core_copy(step):
        q = (x + 1 + step) % 4
        span = pl.ds(pl.multiple_of(q * QUARTER, 16), QUARTER)
        return remote(dks.at[span], dkr.at[span], csem.at[step], cpeer)

    def quarter(step):
        q = (x + 1 + step) % 4
        if step == 0:
            @pl.when(x < 3)
            def _():
                one_tap(7 * x + 6)

        for i in range(6):
            one_tap(7 * q + i)
        if step < 3:
            one_tap(7 * q + 6 - q // 3)
        core_copy(step).start()

    def x_first(step):
        return remote(b0.at[step], rx.at[step], xsem.at[step], at(s, step + 1, zh, 0, 0))

    def y_first(step, k):
        return remote(b1.at[step, (y + k) % 4], ry.at[k - 1, step], ysem.at[step, k - 1], at(s, 0, zh, k, 0))

    pad8 = jnp.zeros((8, 128), F32)

    def join(step):
        core_copy(step).wait()
        for half in range(4):
            rows = own_rows(step, half * 432, 432)
            both_cores = dko[rows, :] + dkr[rows, :].astype(F32)
            dko[rows, :] = both_cores
            if half >= 2:
                for i in range(2):
                    piece = jnp.concatenate([both_cores[i * 216 : i * 216 + 216], pad8], axis=0)
                    b1[step, (half - 2) * 2 + i] = piece.astype(BF16)
            elif step < 3:
                b0[step, half * 432 : half * 432 + 432, :] = both_cores.astype(BF16)
        if step < 3:
            x_first(step).start()
        for k in (2, 1, 3):
            y_first(step, k).start()

    def then_x(step):
        return remote(p1.at[step], r2x.at[step], xsem2.at[step], at(s, step + 1, zh, 0, 0))

    def then_y(k):
        return remote(p0.at[(y + k) % 4], r2y.at[k - 1], ysem2.at[k - 1], at(s, 0, zh, k, 0))

    def sum_y(step):
        for k in range(1, 4):
            y_first(step, k).wait()
        acc = dko[own_rows(step, 864 + y * 216, 216), :]
        for k in range(3):
            acc = acc + ry[k, step].astype(F32)[0:216]
        if step < 3:
            p1[step] = jnp.concatenate([acc, pad8], axis=0).astype(BF16)
            then_x(step).start()
        else:
            t1[...] = acc

    def sum_x():
        for step in range(3):
            x_first(step).wait()
        for half in range(2):
            acc = dko[own_rows(3, half * 432, 432), :]
            for k in range(3):
                acc = acc + rx[k, half * 432 : half * 432 + 432, :].astype(F32)
            for i in range(2):
                piece = acc[i * 216 : i * 216 + 216]
                t0[half * 2 + i] = piece
                p0[half * 2 + i] = jnp.concatenate([piece, pad8], axis=0).astype(BF16)
        for k in (2, 1, 3):
            then_y(k).start()

    @pl.when(s == 3)
    def _():
        gcen[...] = gc[0:FR].astype(F32).reshape(ROWS, CH)
        for f in range(6):
            cols[f * 2 * PX + PX : f * 2 * PX + 2 * PX, :] = jnp.zeros((PX, 9 * CH), BF16)

    @pl.when(s < 3)
    def _():
        remote(zg.at[pl.ds(0, 8)], unear, tsem.at[3], cpeer).wait_recv()
        fill_correction(range(4), 0, 0, unear[...])

        @pl.when(zh == 0)
        def _():
            remote(zg.at[pl.ds(0, 8)], ufar, tsem.at[2], cpeer).wait_recv()
            fill_correction(range(4, 6), 1, 32, ufar[...])


    @pl.when(s == 0)
    def _():
        quarter(0)
        quarter(1)
        join(0)
        quarter(2)
        join(1)
        quarter(3)
        join(2)
        join(3)

    @pl.when(s < 3)
    def _():
        da[...] = da[...] - convolve(PX)

    dh3 = (da[...] * dfac[...]).reshape(FR, PX, CH)
    dh_sum = jnp.sum(dh3, axis=1)
    dhx_sum = jnp.sum(dh3 * xhat[...].reshape(FR, PX, CH), axis=1)
    gain_part = jnp.sum(dhx_sum, axis=0, keepdims=True)
    bias_part = jnp.sum(dh_sum, axis=0, keepdims=True)
    ua[core] = jnp.concatenate(
        [
            grouped(dh_sum * gain, dhx_sum * gain),
            gain_part[:, :128], gain_part[:, 128:], bias_part[:, :128], bias_part[:, 128:],
            jnp.zeros((4, 128), F32),
        ],
        axis=0,
    )
    ua_copy = core_sum_copy(ua, ucs)
    ua_copy.start()

    w = gcen[...] + (rstd[:, None, :] * (dh3 * gain[None])).reshape(ROWS, CH)
    dfac[...] = w

    w_copies = piece_copies(s - 1, w_send, w_recv, w_sems)

    @pl.when(s > 0)
    def _():
        pack(w, w_send, w_copies)

    ua_copy.wait()
    ub[chip] = ua[0] + ua[1]
    ub_copies = chip_copies(ub, ups)
    each(ub_copies, "start")

    @pl.when((s > 0) & (zh == 1))
    def _():
        each(w_copies[2], "start")

    @pl.when(s > 0)
    def _():
        quarter(0)
        quarter(1)

    def axis_sums():
        sum_y(0)
        sum_y(1)
        sum_y(2)
        sum_x()
        sum_y(3)

    @pl.when(s == 0)
    def _():
        axis_sums()

    each(ub_copies, "wait")
    total = jnp.sum(ub[...], axis=0)
    zg[...] = total
    near_sum = remote(zg.at[pl.ds(0, 8)], unear, tsem.at[3], at(s - 1, 0, zh, 0, 0))
    far_sum = remote(zg.at[pl.ds(0, 8)], ufar, tsem.at[2], at(s - 1, 0, 0, 0, 0))

    @pl.when(s > 0)
    def _():
        near_sum.start()

        @pl.when(zh == 1)
        def _():
            far_sum.start()

    zg_copy = remote(zg, zgr, zsem.at[3], zpeer)
    zg_copy.start()
    both = spread(total[0:8] / ENTRIES)
    c1, c2 = rstd * both[0:4], rstd * both[4:8]
    xh = xhat[...].reshape(FR, PX, CH)
    final = dfac[...].reshape(FR, PX, CH) - c1[:, None, :] - xh * c2[:, None, :]
    final = final.astype(BF16).reshape(FR, 2, 32, CH)
    osend[...] = jnp.where(zh == 0, final[:, 1], final[:, 0])
    o_copy = remote(osend, orecv, zsem.at[2], zpeer)
    o_copy.start()
    out_ref[ours] = jnp.where(zh == 0, final[:, 0], final[:, 1])

    @pl.when(s > 0)
    def _():
        join(0)
        quarter(2)
        join(1)
        quarter(3)
        join(2)
        join(3)

    @pl.when(s > 0)
    def _():
        axis_sums()

    pad4 = jnp.zeros((4, 128), F32)

    def to_owner(plane_id, dc):
        return pltpu.make_async_remote_copy(
            src_ref=p3.at[plane_id, (core + dc) % 2], dst_ref=r3.at[core, zh],
            send_sem=psem.at[plane_id, 0, dc], recv_sem=psem.at[zh, 1, dc],
            device_id=at(s, 0, plane_id, 0, dc), device_id_type=MESH,
        )

    def finish(plane_id):
        if plane_id:
            acc = t1[...]
            for step in range(3):
                then_x(step).wait()
                acc = acc + r2x[step].astype(F32)[0:216]
        else:
            acc = t0[y]
            for k in range(1, 4):
                then_y(k).wait()
                acc = acc + r2y[k - 1].astype(F32)[0:216]
        p3[plane_id, 0] = jnp.concatenate([acc[0:108], pad4], axis=0).astype(BF16)
        p3[plane_id, 1] = jnp.concatenate([acc[108:216], pad4], axis=0).astype(BF16)
        to_owner(plane_id, 1).start()

        @pl.when(zh != plane_id)
        def _():
            to_owner(plane_id, 0).start()

        @pl.when(zh == plane_id)
        def _():
            r3[core, zh] = p3[plane_id, core]

    finish(1)
    finish(0)

    zg_copy.wait()
    sums = (zg[...] + zgr[...]) * SCALE
    gout_ref[:, 0:128] = sums[8:9]
    gout_ref[:, 128:256] = sums[9:10]
    bout_ref[:, 0:128] = sums[10:11]
    bout_ref[:, 128:256] = sums[11:12]
    o_copy.wait()
    out_ref[theirs] = orecv[...]

    @pl.when(s > 0)
    def _():
        wait_sent(piece_copies(s - 1, x_send, x_recv, x_sems), True)
        wait_sent(w_copies, True)
        xt_near.wait_send()
        near_sum.wait_send()

        @pl.when(zh == 1)
        def _():
            xt_far.wait_send()
            far_sum.wait_send()

    for source in range(2):
        for dc in range(2):
            arrival = pltpu.make_async_remote_copy(
                src_ref=p3.at[0, 0], dst_ref=r3.at[0, 0], send_sem=psem.at[0, 0, dc],
                recv_sem=psem.at[source, 1, dc], device_id=cpeer, device_id_type=MESH,
            )
            if dc:
                arrival.wait_recv()
            else:

                @pl.when(zh != source)
                def _():
                    arrival.wait_recv()

    for half in range(2):
        value = r3[half, 0].astype(F32) + r3[half, 1].astype(F32)
        kout_ref[:, 0, half * 128 : half * 128 + 128] = value[0:108] * SCALE

    for plane_id in range(2):
        to_owner(plane_id, 1).wait_send()

        @pl.when(zh != plane_id)
        def _():
            to_owner(plane_id, 0).wait_send()


def write_out(*refs):
    for source, target in zip(refs[:4], refs[4:]):
        target[...] = source[...]


def on_device(saved_inputs, cotangent, kernels, gains, biases):
    inputs = saved_inputs.reshape(8, 32, CH)
    seeds = cotangent.reshape(8, 32, CH)
    vmem = pl.BlockSpec(memory_space=pltpu.VMEM)
    hbm = pl.BlockSpec(memory_space=pltpu.HBM)
    v = pltpu.VMEM
    dma = pltpu.SemaphoreType.DMA
    made = pl.pallas_call(
        kernel,
        out_shape=(
            jax.ShapeDtypeStruct((8, 32, CH), BF16),
            jax.ShapeDtypeStruct((108, 1, CH), F32),
            jax.ShapeDtypeStruct((1, CH), F32),
            jax.ShapeDtypeStruct((1, CH), F32),
        ),
        in_specs=[hbm] * 5,
        out_specs=[vmem] * 4,
        scratch_shapes=[
            v((8, 32, CH), BF16), v((8, 32, CH), BF16), v((27 * CH, CH), BF16), v((1, CH), F32), v((1, CH), F32),
            v((FR, 32, CH), BF16), v((2, 8, 128), F32), v((4, 8, 128), F32), v((FR, 32, CH), BF16), v((FR, 32, CH), BF16),
            v((ROWS, CH), F32), v((32, CH), F32),
            v((2, 32, CH), BF16), v((64, CH), BF16), v((2, 2, 16, CH), BF16), v((2, 2, 32, CH), BF16),
            v((FR, 2, 32, CH), BF16), v((4, 32, CH), BF16), v((4, 16, CH), BF16),
            v((6, 2, 32, CH), BF16), v((4, 48, CH), BF16), v((4, 2, 16, CH), BF16),
            v((FR, 2, 32, CH), BF16), v((4, 32, CH), BF16), v((4, 16, CH), BF16),
            v((6, 2, 32, CH), BF16), v((4, 48, CH), BF16), v((4, 2, 16, CH), BF16),
            v((ALL, CH), F32), v((4, 48, CH), F32), v((2, 4, 16, CH), F32), v((60, 24, CH), F32),
            v((ROWS, CH), F32), v((2 * ALL, 9 * CH), BF16), v((27 * CH, CH), BF16),
            v((CH, 2 * ROWS), BF16), v((ROWS, CH), F32), v((ROWS, CH), F32), v((ROWS, CH), F32), v((8, CH), F32),
            v((16, 8, 128), F32), v((2, 16, 128), F32), v((16, 16, 128), F32),
            v((8, 128), F32), v((8, 128), F32), v((8, 128), F32), v((2, 8, 128), F32), v((8, CH), F32),
            v((16, 128), F32), v((16, 128), F32),
            v((27 * CH, 128), F32), v((27 * CH, 128), BF16), v((27 * CH, 128), BF16),
            v((3, 864, 128), BF16), v((4, 4, 224, 128), BF16), v((3, 864, 128), BF16), v((3, 4, 224, 128), BF16),
            v((4, 224, 128), BF16), v((3, 224, 128), BF16), v((4, 216, 128), F32), v((216, 128), F32),
            v((3, 224, 128), BF16), v((3, 224, 128), BF16), v((2, 2, 112, 128), BF16), v((2, 2, 112, 128), BF16),
            dma((6,)), dma((4, 2)), dma((2, 2, 6)), dma((2, 2)), dma((2, 4, 2)), dma((2, 4, 2)),
            dma((2, 2)), dma((2, 4, 2)), dma((2, 4, 2)),
            dma((3, 2)), dma((16, 2)), dma((2,)), dma((16, 2)), dma((4, 2)), dma((4, 2)),
            dma((3, 2)), dma((4, 3, 2)), dma((3, 2)), dma((3, 2)), dma((2, 2, 2)),
        ],
        compiler_params=pltpu.CompilerParams(
            collective_id=0, has_side_effects=True, vmem_limit_bytes=VMEM_LIMIT
        ),
        name="blocks",
    )(inputs, seeds, kernels[0], gains, biases)
    out, kout, gout, bout = pl.pallas_call(
        write_out,
        out_shape=tuple(jax.ShapeDtypeStruct(m.shape, m.dtype) for m in made),
        in_specs=[vmem] * 4,
        out_specs=[vmem] * 4,
        name="write_out",
    )(*made)
    return out.reshape(1, 8, 1, 4, 8, CH), kout.reshape(1, 108, CH), gout, bout


def solution(mesh):
    in_specs = (
        P("section", None, "tile", None, None, None),
        P(None, "tile", None, None, None),
        P("section", None, None),
        P("section", None),
        P("section", None),
    )
    out_specs = (
        P("section", None, "tile", None, None, None),
        P("section", "tile", None),
        P("section", None),
        P("section", None),
    )
    return jax.shard_map(
        on_device, mesh=mesh, in_specs=in_specs, out_specs=out_specs, check_vma=False
    )
```
